128 devices in a mesh: along: 16 (over z, x), cross: 8 (over y, core).
Axes of the slice: x: 4, y: 4, z: 4, core: 2. Of those that a mesh axis runs over, the one named last changes fastest.
Arguments:
- offsets: float32 [2, 64, 128, 128], P(None, 'along', 'cross'), may hold values from 0 to 1
- velocity: float32 [2, 64, 128, 128], P(None, 'along', 'cross'), may hold values from -6 to 6
- particle_mass: float32 [64, 128, 128], P('along', 'cross'), may hold values from 0.5 to 2
- neighbours: int32 [64, 128, 9], P('along', 'cross'), may hold values from -1 to 8, as said below
- owner_device: int32 [16, 8, 8192, 1], P('along', 'cross'), may hold values from 0 to 127; in each aligned block of 8192 rows (0 to 8191, 8192 to 16383, ..., all dimensions but the last counted through in order) at most 192 rows name the same one
- target_cell: int32 [16, 8, 8192], P('along', 'cross'), may hold values from 0 to 65535
- surface: float32 [3, 2048, 4096], P(None, 'along', 'cross'), may hold values from -6 to 6
- water_depth: float32 [2048, 4096], P('along', 'cross'), may hold values from 0.5 to 2
Outputs:
- grid_state: float32 [3, 2048, 4096], P(None, 'along', 'cross')
- density: float32 [64, 128, 128], P('along', 'cross')
- feedback: float32 [3, 64, 128, 128], P(None, 'along', 'cross')
The draws below stay inside these ranges and needn't reach their ends.
Inputs may be any that keep to these rules, and one draw needn't show every extreme that they name: `owner_device`: in the rows of one device, at most 192 particles name one owner device (numbered as along index times 8 plus cross index), a bound that some block reaches. `neighbours`: slot 0 holds 4, the tile itself; the other slots hold distinct window positions or -1 for padding.
All inputs are finite; a program needn't handle non-finite values.
Results may differ from the reference program's by a relative error of at most 0.0003.
Values sent between devices are 32-bit elements; how exact they have to be, the bound alone decides.
A program may use at most 64 MiB of HBM per device.

```python
import math
import jax
import jax.numpy as jnp
import numpy as np
from jax import lax

TILE = 128
TA = 4
TC = 16
GA = 128
GC = 512
SUBSTEPS = 4
PART_DEV = 8192
CAP = 192
NTA = 64
NTC = 128
NA = 2048
NC = 4096
N_ALONG = 16
N_CROSS = 8
DEVICES = 128


def draw_neighbours(key, part):
    shape_tiles = (NTA, NTC)
    key_order, key_drop = jax.random.split(jax.random.fold_in(key, 7))
    scores = jax.random.randint(key_order, shape_tiles + (8,), 0, 1 << 20) * 8 + jnp.arange(8, dtype=jnp.int32)
    ranking = jnp.argsort(scores, axis=-1, stable=True)
    others = jnp.array([0, 1, 2, 3, 5, 6, 7, 8], jnp.int32)
    chosen = others[ranking]
    dropped = jax.random.randint(key_drop, shape_tiles + (8,), 0, 3) == 0
    chosen = jnp.where(dropped, -1, chosen)
    own_tile = jnp.full(shape_tiles + (1,), 4, jnp.int32)
    return jnp.concatenate([own_tile, chosen], axis=-1).astype(jnp.int32)


def touch_ends(entries, key, smallest, largest):
    longest = entries.shape.index(max(entries.shape))
    spots = []
    for shift in (0, 1):
        where = [jax.random.randint(jax.random.fold_in(key, axis), (), 0, length) for axis, length in enumerate(entries.shape)]
        where[longest] = (where[longest] + shift) % entries.shape[longest]
        spots.append(tuple(where))
    return entries.at[spots[0]].set(smallest).at[spots[1]].set(largest)


def shard_levels(key, dims, shards, smallest, top_value):
    def one(dim, blocks):
        draws = jax.random.uniform(jax.random.fold_in(jax.random.fold_in(key, 6), dim), (blocks,), jnp.float32, smallest / len(shards), top_value / len(shards))
        return jnp.repeat(jnp.exp(draws), dims[dim] // blocks).reshape((-1,) + (1,) * (len(dims) - dim - 1))

    factor_of = one(*shards[0])
    for cut in shards[1:]:
        factor_of = factor_of * one(*cut)
    return factor_of


def shared_out(key, own, number, rows, amount, top, bound, slope):
    order = jax.random.permutation(key, amount)
    crowded, usual = load_shares(amount, rows * top, bound, slope, True), load_shares(amount, rows * top, bound, slope, False)
    places = jnp.arange(amount)

    def named(sizes, turn):
        used = int((sizes > 0).sum())
        fixed = max(1, used // 4)
        passed = fixed + (places - fixed + turn * (used - fixed)) % max(1, amount - fixed)
        return jnp.zeros((amount,), jnp.int32).at[order[jnp.where(places < fixed, places, passed)]].set(jnp.asarray(sizes, jnp.int32))

    sizes = jnp.where(number % 4 == 0, named(crowded, number // 4), named(usual, number - number // 4 - 1))
    mixed = jax.random.permutation(jax.random.fold_in(own, 3), amount)
    source_of, receiver = mixed[0:amount // 2 * 2:2], mixed[1:amount // 2 * 2:2]
    slack = jnp.minimum(sizes[source_of] - 1, bound - sizes[receiver]) // 2
    slack = jnp.where((source_of == order[0]) | (receiver == order[0]) | (sizes[receiver] == 0), 0, jnp.maximum(slack, 0))
    passed = jax.random.randint(jax.random.fold_in(own, 4), (amount // 2,), 0, 1 << 20) % (slack + 1)
    sizes = sizes.at[source_of].add(-passed).at[receiver].add(passed)
    labels = jnp.searchsorted(jnp.cumsum(sizes), jnp.arange(rows * top), side="right").astype(jnp.int32)
    grid = labels.reshape(top, rows).T
    grid = grid[jax.random.permutation(jax.random.fold_in(own, 1), rows)]
    turn = jax.random.randint(jax.random.fold_in(own, 2), (rows, 1), 0, top)
    return jnp.take_along_axis(grid, (jnp.arange(top)[None, :] + turn) % top, axis=1)


def load_shares(amount, total, bound, lean, full):
    portions = [(1 << 20) // math.isqrt(standing ** lean) + 1 for standing in range(1, amount + 1)]
    largest = bound if full else min(bound, max(-(-total // amount), total * portions[0] // sum(portions)))
    least = 1 if total - largest >= amount - 1 else 0
    holding, rest = [largest] + [least] * (amount - 1), total - largest - least * (amount - 1)
    while rest > 0:
        candidates = [i for i in range(1, amount) if holding[i] < largest] or [i for i in range(1, amount) if holding[i] < bound]
        mass, budget = sum([portions[i] for i in candidates]), rest
        for i in candidates:
            more = min(bound - holding[i], max(1, budget * portions[i] // mass), rest)
            holding[i] = holding[i] + more
            rest = rest - more
    return np.array(holding)


def noise(key, extent, spread, most, pieces=(), kind=jnp.bfloat16):
    result = spread * jax.random.normal(key, extent, jnp.float32)
    if pieces:
        result = result * shard_levels(key, extent, pieces, -0.22, 0.18)
    return jnp.clip(result, -most, most).astype(kind)


def setup_inputs(seed: int = 0) -> dict:
    seeds = jax.random.split(jax.random.key(seed), 9)
    offsets = jnp.clip(1.0 * jax.random.uniform(seeds[0], (2, NTA, NTC, TILE), jnp.float32) ** shard_levels(seeds[0], (2, NTA, NTC, TILE), ((1, 16), (2, 8)), -0.2, 0.2), 0.0, 1.0)
    velocity = noise(seeds[1], (2, NTA, NTC, TILE), 1.0, 6.0, ((1, 16), (2, 8)), jnp.float32)
    particle_mass = jnp.clip(jnp.exp(math.log(2.0) - 1.3862944 * jax.random.uniform(seeds[2], (NTA, NTC, TILE), jnp.float32) ** shard_levels(seeds[2], (NTA, NTC, TILE), ((0, 16), (1, 8)), -0.2, 0.2)), 0.5, 2.0)
    neighbours = draw_neighbours(jax.random.fold_in(seeds[8], 71), 0)
    owner_device_keys = jax.random.split(jax.random.fold_in(seeds[4], 1), N_ALONG * N_CROSS * PART_DEV // PART_DEV)
    owner_device_turns = jax.random.permutation(jax.random.fold_in(seeds[4], 3), N_ALONG * N_CROSS * PART_DEV // PART_DEV)
    owner_device = jax.vmap(lambda own, number: shared_out(jax.random.fold_in(seeds[4], 2), own, number, PART_DEV, DEVICES, 1, CAP, 2))(owner_device_keys, owner_device_turns).reshape((N_ALONG, N_CROSS, PART_DEV, 1))
    target_cell = touch_ends(jax.random.randint(seeds[5], (N_ALONG, N_CROSS, PART_DEV), 0, GA * GC), jax.random.fold_in(seeds[5], 1), 0, (GA * GC) - 1).astype(jnp.int32)
    surface = noise(seeds[6], (3, NA, NC), 1.0, 6.0, ((1, 16), (2, 8)), jnp.float32)
    water_depth = jnp.clip(jnp.exp(math.log(2.0) - 1.3862944 * jax.random.uniform(seeds[7], (NA, NC), jnp.float32) ** shard_levels(seeds[7], (NA, NC), ((0, 16), (1, 8)), -0.2, 0.2)), 0.5, 2.0)
    return {"offsets": offsets, "velocity": velocity, "particle_mass": particle_mass, "neighbours": neighbours, "owner_device": owner_device, "target_cell": target_cell, "surface": surface, "water_depth": water_depth}


courant = 0.4
kernel_width = 1.0


def tile_sums(window_rows, present_row):
    columns = window_rows.shape[2] - 2
    own_row = window_rows[:, 1, 1:columns + 1, :]
    totals = jnp.zeros((3, columns, window_rows.shape[3]), jnp.float32)
    for window in range(9):
        row_shift = window // 3
        col_shift = window % 3
        nearby = window_rows[:, row_shift, col_shift:col_shift + columns, :]
        delta_x = own_row[0][:, :, None] - nearby[0][:, None, :] - (row_shift - 1.0)
        delta_y = own_row[1][:, :, None] - nearby[1][:, None, :] - (col_shift - 1.0)
        weights = jnp.exp(-(delta_x * delta_x + delta_y * delta_y) / kernel_width)
        weights = weights * present_row[:, window][:, None, None]
        carried = jnp.stack([nearby[4], nearby[4] * nearby[2], nearby[4] * nearby[3]])
        totals = totals + jnp.einsum("tab,ktb->kta", weights, carried, precision=lax.Precision.HIGHEST)
    return totals


def particle_pass(padded, neighbours):
    rows = padded.shape[1] - 2
    present = jnp.any(neighbours[..., :, None] == jnp.arange(9, dtype=jnp.int32), axis=-2).astype(jnp.float32)

    def one_row(row_index):
        window_rows = lax.dynamic_slice_in_dim(padded, row_index, 3, 1)
        present_row = lax.dynamic_index_in_dim(present, row_index, 0, keepdims=False)
        return tile_sums(window_rows, present_row)

    totals = lax.map(one_row, jnp.arange(rows, dtype=jnp.int32))
    return jnp.transpose(totals, (1, 0, 2, 3))


def particle_sources(totals, particle_mass, tile_size):
    density = totals[0] / tile_size
    volume = particle_mass / density
    smooth_x = totals[1] / totals[0]
    smooth_y = totals[2] / totals[0]
    return density, jnp.stack([volume, volume * smooth_x, volume * smooth_y])


def lax_friedrichs(state_pad, depth_pad):
    height = state_pad[0]
    speed_x = state_pad[1]
    speed_y = state_pad[2]
    flux_x = depth_pad * speed_x
    flux_y = depth_pad * speed_y

    def average(quantity):
        return 0.25 * (quantity[2:, 1:-1] + quantity[:-2, 1:-1] + quantity[1:-1, 2:] + quantity[1:-1, :-2])

    next_height = average(height) - 0.5 * courant * (flux_x[2:, 1:-1] - flux_x[:-2, 1:-1] + flux_y[1:-1, 2:] - flux_y[1:-1, :-2])
    next_speed_x = average(speed_x) - 0.5 * courant * (height[2:, 1:-1] - height[:-2, 1:-1])
    next_speed_y = average(speed_y) - 0.5 * courant * (height[1:-1, 2:] - height[1:-1, :-2])
    return jnp.stack([next_height, next_speed_x, next_speed_y])


def reference(offsets, velocity, particle_mass, neighbours, owner_device, target_cell, surface, water_depth):
    stacked = jnp.concatenate([offsets, velocity, particle_mass[None]], axis=0)
    padded = jnp.pad(stacked, ((0, 0), (1, 1), (1, 1), (0, 0)))
    totals = particle_pass(padded, neighbours)
    density, sources = particle_sources(totals, particle_mass, TILE)
    ordered = sources.reshape(3, N_ALONG, TA, N_CROSS, TC, TILE).transpose(0, 1, 3, 2, 4, 5).reshape(3, -1)
    owners = owner_device.reshape(-1)
    cells = target_cell.reshape(-1)
    grid_row = (owners // N_CROSS) * GA + cells // GC
    grid_col = (owners % N_CROSS) * GC + cells % GC
    flat_cell = (grid_row * NC + grid_col).astype(jnp.int32)
    grid_source = jnp.zeros((3, NA * NC), jnp.float32).at[:, flat_cell].add(ordered).reshape(3, NA, NC)
    depth_pad = jnp.pad(water_depth, 1)
    water_state = surface
    for substep in range(SUBSTEPS):
        state_pad = jnp.pad(water_state, ((0, 0), (1, 1), (1, 1)))
        water_state = lax_friedrichs(state_pad, depth_pad) + grid_source
    looked = water_state.reshape(3, -1)[:, flat_cell]
    feedback = looked.reshape(3, N_ALONG, N_CROSS, TA, TC, TILE).transpose(0, 1, 3, 2, 4, 5).reshape(3, NTA, NTC, TILE)
    return water_state, density, feedback
```

```python
import math

import jax
import jax.numpy as jnp
from jax import lax
from jax.experimental import pallas as pl
from jax.experimental.pallas import tpu as pltpu
from jax.sharding import PartitionSpec as P

SUBSTEPS = 4
KAPPA = math.sqrt(math.log2(math.e))
F32 = jnp.float32
BF16 = jnp.bfloat16
NN = (((1,), (0,)), ((), ()))
NT = (((1,), (1,)), ((), ()))
VMEM_LIMIT = 56 * 1024 * 1024

courant = 0.4


def dot(a, b, dims):
    return lax.dot_general(a, b, dims, preferred_element_type=F32)


def split2(x):
    hi = x.astype(BF16).astype(F32)
    return hi, x - hi


def iota(shape, dim):
    return lax.broadcasted_iota(jnp.int32, shape, dim)


def cross_rows(x, y, pattern, scale):
    q = iota((16, 128), 0)
    v = jnp.where(q < 6, jnp.broadcast_to(x, (16, 128)), jnp.broadcast_to(y, (16, 128)))
    hi, rest = split2(v)
    mid, low = split2(rest)
    out = jnp.zeros((16, 128), F32)
    for r, p in enumerate(pattern * 2):
        out = jnp.where(q == r, (hi, mid, low)[p], out)
    return (out * scale).astype(BF16)


def window_sums(pad_ref, present_ref, sums_ref, cols_ref):
    rows_pad, cols_pad = pad_ref.shape[1], pad_ref.shape[2]
    rows, cols = rows_pad - 2, cols_pad - 2

    def features(g, carry):
        i = g // cols_pad
        j = g - i * cols_pad
        x = pad_ref[0, i, pl.ds(j, 1), :] * KAPPA
        y = pad_ref[1, i, pl.ds(j, 1), :] * KAPPA
        feats = cross_rows(x, y, [0, 1, 0, 1, 2, 0], 2.0)
        cols_ref[g, :, 0:16] = feats.astype(F32).T.astype(BF16)
        return carry

    lax.fori_loop(0, rows_pad * cols_pad, features, 0)
    q16 = iota((16, 128), 0)
    kind = jnp.where(q16 >= 3, q16 - 3, q16)

    def tile(t, carry):
        i = t // cols
        j = t - i * cols
        x = pad_ref[0, i + 1, pl.ds(j + 1, 1), :] * KAPPA
        y = pad_ref[1, i + 1, pl.ds(j + 1, 1), :] * KAPPA
        own = cross_rows(x, y, [0, 0, 1, 1, 0, 2], 1.0)
        acc = jnp.zeros((16, 128), F32)
        for w in range(9):
            di, dj = w // 3, w % 3
            sx, sy = di - 1.0, dj - 1.0
            bi = i + di
            bj = j + dj
            weights = jnp.exp2(dot(cols_ref[bi * cols_pad + bj, :, 0:16], own, NN))
            hi = weights.astype(BF16)
            lo = (weights - hi.astype(F32)).astype(BF16)
            bx = pad_ref[0, bi, pl.ds(bj, 1), :] * KAPPA
            by = pad_ref[1, bi, pl.ds(bj, 1), :] * KAPPA
            vx = pad_ref[2, bi, pl.ds(bj, 1), :]
            vy = pad_ref[3, bi, pl.ds(bj, 1), :]
            mass = pad_ref[4, bi, pl.ds(bj, 1), :]
            b_part = mass * jnp.exp2(-2.0 * KAPPA * (sx * bx + sy * by) - bx * bx - by * by)
            rows16 = jnp.broadcast_to(b_part, (16, 128)) * jnp.where(
                kind == 0, 1.0, jnp.where(kind == 1, vx, vy)
            )
            c_hi, c_lo = split2(rows16)
            carried = jnp.where(q16 < 3, c_hi, jnp.where(q16 < 6, c_lo, 0.0)).astype(BF16)
            out = dot(
                jnp.concatenate([carried, carried], 1), jnp.concatenate([hi, lo], 0), NN
            )
            a_part = jnp.exp2(
                2.0 * KAPPA * (sx * x + sy * y)
                - x * x
                - y * y
                - KAPPA * KAPPA * (sx * sx + sy * sy)
            )
            acc = acc + out * (a_part * present_ref[t * 9 + w])
        for k in range(3):
            sums_ref[k, pl.ds(t, 1), :] = acc[k : k + 1] + acc[k + 3 : k + 4]
        return carry

    lax.fori_loop(0, rows * cols, tile, 0)


def pack(dest_ref, vals_ref, rank_ref, send_ref, left_ref, slots_ref, acc_ref):
    groups = dest_ref.shape[0] // 8
    d_iota = iota((128, 128), 0)
    before = jnp.concatenate(
        [
            (iota((128, 128), 0) < iota((128, 128), 1)).astype(F32),
            jnp.ones((128, 128), F32),
        ],
        1,
    ).astype(BF16)
    p_iota = iota((192, 128), 0).astype(F32)
    acc_ref[...] = jnp.zeros_like(acc_ref)

    def group(g, running):
        dest8 = dest_ref[pl.ds(g * 8, 8), :]
        vals8 = [split2(vals_ref[k, pl.ds(g * 8, 8), :]) for k in range(4)]
        ranks = []
        for r in range(8):
            hit = d_iota == jnp.broadcast_to(dest8[r : r + 1], (128, 128))
            counts = dot(jnp.where(hit, 1.0, 0.0).astype(BF16), before, NN)
            rank = jnp.sum(
                jnp.where(hit, counts[:, :128] + running, 0.0), axis=0, keepdims=True
            )
            running = running + counts[:, 128:]
            ranks.append(rank)
            lanes = slice(r * 128, r * 128 + 128)
            slots_ref[:, lanes] = jnp.where(
                p_iota == jnp.broadcast_to(rank, (192, 128)), 1.0, 0.0
            ).astype(BF16)
            for part in range(2):
                for k in range(4):
                    v = jnp.broadcast_to(vals8[k][part][r : r + 1], (128, 128))
                    at = (part * 4 + k) * 128
                    left_ref[at : at + 128, lanes] = jnp.where(hit, v, 0.0).astype(BF16)
        rank_ref[pl.ds(g * 8, 8), :] = jnp.concatenate(ranks, 0)
        acc_ref[:, 0:192] += dot(left_ref[...], slots_ref[...], NT)
        return running

    lax.fori_loop(0, groups, group, jnp.zeros((128, 128), F32))
    tails = []
    for k in range(4):
        send_ref[k] = acc_ref[k * 128 : k * 128 + 128, 0:128] + acc_ref[
            512 + k * 128 : 640 + k * 128, 0:128
        ]
        tails.append(
            acc_ref[k * 128 : k * 128 + 128, 128:256]
            + acc_ref[512 + k * 128 : 640 + k * 128, 128:256]
        )
    low_half = iota((128, 128), 1) < 64
    for h in range(2):
        send_ref[4 + h] = jnp.where(
            low_half, tails[2 * h], pltpu.roll(tails[2 * h + 1], 64, 1)
        )


def particles_kernel(
    pad_ref, present_ref, dest_ref, cell_ref,
    dens_ref, rank_ref, send_ref,
    sums_ref, cols_ref, vals_ref, left_ref, slots_ref, acc_ref,
):
    window_sums(pad_ref, present_ref, sums_ref, cols_ref)
    rows, cols = pad_ref.shape[1] - 2, pad_ref.shape[2] - 2
    for i in range(rows):
        at = slice(i * cols, (i + 1) * cols)
        s0 = sums_ref[0, at, :]
        density = s0 / 128.0
        dens_ref[at, :] = density
        volume = pad_ref[4, i + 1, 1 : cols + 1, :] / density
        vals_ref[0, at, :] = cell_ref[at, :].astype(F32)
        vals_ref[1, at, :] = volume
        vals_ref[2, at, :] = volume * (sums_ref[1, at, :] / s0)
        vals_ref[3, at, :] = volume * (sums_ref[2, at, :] / s0)
    pack(dest_ref, vals_ref, rank_ref, send_ref, left_ref, slots_ref, acc_ref)


def vmem():
    return pl.BlockSpec(memory_space=pltpu.VMEM)


def particles_call(pad, present, dest, cell):
    return pl.pallas_call(
        particles_kernel,
        out_shape=(
            jax.ShapeDtypeStruct((64, 128), F32),
            jax.ShapeDtypeStruct((64, 128), F32),
            jax.ShapeDtypeStruct((6, 128, 128), F32),
        ),
        in_specs=[vmem(), pl.BlockSpec(memory_space=pltpu.SMEM), vmem(), vmem()],
        out_specs=(vmem(), vmem(), vmem()),
        scratch_shapes=[
            pltpu.VMEM((3, 64, 128), F32),
            pltpu.VMEM((pad.shape[1] * pad.shape[2], 128, 128), BF16),
            pltpu.VMEM((4, 64, 128), F32),
            pltpu.VMEM((1024, 1024), BF16),
            pltpu.VMEM((192, 1024), BF16),
            pltpu.VMEM((1024, 256), F32),
        ],
        compiler_params=pltpu.CompilerParams(vmem_limit_bytes=VMEM_LIMIT),
        name="particles",
    )(pad, present, dest, cell)


def unfold(got_ref, out_ref, kinds):
    low_half = iota((64, 128), 1) < 64
    for k in range(kinds):
        out_ref[k, 0:128, :] = got_ref[k]
        row = got_ref[kinds + k // 2]
        first, second = row[0:64], row[64:128]
        if k % 2 == 0:
            out_ref[k, 128:192, :] = jnp.where(low_half, first, pltpu.roll(second, 64, 1))
        else:
            out_ref[k, 128:192, :] = jnp.where(low_half, pltpu.roll(first, 64, 1), second)


ROWS_STEP = 8


def row_and_column(cell):
    row = jnp.floor(cell * (1.0 / 512.0))
    return row, cell - row * 512.0


def deposit_kernel(got_ref, out_ref, slots_ref, left_ref, right_ref, acc_ref):
    unfold(got_ref, slots_ref, 4)
    acc_ref[...] = jnp.zeros_like(acc_ref)
    r_iota = iota((128, 128), 0).astype(F32)
    c_iota = iota((512, 128), 0).astype(F32)

    def step(g, carry):
        at = pl.ds(g * ROWS_STEP, ROWS_STEP)
        row8, col8 = row_and_column(slots_ref[0, at, :])
        vals8 = [split2(slots_ref[1 + k, at, :]) for k in range(3)]
        for r in range(ROWS_STEP):
            lanes = slice(r * 128, r * 128 + 128)
            hit = r_iota == jnp.broadcast_to(row8[r : r + 1], (128, 128))
            for part in range(2):
                for k in range(3):
                    v = jnp.broadcast_to(vals8[k][part][r : r + 1], (128, 128))
                    base = (part * 3 + k) * 128
                    left_ref[base : base + 128, lanes] = jnp.where(hit, v, 0.0).astype(BF16)
            right_ref[:, lanes] = jnp.where(
                c_iota == jnp.broadcast_to(col8[r : r + 1], (512, 128)), 1.0, 0.0
            ).astype(BF16)
        acc_ref[...] += dot(left_ref[...], right_ref[...], NT)
        return carry

    lax.fori_loop(0, 192 // ROWS_STEP, step, 0)
    for k in range(3):
        out_ref[k] = acc_ref[k * 128 : k * 128 + 128, :] + acc_ref[384 + k * 128 : 512 + k * 128, :]


def deposit_call(got):
    width = ROWS_STEP * 128
    return pl.pallas_call(
        deposit_kernel,
        out_shape=jax.ShapeDtypeStruct((3, 128, 512), F32),
        in_specs=[vmem()],
        out_specs=vmem(),
        scratch_shapes=[
            pltpu.VMEM((4, 192, 128), F32),
            pltpu.VMEM((768, width), BF16),
            pltpu.VMEM((512, width), BF16),
            pltpu.VMEM((768, 512), F32),
        ],
        compiler_params=pltpu.CompilerParams(vmem_limit_bytes=VMEM_LIMIT),
        name="deposit",
    )(got)


def lookup_kernel(got_ref, state_ref, back_ref, cells_ref, table_ref, found_ref):
    cells_ref[0:128, :] = got_ref[0]
    low_half = iota((64, 128), 1) < 64
    tail = got_ref[4]
    cells_ref[128:192, :] = jnp.where(low_half, tail[0:64], pltpu.roll(tail[64:128], 64, 1))
    for k in range(3):
        hi, lo = split2(state_ref[k])
        table_ref[k * 128 : k * 128 + 128, 0:512] = hi.astype(BF16)
        table_ref[k * 128 : k * 128 + 128, 512:1024] = lo.astype(BF16)
    r_iota = iota((128, 128), 0).astype(F32)
    c_iota = iota((512, 128), 0).astype(F32)

    def step(g, carry):
        at = pl.ds(g * 8, 8)
        row8, col8 = row_and_column(cells_ref[at, :])
        found = [[], [], []]
        for pair in range(4):
            right = jnp.concatenate(
                [
                    jnp.where(
                        c_iota == jnp.broadcast_to(col8[r : r + 1], (512, 128)), 1.0, 0.0
                    ).astype(BF16)
                    for r in (2 * pair, 2 * pair + 1)
                ],
                1,
            )
            got = dot(table_ref[...], jnp.concatenate([right, right], 0), NN)
            for k in range(3):
                for h in range(2):
                    r = 2 * pair + h
                    hit = r_iota == jnp.broadcast_to(row8[r : r + 1], (128, 128))
                    part = got[k * 128 : k * 128 + 128, h * 128 : h * 128 + 128]
                    found[k].append(jnp.sum(jnp.where(hit, part, 0.0), axis=0, keepdims=True))
        for k in range(3):
            found_ref[k, at, :] = jnp.concatenate(found[k], 0)
        return carry

    lax.fori_loop(0, 24, step, 0)
    tails = [found_ref[k, 128:192, :] for k in range(3)]
    for k in range(3):
        back_ref[k] = found_ref[k, 0:128, :]
    turned = [pltpu.roll(t, 64, 1) for t in tails]
    back_ref[3, 0:64, :] = jnp.where(low_half, tails[0], turned[1])
    back_ref[3, 64:128, :] = jnp.where(low_half, turned[0], tails[1])
    back_ref[4, 0:64, :] = tails[2]
    back_ref[4, 64:128, :] = turned[2]


def lookup_call(got, state):
    return pl.pallas_call(
        lookup_kernel,
        out_shape=jax.ShapeDtypeStruct((5, 128, 128), F32),
        in_specs=[vmem(), vmem()],
        out_specs=vmem(),
        scratch_shapes=[
            pltpu.VMEM((192, 128), F32),
            pltpu.VMEM((384, 1024), BF16),
            pltpu.VMEM((3, 192, 128), F32),
        ],
        compiler_params=pltpu.CompilerParams(vmem_limit_bytes=VMEM_LIMIT),
        name="lookup",
    )(got, state)


def unpack_kernel(back_ref, dest_ref, rank_ref, out_ref, table_ref):
    turned = pltpu.roll(back_ref[3], 64, 1)
    tails = [back_ref[3], turned, back_ref[4]]
    for k in range(3):
        for part, piece in enumerate(split2(back_ref[k])):
            table_ref[k * 128 : k * 128 + 128, part * 192 : part * 192 + 128] = piece.astype(BF16)
        for part, piece in enumerate(split2(tails[k])):
            table_ref[
                k * 128 : k * 128 + 128, part * 192 + 128 : part * 192 + 192
            ] = piece[:, 0:64].astype(BF16)
    d_iota = iota((128, 128), 0)
    p_iota = iota((192, 128), 0).astype(F32)

    def step(g, carry):
        at = pl.ds(g * 8, 8)
        dest8 = dest_ref[at, :]
        rank8 = rank_ref[at, :]
        found = [[], [], []]
        for pair in range(4):
            slots = jnp.concatenate(
                [
                    jnp.where(
                        p_iota == jnp.broadcast_to(rank8[r : r + 1], (192, 128)), 1.0, 0.0
                    ).astype(BF16)
                    for r in (2 * pair, 2 * pair + 1)
                ],
                1,
            )
            got = dot(table_ref[...], jnp.concatenate([slots, slots], 0), NN)
            for k in range(3):
                for h in range(2):
                    r = 2 * pair + h
                    hit = d_iota == jnp.broadcast_to(dest8[r : r + 1], (128, 128))
                    part = got[k * 128 : k * 128 + 128, h * 128 : h * 128 + 128]
                    found[k].append(jnp.sum(jnp.where(hit, part, 0.0), axis=0, keepdims=True))
        for k in range(3):
            out_ref[k, at, :] = jnp.concatenate(found[k], 0)
        return carry

    lax.fori_loop(0, dest_ref.shape[0] // 8, step, 0)


def unpack_call(back, dest, rank):
    return pl.pallas_call(
        unpack_kernel,
        out_shape=jax.ShapeDtypeStruct((3, 64, 128), F32),
        in_specs=[vmem(), vmem(), vmem()],
        out_specs=vmem(),
        scratch_shapes=[pltpu.VMEM((384, 384), BF16)],
        compiler_params=pltpu.CompilerParams(vmem_limit_bytes=VMEM_LIMIT),
        name="unpack",
    )(back, dest, rank)


def padded_2(cells, sides, width):
    for axis, dim in sides:
        count = lax.axis_size(axis)
        ends = count - 1
        head = lax.slice_in_dim(cells, 0, width, axis=dim)
        tail = lax.slice_in_dim(cells, cells.shape[dim] - width, cells.shape[dim], axis=dim)
        cells = jnp.concatenate(
            [
                lax.ppermute(tail, axis, [(i, (i + 1) % count) for i in range(ends)]),
                cells,
                lax.ppermute(head, axis, [((i + 1) % count, i) for i in range(ends)]),
            ],
            axis=dim,
        )
    return cells


def lax_friedrichs(state_pad, depth_pad):
    height = state_pad[0]
    speed_x = state_pad[1]
    speed_y = state_pad[2]
    flux_x = depth_pad * speed_x
    flux_y = depth_pad * speed_y

    def average(quantity):
        return 0.25 * (
            quantity[2:, 1:-1] + quantity[:-2, 1:-1] + quantity[1:-1, 2:] + quantity[1:-1, :-2]
        )

    next_height = average(height) - 0.5 * courant * (
        flux_x[2:, 1:-1] - flux_x[:-2, 1:-1] + flux_y[1:-1, 2:] - flux_y[1:-1, :-2]
    )
    next_speed_x = average(speed_x) - 0.5 * courant * (height[2:, 1:-1] - height[:-2, 1:-1])
    next_speed_y = average(speed_y) - 0.5 * courant * (height[1:-1, 2:] - height[1:-1, :-2])
    return jnp.stack([next_height, next_speed_x, next_speed_y])


def shards(
    offsets, velocity, particle_mass, neighbours, owner_device, target_cell, surface, water_depth
):
    stacked = jnp.concatenate([offsets, velocity, particle_mass[None]], axis=0)
    padded = padded_2(stacked, (("along", 1), ("cross", 2)), 1)
    present = jnp.any(
        neighbours[..., :, None] == jnp.arange(9, dtype=jnp.int32), axis=-2
    ).astype(F32)
    dest = owner_device.reshape(64, 128)
    cell = target_cell.reshape(64, 128)
    density, rank, send = particles_call(padded, present.reshape(-1), dest, cell)
    got = lax.all_to_all(send, ("along", "cross"), split_axis=1, concat_axis=1, tiled=True)
    grid_source = deposit_call(got)
    depth_pad = padded_2(water_depth, (("along", 0), ("cross", 1)), 1)
    water_state = surface
    for substep in range(SUBSTEPS):
        state_pad = padded_2(water_state, (("along", 1), ("cross", 2)), 1)
        water_state = lax_friedrichs(state_pad, depth_pad) + grid_source
    back = lookup_call(got, water_state)
    back = lax.all_to_all(back, ("along", "cross"), split_axis=1, concat_axis=1, tiled=True)
    feedback = unpack_call(back, dest, rank)
    return (
        water_state,
        density.reshape(particle_mass.shape),
        feedback.reshape((3,) + particle_mass.shape),
    )


def solution(mesh):
    in_specs = (
        P(None, "along", "cross", None),
        P(None, "along", "cross", None),
        P("along", "cross", None),
        P("along", "cross", None),
        P("along", "cross", None, None),
        P("along", "cross", None),
        P(None, "along", "cross"),
        P("along", "cross"),
    )
    out_specs = (
        P(None, "along", "cross"),
        P("along", "cross", None),
        P(None, "along", "cross", None),
    )
    return jax.shard_map(shards, mesh=mesh, in_specs=in_specs, out_specs=out_specs, check_vma=False)
```

```python
import math

import jax
import jax.numpy as jnp
from jax import lax
from jax.experimental import pallas as pl
from jax.experimental.pallas import tpu as pltpu
from jax.sharding import PartitionSpec as P

SUBSTEPS = 4
KAPPA = math.sqrt(math.log2(math.e))
F32 = jnp.float32
BF16 = jnp.bfloat16
NN = (((1,), (0,)), ((), ()))
NT = (((1,), (1,)), ((), ()))
VMEM_LIMIT = 56 * 1024 * 1024

courant = 0.4


def dot(a, b, dims):
    return lax.dot_general(a, b, dims, preferred_element_type=F32)


def split2(x):
    hi = x.astype(BF16).astype(F32)
    return hi, x - hi


def iota(shape, dim):
    return lax.broadcasted_iota(jnp.int32, shape, dim)


def cross_rows(x, y, pattern, scale):
    q = iota((16, 128), 0)
    v = jnp.where(q < 6, jnp.broadcast_to(x, (16, 128)), jnp.broadcast_to(y, (16, 128)))
    hi, rest = split2(v)
    mid, low = split2(rest)
    out = jnp.zeros((16, 128), F32)
    for r, p in enumerate(pattern * 2):
        out = jnp.where(q == r, (hi, mid, low)[p], out)
    return (out * scale).astype(BF16)


def window_sums(pad_ref, present_ref, sums_ref, cols_ref):
    rows_pad, cols_pad = pad_ref.shape[1], pad_ref.shape[2]
    rows, cols = rows_pad - 2, cols_pad - 2

    def features(g, carry):
        i = g // cols_pad
        j = g - i * cols_pad
        x = pad_ref[0, i, pl.ds(j, 1), :] * KAPPA
        y = pad_ref[1, i, pl.ds(j, 1), :] * KAPPA
        feats = cross_rows(x, y, [0, 1, 0, 1, 2, 0], 2.0)
        cols_ref[g, :, 0:16] = feats.astype(F32).T.astype(BF16)
        return carry

    lax.fori_loop(0, rows_pad * cols_pad, features, 0)
    q16 = iota((16, 128), 0)
    kind = jnp.where(q16 >= 3, q16 - 3, q16)

    def tile(t, carry):
        i = t // cols
        j = t - i * cols
        x = pad_ref[0, i + 1, pl.ds(j + 1, 1), :] * KAPPA
        y = pad_ref[1, i + 1, pl.ds(j + 1, 1), :] * KAPPA
        own = cross_rows(x, y, [0, 0, 1, 1, 0, 2], 1.0)
        acc = jnp.zeros((16, 128), F32)
        for w in range(9):
            di, dj = w // 3, w % 3
            sx, sy = di - 1.0, dj - 1.0
            bi = i + di
            bj = j + dj
            weights = jnp.exp2(dot(cols_ref[bi * cols_pad + bj, :, 0:16], own, NN))
            hi = weights.astype(BF16)
            lo = (weights - hi.astype(F32)).astype(BF16)
            bx = pad_ref[0, bi, pl.ds(bj, 1), :] * KAPPA
            by = pad_ref[1, bi, pl.ds(bj, 1), :] * KAPPA
            vx = pad_ref[2, bi, pl.ds(bj, 1), :]
            vy = pad_ref[3, bi, pl.ds(bj, 1), :]
            mass = pad_ref[4, bi, pl.ds(bj, 1), :]
            b_part = mass * jnp.exp2(-2.0 * KAPPA * (sx * bx + sy * by) - bx * bx - by * by)
            rows16 = jnp.broadcast_to(b_part, (16, 128)) * jnp.where(
                kind == 0, 1.0, jnp.where(kind == 1, vx, vy)
            )
            c_hi, c_lo = split2(rows16)
            carried = jnp.where(q16 < 3, c_hi, jnp.where(q16 < 6, c_lo, 0.0)).astype(BF16)
            out = dot(
                jnp.concatenate([carried, carried], 1), jnp.concatenate([hi, lo], 0), NN
            )
            a_part = jnp.exp2(
                2.0 * KAPPA * (sx * x + sy * y)
                - x * x
                - y * y
                - KAPPA * KAPPA * (sx * sx + sy * sy)
            )
            acc = acc + out * (a_part * present_ref[t * 9 + w])
        for k in range(3):
            sums_ref[k, pl.ds(t, 1), :] = acc[k : k + 1] + acc[k + 3 : k + 4]
        return carry

    lax.fori_loop(0, rows * cols, tile, 0)


def pack(dest_ref, vals_ref, rank_ref, send_ref, left_ref, slots_ref, acc_ref):
    groups = dest_ref.shape[0] // 8
    d_iota = iota((128, 128), 0)
    before = jnp.concatenate(
        [
            (iota((128, 128), 0) < iota((128, 128), 1)).astype(F32),
            jnp.ones((128, 128), F32),
        ],
        1,
    ).astype(BF16)
    p_iota = iota((192, 128), 0).astype(F32)
    acc_ref[...] = jnp.zeros_like(acc_ref)

    def group(g, running):
        dest8 = dest_ref[pl.ds(g * 8, 8), :]
        vals8 = [split2(vals_ref[k, pl.ds(g * 8, 8), :]) for k in range(4)]
        ranks = []
        for r in range(8):
            hit = d_iota == jnp.broadcast_to(dest8[r : r + 1], (128, 128))
            counts = dot(jnp.where(hit, 1.0, 0.0).astype(BF16), before, NN)
            rank = jnp.sum(
                jnp.where(hit, counts[:, :128] + running, 0.0), axis=0, keepdims=True
            )
            running = running + counts[:, 128:]
            ranks.append(rank)
            lanes = slice(r * 128, r * 128 + 128)
            slots_ref[:, lanes] = jnp.where(
                p_iota == jnp.broadcast_to(rank, (192, 128)), 1.0, 0.0
            ).astype(BF16)
            for part in range(2):
                for k in range(4):
                    v = jnp.broadcast_to(vals8[k][part][r : r + 1], (128, 128))
                    at = (part * 4 + k) * 128
                    left_ref[at : at + 128, lanes] = jnp.where(hit, v, 0.0).astype(BF16)
        rank_ref[pl.ds(g * 8, 8), :] = jnp.concatenate(ranks, 0)
        acc_ref[:, 0:192] += dot(left_ref[...], slots_ref[...], NT)
        return running

    lax.fori_loop(0, groups, group, jnp.zeros((128, 128), F32))
    tails = []
    for k in range(4):
        send_ref[pl.ds(k, 128, stride=8), :] = acc_ref[k * 128 : k * 128 + 128, 0:128] + acc_ref[
            512 + k * 128 : 640 + k * 128, 0:128
        ]
        tails.append(
            acc_ref[k * 128 : k * 128 + 128, 128:256]
            + acc_ref[512 + k * 128 : 640 + k * 128, 128:256]
        )
    low_half = iota((128, 128), 1) < 64
    for k in range(6, 8):
        send_ref[pl.ds(k, 128, stride=8), :] = jnp.zeros((128, 128), F32)
    for h in range(2):
        send_ref[pl.ds(4 + h, 128, stride=8), :] = jnp.where(
            low_half, tails[2 * h], pltpu.roll(tails[2 * h + 1], 64, 1)
        )


def particles_kernel(
    pad_ref, present_ref, dest_ref, cell_ref,
    dens_ref, rank_ref, send_ref,
    sums_ref, cols_ref, vals_ref, left_ref, slots_ref, acc_ref,
):
    window_sums(pad_ref, present_ref, sums_ref, cols_ref)
    rows, cols = pad_ref.shape[1] - 2, pad_ref.shape[2] - 2
    for i in range(rows):
        at = slice(i * cols, (i + 1) * cols)
        s0 = sums_ref[0, at, :]
        density = s0 / 128.0
        dens_ref[at, :] = density
        volume = pad_ref[4, i + 1, 1 : cols + 1, :] / density
        vals_ref[0, at, :] = cell_ref[at, :].astype(F32)
        vals_ref[1, at, :] = volume
        vals_ref[2, at, :] = volume * (sums_ref[1, at, :] / s0)
        vals_ref[3, at, :] = volume * (sums_ref[2, at, :] / s0)
    pack(dest_ref, vals_ref, rank_ref, send_ref, left_ref, slots_ref, acc_ref)


def vmem():
    return pl.BlockSpec(memory_space=pltpu.VMEM)


def particles_call(pad, present, dest, cell):
    return pl.pallas_call(
        particles_kernel,
        out_shape=(
            jax.ShapeDtypeStruct((64, 128), F32),
            jax.ShapeDtypeStruct((64, 128), F32),
            jax.ShapeDtypeStruct((1024, 128), F32),
        ),
        in_specs=[vmem(), pl.BlockSpec(memory_space=pltpu.SMEM), vmem(), vmem()],
        out_specs=(vmem(), vmem(), vmem()),
        scratch_shapes=[
            pltpu.VMEM((3, 64, 128), F32),
            pltpu.VMEM((pad.shape[1] * pad.shape[2], 128, 128), BF16),
            pltpu.VMEM((4, 64, 128), F32),
            pltpu.VMEM((1024, 1024), BF16),
            pltpu.VMEM((192, 1024), BF16),
            pltpu.VMEM((1024, 256), F32),
        ],
        compiler_params=pltpu.CompilerParams(vmem_limit_bytes=VMEM_LIMIT),
        name="particles",
    )(pad, present, dest, cell)


def unfold(got_ref, out_ref, kinds):
    low_half = iota((64, 128), 1) < 64
    for k in range(kinds):
        out_ref[k, 0:128, :] = got_ref[pl.ds(k, 128, stride=8), :]
        row = got_ref[pl.ds(kinds + k // 2, 128, stride=8), :]
        first, second = row[0:64], row[64:128]
        if k % 2 == 0:
            out_ref[k, 128:192, :] = jnp.where(low_half, first, pltpu.roll(second, 64, 1))
        else:
            out_ref[k, 128:192, :] = jnp.where(low_half, pltpu.roll(first, 64, 1), second)


ROWS_STEP = 8


def row_and_column(cell):
    row = jnp.floor(cell * (1.0 / 512.0))
    return row, cell - row * 512.0


def deposit_kernel(got_ref, out_ref, slots_ref, left_ref, right_ref, acc_ref):
    unfold(got_ref, slots_ref, 4)
    acc_ref[...] = jnp.zeros_like(acc_ref)
    r_iota = iota((128, 128), 0).astype(F32)
    c_iota = iota((512, 128), 0).astype(F32)

    def step(g, carry):
        at = pl.ds(g * ROWS_STEP, ROWS_STEP)
        row8, col8 = row_and_column(slots_ref[0, at, :])
        vals8 = [split2(slots_ref[1 + k, at, :]) for k in range(3)]
        for r in range(ROWS_STEP):
            lanes = slice(r * 128, r * 128 + 128)
            hit = r_iota == jnp.broadcast_to(row8[r : r + 1], (128, 128))
            for part in range(2):
                for k in range(3):
                    v = jnp.broadcast_to(vals8[k][part][r : r + 1], (128, 128))
                    base = (part * 3 + k) * 128
                    left_ref[base : base + 128, lanes] = jnp.where(hit, v, 0.0).astype(BF16)
            right_ref[:, lanes] = jnp.where(
                c_iota == jnp.broadcast_to(col8[r : r + 1], (512, 128)), 1.0, 0.0
            ).astype(BF16)
        acc_ref[...] += dot(left_ref[...], right_ref[...], NT)
        return carry

    lax.fori_loop(0, 192 // ROWS_STEP, step, 0)
    for k in range(3):
        out_ref[k] = acc_ref[k * 128 : k * 128 + 128, :] + acc_ref[384 + k * 128 : 512 + k * 128, :]


def deposit_call(got):
    width = ROWS_STEP * 128
    return pl.pallas_call(
        deposit_kernel,
        out_shape=jax.ShapeDtypeStruct((3, 128, 512), F32),
        in_specs=[vmem()],
        out_specs=vmem(),
        scratch_shapes=[
            pltpu.VMEM((4, 192, 128), F32),
            pltpu.VMEM((768, width), BF16),
            pltpu.VMEM((512, width), BF16),
            pltpu.VMEM((768, 512), F32),
        ],
        compiler_params=pltpu.CompilerParams(vmem_limit_bytes=VMEM_LIMIT),
        name="deposit",
    )(got)


def lookup_kernel(got_ref, state_ref, back_ref, cells_ref, table_ref, found_ref):
    cells_ref[0:128, :] = got_ref[pl.ds(0, 128, stride=8), :]
    low_half = iota((64, 128), 1) < 64
    tail = got_ref[pl.ds(4, 128, stride=8), :]
    cells_ref[128:192, :] = jnp.where(low_half, tail[0:64], pltpu.roll(tail[64:128], 64, 1))
    for k in range(3):
        hi, lo = split2(state_ref[k])
        table_ref[k * 128 : k * 128 + 128, 0:512] = hi.astype(BF16)
        table_ref[k * 128 : k * 128 + 128, 512:1024] = lo.astype(BF16)
    r_iota = iota((128, 128), 0).astype(F32)
    c_iota = iota((512, 128), 0).astype(F32)

    def step(g, carry):
        at = pl.ds(g * 8, 8)
        row8, col8 = row_and_column(cells_ref[at, :])
        found = [[], [], []]
        for pair in range(4):
            right = jnp.concatenate(
                [
                    jnp.where(
                        c_iota == jnp.broadcast_to(col8[r : r + 1], (512, 128)), 1.0, 0.0
                    ).astype(BF16)
                    for r in (2 * pair, 2 * pair + 1)
                ],
                1,
            )
            got = dot(table_ref[...], jnp.concatenate([right, right], 0), NN)
            for k in range(3):
                for h in range(2):
                    r = 2 * pair + h
                    hit = r_iota == jnp.broadcast_to(row8[r : r + 1], (128, 128))
                    part = got[k * 128 : k * 128 + 128, h * 128 : h * 128 + 128]
                    found[k].append(jnp.sum(jnp.where(hit, part, 0.0), axis=0, keepdims=True))
        for k in range(3):
            found_ref[k, at, :] = jnp.concatenate(found[k], 0)
        return carry

    lax.fori_loop(0, 24, step, 0)
    tails = [found_ref[k, 128:192, :] for k in range(3)]
    for k in range(3):
        back_ref[pl.ds(k, 128, stride=8), :] = found_ref[k, 0:128, :]
    turned = [pltpu.roll(t, 64, 1) for t in tails]
    back_ref[pl.ds(3, 64, stride=8), :] = jnp.where(low_half, tails[0], turned[1])
    back_ref[pl.ds(515, 64, stride=8), :] = jnp.where(low_half, turned[0], tails[1])
    back_ref[pl.ds(4, 64, stride=8), :] = tails[2]
    back_ref[pl.ds(516, 64, stride=8), :] = turned[2]
    for k in range(5, 8):
        back_ref[pl.ds(k, 128, stride=8), :] = jnp.zeros((128, 128), F32)


def lookup_call(got, state):
    return pl.pallas_call(
        lookup_kernel,
        out_shape=jax.ShapeDtypeStruct((1024, 128), F32),
        in_specs=[vmem(), vmem()],
        out_specs=vmem(),
        scratch_shapes=[
            pltpu.VMEM((192, 128), F32),
            pltpu.VMEM((384, 1024), BF16),
            pltpu.VMEM((3, 192, 128), F32),
        ],
        compiler_params=pltpu.CompilerParams(vmem_limit_bytes=VMEM_LIMIT),
        name="lookup",
    )(got, state)


def unpack_kernel(back_ref, dest_ref, rank_ref, out_ref, table_ref):
    tail = back_ref[pl.ds(3, 128, stride=8), :]
    tails = [tail, pltpu.roll(tail, 64, 1), back_ref[pl.ds(4, 128, stride=8), :]]
    for k in range(3):
        for part, piece in enumerate(split2(back_ref[pl.ds(k, 128, stride=8), :])):
            table_ref[k * 128 : k * 128 + 128, part * 192 : part * 192 + 128] = piece.astype(BF16)
        for part, piece in enumerate(split2(tails[k])):
            table_ref[
                k * 128 : k * 128 + 128, part * 192 + 128 : part * 192 + 192
            ] = piece[:, 0:64].astype(BF16)
    d_iota = iota((128, 128), 0)
    p_iota = iota((192, 128), 0).astype(F32)

    def step(g, carry):
        at = pl.ds(g * 8, 8)
        dest8 = dest_ref[at, :]
        rank8 = rank_ref[at, :]
        found = [[], [], []]
        for pair in range(4):
            slots = jnp.concatenate(
                [
                    jnp.where(
                        p_iota == jnp.broadcast_to(rank8[r : r + 1], (192, 128)), 1.0, 0.0
                    ).astype(BF16)
                    for r in (2 * pair, 2 * pair + 1)
                ],
                1,
            )
            got = dot(table_ref[...], jnp.concatenate([slots, slots], 0), NN)
            for k in range(3):
                for h in range(2):
                    r = 2 * pair + h
                    hit = d_iota == jnp.broadcast_to(dest8[r : r + 1], (128, 128))
                    part = got[k * 128 : k * 128 + 128, h * 128 : h * 128 + 128]
                    found[k].append(jnp.sum(jnp.where(hit, part, 0.0), axis=0, keepdims=True))
        for k in range(3):
            out_ref[k, at, :] = jnp.concatenate(found[k], 0)
        return carry

    lax.fori_loop(0, dest_ref.shape[0] // 8, step, 0)


def unpack_call(back, dest, rank):
    return pl.pallas_call(
        unpack_kernel,
        out_shape=jax.ShapeDtypeStruct((3, 64, 128), F32),
        in_specs=[vmem(), vmem(), vmem()],
        out_specs=vmem(),
        scratch_shapes=[pltpu.VMEM((384, 384), BF16)],
        compiler_params=pltpu.CompilerParams(vmem_limit_bytes=VMEM_LIMIT),
        name="unpack",
    )(back, dest, rank)


MESH = pl.DeviceIdType.MESH
AROUND = [(-1, 0), (1, 0), (0, -1), (0, 1), (-1, -1), (-1, 1), (1, -1), (1, 1)]


def my_place():
    return lax.axis_index("along"), lax.axis_index("cross")


def sizes():
    return lax.axis_size("along"), lax.axis_size("cross")


def at_step(step):
    (a, c), (na, nc) = my_place(), sizes()
    return lax.rem(a + step[0] + na, na), lax.rem(c + step[1] + nc, nc)


def greet_around():
    barrier = pltpu.get_barrier_semaphore()
    for step in AROUND:
        pl.semaphore_signal(barrier, inc=1, device_id=at_step(step), device_id_type=MESH)
    pl.semaphore_wait(barrier, len(AROUND))


def rim_copies(out_refs, in_refs, send_sem, recv_sem):
    copies = []
    for n, step in enumerate(AROUND):
        opposite = AROUND.index((-step[0], -step[1]))
        copies.append(
            pltpu.make_async_remote_copy(
                src_ref=out_refs[n],
                dst_ref=in_refs[opposite],
                send_sem=send_sem.at[n],
                recv_sem=recv_sem.at[opposite],
                device_id=at_step(step),
                device_id_type=MESH,
            )
        )
    return copies


DEEP = 4
SIDE_PARTICLES = 24


def column_strip(fields, right):
    lanes = iota((fields[0].shape[0], 128), 1)
    out = jnp.zeros((fields[0].shape[0], 128), F32)
    for f, field in enumerate(fields):
        turn = DEEP * f + (DEEP if right else 0)
        moved = pltpu.roll(field, turn, 1) if turn else field
        out = jnp.where((lanes >= DEEP * f) & (lanes < DEEP * f + DEEP), moved, out)
    return out


def write_rims(out_refs, base, fields):
    top, bottom = slice(0, 8), slice(120, 128)
    for n, rows in ((0, top), (1, bottom)):
        for f, field in enumerate(fields):
            for b in range(4):
                at = base[n] + (f * 4 + b) * 8
                out_refs[n][at : at + 8, :] = field(rows, slice(b * 128, b * 128 + 128))
    for right in range(2):
        lanes = slice(384, 512) if right else slice(0, 128)
        strip = column_strip([field(slice(0, 128), lanes) for field in fields], right == 1)
        at = base[2 + right]
        out_refs[2 + right][at : at + 128, :] = strip
        out_refs[4 + right][base[4] : base[4] + 8, :] = strip[0:8]
        out_refs[6 + right][base[4] : base[4] + 8, :] = strip[120:128]


def rims_kernel(
    off_ref, vel_ref, mass_ref, surface_ref, depth_ref,
    pad_ref, up_ref, down_ref, left_ref, right_ref, c0_ref, c1_ref, c2_ref, c3_ref,
    o0, o1, o2, o3, o4, o5, o6, o7, i0, i1, i2, i3, i4, i5, i6, i7, send_sem, recv_sem,
):
    outs = [o0, o1, o2, o3, o4, o5, o6, o7]
    ins = [i0, i1, i2, i3, i4, i5, i6, i7]
    rows, cols = mass_ref.shape[0], mass_ref.shape[1]
    particle = [
        (off_ref, 0), (off_ref, 1), (vel_ref, 0), (vel_ref, 1), (mass_ref, None),
    ]

    def tiles(f, i, j):
        ref, part = particle[f]
        return ref[i, j, :] if part is None else ref[part, i, j, :]

    everything = slice(0, cols)
    for f in range(5):
        outs[0][f * cols : (f + 1) * cols, :] = tiles(f, 0, everything)
        outs[1][f * cols : (f + 1) * cols, :] = tiles(f, rows - 1, everything)
        for side, j in ((0, slice(0, 1)), (1, slice(cols - 1, cols))):
            for i in range(rows):
                outs[2 + side][f * rows + i : f * rows + i + 1, :] = tiles(f, i, j)
            outs[4 + side][f : f + 1, :] = tiles(f, 0, j)
            outs[6 + side][f : f + 1, :] = tiles(f, rows - 1, j)
    for side in range(2):
        outs[2 + side][5 * rows :SIDE_PARTICLES, :] = jnp.zeros((SIDE_PARTICLES - 5 * rows, 128), F32)
        outs[4 + side][5:8, :] = jnp.zeros((3, 128), F32)
        outs[6 + side][5:8, :] = jnp.zeros((3, 128), F32)
    fields = [
        lambda r, c: surface_ref[0, r, c],
        lambda r, c: surface_ref[1, r, c],
        lambda r, c: surface_ref[2, r, c],
        lambda r, c: depth_ref[r, c],
    ]
    write_rims(outs, [5 * cols, 5 * cols, SIDE_PARTICLES, SIDE_PARTICLES, 8], fields)
    greet_around()
    copies = rim_copies(outs, ins, send_sem, recv_sem)
    for copy in copies:
        copy.start()
    for f in range(5):
        for i in range(rows):
            pad_ref[f, i + 1, 1 : cols + 1, :] = tiles(f, i, everything)
    for copy in copies:
        copy.wait()
    (a, c), (na, nc) = my_place(), sizes()
    inside = [a > 0, a < na - 1, c > 0, c < nc - 1]

    def kept(f, value, *tests):
        if f < 4:
            return value
        for test in tests:
            value = jnp.where(test, value, 0.0)
        return value

    for f in range(5):
        pad_ref[f, 0, 1 : cols + 1, :] = kept(f, ins[0][f * cols : (f + 1) * cols, :], inside[0])
        pad_ref[f, rows + 1, 1 : cols + 1, :] = kept(f, ins[1][f * cols : (f + 1) * cols, :], inside[1])
        for side, j in ((0, 0), (1, cols + 1)):
            for i in range(rows):
                pad_ref[f, i + 1, j : j + 1, :] = kept(
                    f, ins[2 + side][f * rows + i : f * rows + i + 1, :], inside[2 + side]
                )
            pad_ref[f, 0, j : j + 1, :] = kept(f, ins[4 + side][f : f + 1, :], inside[0], inside[2 + side])
            pad_ref[f, rows + 1, j : j + 1, :] = kept(f, ins[6 + side][f : f + 1, :], inside[1], inside[2 + side])
    up_ref[...] = ins[0][5 * cols : 5 * cols + 128, :]
    down_ref[...] = ins[1][5 * cols : 5 * cols + 128, :]
    left_ref[...] = ins[2][SIDE_PARTICLES : SIDE_PARTICLES + 128, :]
    right_ref[...] = ins[3][SIDE_PARTICLES : SIDE_PARTICLES + 128, :]
    for n, ref in enumerate((c0_ref, c1_ref, c2_ref, c3_ref)):
        ref[...] = ins[4 + n][8:16, :]


def rims_call(offsets, velocity, mass, surface, depth):
    rows, cols = mass.shape[0], mass.shape[1]
    tall, wide, corner = 5 * cols + 128, SIDE_PARTICLES + 128, 16
    heights = [tall, tall, wide, wide, corner, corner, corner, corner]
    buffers = [pltpu.VMEM((h, 128), F32) for h in heights]
    return pl.pallas_call(
        rims_kernel,
        out_shape=(
            jax.ShapeDtypeStruct((5, rows + 2, cols + 2, 128), F32),
            *[jax.ShapeDtypeStruct((128, 128), F32)] * 4,
            *[jax.ShapeDtypeStruct((8, 128), F32)] * 4,
        ),
        in_specs=[vmem()] * 5,
        out_specs=tuple([vmem()] * 9),
        scratch_shapes=[
            *buffers,
            *buffers,
            pltpu.SemaphoreType.DMA((8,)),
            pltpu.SemaphoreType.DMA((8,)),
        ],
        compiler_params=pltpu.CompilerParams(
            vmem_limit_bytes=VMEM_LIMIT, collective_id=0, has_side_effects=True
        ),
        name="rims",
    )(offsets, velocity, mass, surface, depth)


def exchange_kernel(out_ref, in_ref, send_sem, recv_sem):
    (a, c), (na, nc) = my_place(), sizes()
    count = na * nc
    me = a * nc + c

    def block(ref, n):
        return ref.at[pl.ds(pl.multiple_of(n * 8, 8), 8), :]

    def start(step, carry):
        to = lax.rem(me + step, count)
        pltpu.make_async_remote_copy(
            src_ref=block(out_ref, to),
            dst_ref=block(in_ref, me),
            send_sem=send_sem,
            recv_sem=recv_sem,
            device_id=(lax.div(to, nc), lax.rem(to, nc)),
            device_id_type=MESH,
        ).start()
        return carry

    lax.fori_loop(1, count, start, 0)
    own = pl.ds(pl.multiple_of(me * 8, 8), 8)
    in_ref[own, :] = out_ref[own, :]
    most = (count - 1) * 8
    pltpu.make_async_copy(out_ref.at[0:most, :], out_ref.at[0:most, :], send_sem).wait()
    pltpu.make_async_copy(in_ref.at[0:most, :], in_ref.at[0:most, :], recv_sem).wait()


def exchange_call(blocks, name):
    return pl.pallas_call(
        exchange_kernel,
        out_shape=jax.ShapeDtypeStruct(blocks.shape, F32),
        in_specs=[vmem()],
        out_specs=vmem(),
        scratch_shapes=[pltpu.SemaphoreType.DMA, pltpu.SemaphoreType.DMA],
        compiler_params=pltpu.CompilerParams(
            vmem_limit_bytes=VMEM_LIMIT, has_side_effects=True
        ),
        name=name,
    )(blocks)


TALL = 160
BROAD = 768
FIRST = 16


def place_rims(wide_ref, index, f, refs, bases):
    up, down, left, right, *corners = refs
    for b in range(4):
        lanes = slice(128 + b * 128, 256 + b * 128)
        at = (f * 4 + b) * 8
        wide_ref[index, FIRST - 8 : FIRST, lanes] = up[bases[0] + at : bases[0] + at + 8, :]
        wide_ref[index, FIRST + 128 : FIRST + 136, lanes] = down[bases[0] + at : bases[0] + at + 8, :]
    for side in range(2):
        lanes = slice(0, 128) if side == 0 else slice(BROAD - 128, BROAD)
        turn = (128 - DEEP - DEEP * f) % 128 if side == 0 else (128 - DEEP * f) % 128
        for rows, ref, base in (
            (slice(FIRST, FIRST + 128), (left, right)[side], bases[1]),
            (slice(FIRST - 8, FIRST), corners[side], bases[2]),
            (slice(FIRST + 128, FIRST + 136), corners[2 + side], bases[2]),
        ):
            value = ref[base : base + rows.stop - rows.start, :]
            wide_ref[index, rows, lanes] = pltpu.roll(value, turn, 1) if turn else value


def water_step(old_ref, new_ref, depth_ref, source_ref, with_source):
    (a, c), (na, nc) = my_place(), sizes()
    cols = iota((8, BROAD), 1) + (c * 512 - 128)
    cols_in = (cols >= 0) & (cols < nc * 512)

    def rows8(rb, carry):
        start = pl.multiple_of(rb * 8, 8)
        three = pl.ds(pl.multiple_of(rb * 8 - 8, 8), 24)
        h3, u3, v3 = [old_ref[f, three, :] for f in range(3)]
        fu3 = depth_ref[0, three, :] * u3
        h, u, v = h3[8:16], u3[8:16], v3[8:16]
        fv = depth_ref[0, pl.ds(start, 8), :] * v

        def left(x):
            return pltpu.roll(x, 1, 1)

        def right(x):
            return pltpu.roll(x, BROAD - 1, 1)

        def average(x3, x_left, x_right):
            return 0.25 * (x3[9:17] + x3[7:15] + x_right + x_left)

        hl, hr = left(h), right(h)
        next_h = average(h3, hl, hr) - 0.5 * courant * (
            fu3[9:17] - fu3[7:15] + right(fv) - left(fv)
        )
        next_u = average(u3, left(u), right(u)) - 0.5 * courant * (h3[9:17] - h3[7:15])
        next_v = average(v3, left(v), right(v)) - 0.5 * courant * (hr - hl)
        rows = iota((8, BROAD), 0) + (a * 128 - FIRST + start)
        inside = cols_in & (rows >= 0) & (rows < na * 128)
        for f, value in enumerate((next_h, next_u, next_v)):
            if with_source:
                value = value + source_ref[f, pl.ds(start, 8), :]
            new_ref[f, pl.ds(start, 8), :] = jnp.where(inside, value, 0.0)
        return carry

    lax.fori_loop(1, 19, rows8, 0)


def mask_state(ref):
    (a, c), (na, nc) = my_place(), sizes()
    cols = iota((8, BROAD), 1) + (c * 512 - 128)
    cols_in = (cols >= 0) & (cols < nc * 512)

    def rows8(rb, carry):
        at = pl.ds(pl.multiple_of(rb * 8, 8), 8)
        rows = iota((8, BROAD), 0) + (a * 128 - FIRST + rb * 8)
        inside = cols_in & (rows >= 0) & (rows < na * 128)
        for f in range(3):
            ref[f, at, :] = jnp.where(inside, ref[f, at, :], 0.0)
        return carry

    lax.fori_loop(1, 19, rows8, 0)


def water_kernel(
    source_ref, surface_ref, depth_ref,
    up_ref, down_ref, left_ref, right_ref, c0_ref, c1_ref, c2_ref, c3_ref,
    state_ref,
    even, odd, deep, wide_source,
    o0, o1, o2, o3, o4, o5, o6, o7, i0, i1, i2, i3, i4, i5, i6, i7, send_sem, recv_sem,
):
    outs = [o0, o1, o2, o3, o4, o5, o6, o7]
    ins = [i0, i1, i2, i3, i4, i5, i6, i7]
    write_rims(outs, [0, 0, 0, 0, 0], [
        lambda r, c: source_ref[0, r, c],
        lambda r, c: source_ref[1, r, c],
        lambda r, c: source_ref[2, r, c],
    ])
    greet_around()
    copies = rim_copies(outs, ins, send_sem, recv_sem)
    for copy in copies:
        copy.start()
    rims = [up_ref, down_ref, left_ref, right_ref, c0_ref, c1_ref, c2_ref, c3_ref]
    own_rows, own_lanes = slice(FIRST, FIRST + 128), slice(128, 640)
    for ref in (even, odd, deep):
        for f in range(ref.shape[0]):
            ref[f, 0:8, :] = jnp.zeros((8, BROAD), F32)
            ref[f, TALL - 8 : TALL, :] = jnp.zeros((8, BROAD), F32)
    for f in range(3):
        even[f, own_rows, own_lanes] = surface_ref[f]
        place_rims(even, f, f, rims, [0, 0, 0])
    deep[0, own_rows, own_lanes] = depth_ref[...]
    place_rims(deep, 0, 3, rims, [0, 0, 0])
    mask_state(even)
    for f in range(3):
        wide_source[f, own_rows, own_lanes] = source_ref[f]
    for copy in copies:
        copy.wait()
    for f in range(3):
        place_rims(wide_source, f, f, ins, [0, 0, 0])
    for step in range(SUBSTEPS):
        old, new = (even, odd) if step % 2 == 0 else (odd, even)
        water_step(old, new, deep, wide_source, True)
    for f in range(3):
        state_ref[f] = even[f, own_rows, own_lanes]


def water_call(source, surface, depth, rims):
    heights = [96, 96, 128, 128, 8, 8, 8, 8]
    buffers = [pltpu.VMEM((h, 128), F32) for h in heights]
    return pl.pallas_call(
        water_kernel,
        out_shape=jax.ShapeDtypeStruct((3, 128, 512), F32),
        in_specs=[vmem()] * 11,
        out_specs=vmem(),
        scratch_shapes=[
            pltpu.VMEM((3, TALL, BROAD), F32),
            pltpu.VMEM((3, TALL, BROAD), F32),
            pltpu.VMEM((1, TALL, BROAD), F32),
            pltpu.VMEM((3, TALL, BROAD), F32),
            *buffers,
            *buffers,
            pltpu.SemaphoreType.DMA((8,)),
            pltpu.SemaphoreType.DMA((8,)),
        ],
        compiler_params=pltpu.CompilerParams(
            vmem_limit_bytes=VMEM_LIMIT, collective_id=1, has_side_effects=True
        ),
        name="water",
    )(source, surface, depth, *rims)


def shards(
    offsets, velocity, particle_mass, neighbours, owner_device, target_cell, surface, water_depth
):
    padded, *rims = rims_call(offsets, velocity, particle_mass, surface, water_depth)
    present = jnp.any(
        neighbours[..., :, None] == jnp.arange(9, dtype=jnp.int32), axis=-2
    ).astype(F32)
    dest = owner_device.reshape(64, 128)
    cell = target_cell.reshape(64, 128)
    density, rank, send = particles_call(padded, present.reshape(-1), dest, cell)
    got = exchange_call(send, "send_sources")
    grid_source = deposit_call(got)
    water_state = water_call(grid_source, surface, water_depth, rims)
    back = exchange_call(lookup_call(got, water_state), "send_back")
    feedback = unpack_call(back, dest, rank)
    return (
        water_state,
        density.reshape(particle_mass.shape),
        feedback.reshape((3,) + particle_mass.shape),
    )


def solution(mesh):
    in_specs = (
        P(None, "along", "cross", None),
        P(None, "along", "cross", None),
        P("along", "cross", None),
        P("along", "cross", None),
        P("along", "cross", None, None),
        P("along", "cross", None),
        P(None, "along", "cross"),
        P("along", "cross"),
    )
    out_specs = (
        P(None, "along", "cross"),
        P("along", "cross", None),
        P(None, "along", "cross", None),
    )
    return jax.shard_map(shards, mesh=mesh, in_specs=in_specs, out_specs=out_specs, check_vma=False)
```

```python
import math

import jax
import jax.numpy as jnp
from jax import lax
from jax.experimental import pallas as pl
from jax.experimental.pallas import tpu as pltpu
from jax.sharding import PartitionSpec as P

SUBSTEPS = 4
KAPPA = math.sqrt(math.log2(math.e))
F32 = jnp.float32
BF16 = jnp.bfloat16
NN = (((1,), (0,)), ((), ()))
NT = (((1,), (1,)), ((), ()))
VMEM_LIMIT = 56 * 1024 * 1024

courant = 0.4


def dot(a, b, dims):
    return lax.dot_general(a, b, dims, preferred_element_type=F32)


def split2(x):
    hi = x.astype(BF16).astype(F32)
    return hi, x - hi


def iota(shape, dim):
    return lax.broadcasted_iota(jnp.int32, shape, dim)


def window_sums(pad_ref, present_ref, sums_ref):
    rows, cols = pad_ref.shape[1] - 2, pad_ref.shape[2] - 2

    def tile(t, carry):
        i = t // cols
        j = t - i * cols
        x = pad_ref[0, i + 1, pl.ds(j + 1, 1), :] * KAPPA
        y = pad_ref[1, i + 1, pl.ds(j + 1, 1), :] * KAPPA
        x_col = jnp.broadcast_to(x, (128, 128)).T
        y_col = jnp.broadcast_to(y, (128, 128)).T
        window = []
        for w in range(9):
            bi, bj = i + w // 3, j + w % 3
            bx = (pad_ref[0, bi, pl.ds(bj, 1), :] + (w // 3 - 1.0)) * KAPPA
            by = (pad_ref[1, bi, pl.ds(bj, 1), :] + (w % 3 - 1.0)) * KAPPA
            c0 = pad_ref[4, bi, pl.ds(bj, 1), :] * jnp.exp2(-bx * bx - by * by)
            c0 = c0 * present_ref[t * 9 + w]
            c1 = c0 * pad_ref[2, bi, pl.ds(bj, 1), :]
            c2 = c0 * pad_ref[3, bi, pl.ds(bj, 1), :]
            window.append((2.0 * bx, 2.0 * by, c0, c1, c2))
        acc = [jnp.zeros((128, 128), F32)] * 3
        for bx, by, *carried in window:
            weights = jnp.exp2(x_col * bx + y_col * by)
            acc = [total + weights * c for total, c in zip(acc, carried)]
        scale = jnp.exp2(-x * x - y * y)
        for k in range(3):
            sums_ref[k, pl.ds(t, 1), :] = jnp.sum(acc[k].T, axis=0, keepdims=True) * scale
        return carry

    lax.fori_loop(0, rows * cols, tile, 0, unroll=4)


def pack(dest_ref, vals_ref, rank_ref, send_ref, left_ref, slots_ref, acc_ref):
    groups = dest_ref.shape[0] // 8
    d_iota = iota((128, 128), 0)
    before = jnp.concatenate(
        [
            (iota((128, 128), 0) < iota((128, 128), 1)).astype(F32),
            jnp.ones((128, 128), F32),
        ],
        1,
    ).astype(BF16)
    p_iota = iota((192, 128), 0).astype(F32)
    acc_ref[...] = jnp.zeros_like(acc_ref)

    def group(g, running):
        dest8 = dest_ref[pl.ds(g * 8, 8), :]
        vals8 = [split2(vals_ref[k, pl.ds(g * 8, 8), :]) for k in range(4)]
        ranks = []
        for r in range(8):
            hit = d_iota == jnp.broadcast_to(dest8[r : r + 1], (128, 128))
            counts = dot(jnp.where(hit, 1.0, 0.0).astype(BF16), before, NN)
            rank = jnp.sum(
                jnp.where(hit, counts[:, :128] + running, 0.0), axis=0, keepdims=True
            )
            running = running + counts[:, 128:]
            ranks.append(rank)
            lanes = slice(r * 128, r * 128 + 128)
            slots_ref[:, lanes] = jnp.where(
                p_iota == jnp.broadcast_to(rank, (192, 128)), 1.0, 0.0
            ).astype(BF16)
            for part in range(2):
                for k in range(4):
                    v = jnp.broadcast_to(vals8[k][part][r : r + 1], (128, 128))
                    at = (part * 4 + k) * 128
                    left_ref[at : at + 128, lanes] = jnp.where(hit, v, 0.0).astype(BF16)
        rank_ref[pl.ds(g * 8, 8), :] = jnp.concatenate(ranks, 0)
        acc_ref[:, 0:192] += dot(left_ref[...], slots_ref[...], NT)
        return running

    lax.fori_loop(0, groups, group, jnp.zeros((128, 128), F32))
    tails = []
    for k in range(4):
        send_ref[pl.ds(k, 128, stride=8), :] = acc_ref[k * 128 : k * 128 + 128, 0:128] + acc_ref[
            512 + k * 128 : 640 + k * 128, 0:128
        ]
        tails.append(
            acc_ref[k * 128 : k * 128 + 128, 128:256]
            + acc_ref[512 + k * 128 : 640 + k * 128, 128:256]
        )
    low_half = iota((128, 128), 1) < 64
    for k in range(6, 8):
        send_ref[pl.ds(k, 128, stride=8), :] = jnp.zeros((128, 128), F32)
    for h in range(2):
        send_ref[pl.ds(4 + h, 128, stride=8), :] = jnp.where(
            low_half, tails[2 * h], pltpu.roll(tails[2 * h + 1], 64, 1)
        )


def vmem():
    return pl.BlockSpec(memory_space=pltpu.VMEM)


MESH = pl.DeviceIdType.MESH
AROUND = [(-1, 0), (1, 0), (0, -1), (0, 1), (-1, -1), (-1, 1), (1, -1), (1, 1)]


def my_place():
    return lax.axis_index("along"), lax.axis_index("cross")


def sizes():
    return lax.axis_size("along"), lax.axis_size("cross")


def at_step(step):
    (a, c), (na, nc) = my_place(), sizes()
    return lax.rem(a + step[0] + na, na), lax.rem(c + step[1] + nc, nc)


def greet_around():
    barrier = pltpu.get_barrier_semaphore()
    for step in AROUND:
        pl.semaphore_signal(barrier, inc=1, device_id=at_step(step), device_id_type=MESH)
    pl.semaphore_wait(barrier, len(AROUND))


def rim_copies(out_refs, in_refs, send_sem, recv_sem):
    copies = []
    for n, step in enumerate(AROUND):
        opposite = AROUND.index((-step[0], -step[1]))
        copies.append(
            pltpu.make_async_remote_copy(
                src_ref=out_refs[n],
                dst_ref=in_refs[opposite],
                send_sem=send_sem.at[n],
                recv_sem=recv_sem.at[opposite],
                device_id=at_step(step),
                device_id_type=MESH,
            )
        )
    return copies


DEEP = 4
SIDE_PARTICLES = 24


def column_strip(fields, right):
    lanes = iota((fields[0].shape[0], 128), 1)
    out = jnp.zeros((fields[0].shape[0], 128), F32)
    for f, field in enumerate(fields):
        turn = DEEP * f + (DEEP if right else 0)
        moved = pltpu.roll(field, turn, 1) if turn else field
        out = jnp.where((lanes >= DEEP * f) & (lanes < DEEP * f + DEEP), moved, out)
    return out


def write_rims(out_refs, base, fields):
    top, bottom = slice(0, 8), slice(120, 128)
    for n, rows in ((0, top), (1, bottom)):
        for f, field in enumerate(fields):
            for b in range(4):
                at = base[n] + (f * 4 + b) * 8
                out_refs[n][at : at + 8, :] = field(rows, slice(b * 128, b * 128 + 128))
    for right in range(2):
        lanes = slice(384, 512) if right else slice(0, 128)
        strip = column_strip([field(slice(0, 128), lanes) for field in fields], right == 1)
        at = base[2 + right]
        out_refs[2 + right][at : at + 128, :] = strip
        out_refs[4 + right][base[4] : base[4] + 8, :] = strip[0:8]
        out_refs[6 + right][base[4] : base[4] + 8, :] = strip[120:128]


def rims_kernel(
    off_ref, vel_ref, mass_ref, surface_ref, depth_ref,
    pad_ref, up_ref, down_ref, left_ref, right_ref, c0_ref, c1_ref, c2_ref, c3_ref,
    o0, o1, o2, o3, o4, o5, o6, o7, i0, i1, i2, i3, i4, i5, i6, i7, send_sem, recv_sem,
):
    outs = [o0, o1, o2, o3, o4, o5, o6, o7]
    ins = [i0, i1, i2, i3, i4, i5, i6, i7]
    rows, cols = mass_ref.shape[0], mass_ref.shape[1]
    particle = [
        (off_ref, 0), (off_ref, 1), (vel_ref, 0), (vel_ref, 1), (mass_ref, None),
    ]

    def tiles(f, i, j):
        ref, part = particle[f]
        return ref[i, j, :] if part is None else ref[part, i, j, :]

    everything = slice(0, cols)
    for f in range(5):
        outs[0][f * cols : (f + 1) * cols, :] = tiles(f, 0, everything)
        outs[1][f * cols : (f + 1) * cols, :] = tiles(f, rows - 1, everything)
        for side, j in ((0, slice(0, 1)), (1, slice(cols - 1, cols))):
            for i in range(rows):
                outs[2 + side][f * rows + i : f * rows + i + 1, :] = tiles(f, i, j)
            outs[4 + side][f : f + 1, :] = tiles(f, 0, j)
            outs[6 + side][f : f + 1, :] = tiles(f, rows - 1, j)
    for side in range(2):
        outs[2 + side][5 * rows :SIDE_PARTICLES, :] = jnp.zeros((SIDE_PARTICLES - 5 * rows, 128), F32)
        outs[4 + side][5:8, :] = jnp.zeros((3, 128), F32)
        outs[6 + side][5:8, :] = jnp.zeros((3, 128), F32)
    fields = [
        lambda r, c: surface_ref[0, r, c],
        lambda r, c: surface_ref[1, r, c],
        lambda r, c: surface_ref[2, r, c],
        lambda r, c: depth_ref[r, c],
    ]
    write_rims(outs, [5 * cols, 5 * cols, SIDE_PARTICLES, SIDE_PARTICLES, 8], fields)
    greet_around()
    copies = rim_copies(outs, ins, send_sem, recv_sem)
    for copy in copies:
        copy.start()
    for f in range(5):
        for i in range(rows):
            pad_ref[f, i + 1, 1 : cols + 1, :] = tiles(f, i, everything)
    for copy in copies:
        copy.wait()
    (a, c), (na, nc) = my_place(), sizes()
    inside = [a > 0, a < na - 1, c > 0, c < nc - 1]

    def kept(f, value, *tests):
        if f < 4:
            return value
        for test in tests:
            value = jnp.where(test, value, 0.0)
        return value

    for f in range(5):
        pad_ref[f, 0, 1 : cols + 1, :] = kept(f, ins[0][f * cols : (f + 1) * cols, :], inside[0])
        pad_ref[f, rows + 1, 1 : cols + 1, :] = kept(f, ins[1][f * cols : (f + 1) * cols, :], inside[1])
        for side, j in ((0, 0), (1, cols + 1)):
            for i in range(rows):
                pad_ref[f, i + 1, j : j + 1, :] = kept(
                    f, ins[2 + side][f * rows + i : f * rows + i + 1, :], inside[2 + side]
                )
            pad_ref[f, 0, j : j + 1, :] = kept(f, ins[4 + side][f : f + 1, :], inside[0], inside[2 + side])
            pad_ref[f, rows + 1, j : j + 1, :] = kept(f, ins[6 + side][f : f + 1, :], inside[1], inside[2 + side])
    up_ref[...] = ins[0][5 * cols : 5 * cols + 128, :]
    down_ref[...] = ins[1][5 * cols : 5 * cols + 128, :]
    left_ref[...] = ins[2][SIDE_PARTICLES : SIDE_PARTICLES + 128, :]
    right_ref[...] = ins[3][SIDE_PARTICLES : SIDE_PARTICLES + 128, :]
    for n, ref in enumerate((c0_ref, c1_ref, c2_ref, c3_ref)):
        ref[...] = ins[4 + n][8:16, :]


def rims_call(offsets, velocity, mass, surface, depth):
    rows, cols = mass.shape[0], mass.shape[1]
    tall, wide, corner = 5 * cols + 128, SIDE_PARTICLES + 128, 16
    heights = [tall, tall, wide, wide, corner, corner, corner, corner]
    buffers = [pltpu.VMEM((h, 128), F32) for h in heights]
    return pl.pallas_call(
        rims_kernel,
        out_shape=(
            jax.ShapeDtypeStruct((5, rows + 2, cols + 2, 128), F32),
            *[jax.ShapeDtypeStruct((128, 128), F32)] * 4,
            *[jax.ShapeDtypeStruct((8, 128), F32)] * 4,
        ),
        in_specs=[vmem()] * 5,
        out_specs=tuple([vmem()] * 9),
        scratch_shapes=[
            *buffers,
            *buffers,
            pltpu.SemaphoreType.DMA((8,)),
            pltpu.SemaphoreType.DMA((8,)),
        ],
        compiler_params=pltpu.CompilerParams(
            vmem_limit_bytes=VMEM_LIMIT, collective_id=0, has_side_effects=True
        ),
        name="rims",
    )(offsets, velocity, mass, surface, depth)


def unpack(back_ref, dest_ref, rank_ref, out_ref, table_ref):
    tail = back_ref[pl.ds(3, 128, stride=8), :]
    tails = [tail, pltpu.roll(tail, 64, 1), back_ref[pl.ds(4, 128, stride=8), :]]
    for k in range(3):
        for part, piece in enumerate(split2(back_ref[pl.ds(k, 128, stride=8), :])):
            table_ref[k * 128 : k * 128 + 128, part * 192 : part * 192 + 128] = piece.astype(BF16)
        for part, piece in enumerate(split2(tails[k])):
            table_ref[
                k * 128 : k * 128 + 128, part * 192 + 128 : part * 192 + 192
            ] = piece[:, 0:64].astype(BF16)
    d_iota = iota((128, 128), 0)
    p_iota = iota((192, 128), 0).astype(F32)

    def step(g, carry):
        at = pl.ds(g * 8, 8)
        dest8 = dest_ref[at, :]
        rank8 = rank_ref[at, :]
        found = [[], [], []]
        for pair in range(4):
            slots = jnp.concatenate(
                [
                    jnp.where(
                        p_iota == jnp.broadcast_to(rank8[r : r + 1], (192, 128)), 1.0, 0.0
                    ).astype(BF16)
                    for r in (2 * pair, 2 * pair + 1)
                ],
                1,
            )
            got = dot(table_ref[...], jnp.concatenate([slots, slots], 0), NN)
            for k in range(3):
                for h in range(2):
                    r = 2 * pair + h
                    hit = d_iota == jnp.broadcast_to(dest8[r : r + 1], (128, 128))
                    part = got[k * 128 : k * 128 + 128, h * 128 : h * 128 + 128]
                    found[k].append(jnp.sum(jnp.where(hit, part, 0.0), axis=0, keepdims=True))
        for k in range(3):
            out_ref[k, at, :] = jnp.concatenate(found[k], 0)
        return carry

    lax.fori_loop(0, dest_ref.shape[0] // 8, step, 0)


GROUPS = 4
PER_GROUP = 32
STEP = 8


def row_and_column(cell):
    row = jnp.floor(cell * (1.0 / 512.0))
    return row, cell - row * 512.0


def unfold(got_ref, slots_ref, group):
    low_half = iota((16, 128), 1) < 64
    first_row = group * PER_GROUP * 8
    for k in range(4):
        slots_ref[k, 0:32, :] = got_ref[pl.ds(first_row + k, 32, stride=8), :]
        row = got_ref[pl.ds(first_row + 4 + k // 2, 32, stride=8), :]
        first, second = row[0:16], row[16:32]
        if k % 2 == 0:
            full = jnp.where(low_half, first, pltpu.roll(second, 64, 1))
        else:
            full = jnp.where(low_half, pltpu.roll(first, 64, 1), second)
        slots_ref[k, 32:48, :] = full


def deposit_group(group, slots_ref, cells_ref, left_ref, right_ref, acc_ref):
    r_iota = iota((128, 128), 0).astype(F32)
    c_iota = iota((512, 128), 0).astype(F32)
    cells_ref[pl.ds(pl.multiple_of(group * 48, 8), 48), :] = slots_ref[0]

    def step(g, carry):
        at = pl.ds(pl.multiple_of(g * STEP, STEP), STEP)
        row8, col8 = row_and_column(slots_ref[0, at, :])
        vals8 = [split2(slots_ref[1 + k, at, :]) for k in range(3)]
        for r in range(STEP):
            lanes = slice(r * 128, r * 128 + 128)
            hit = r_iota == jnp.broadcast_to(row8[r : r + 1], (128, 128))
            for part in range(2):
                for k in range(3):
                    v = jnp.broadcast_to(vals8[k][part][r : r + 1], (128, 128))
                    base = (part * 3 + k) * 128
                    left_ref[base : base + 128, lanes] = jnp.where(hit, v, 0.0).astype(BF16)
            right_ref[:, lanes] = jnp.where(
                c_iota == jnp.broadcast_to(col8[r : r + 1], (512, 128)), 1.0, 0.0
            ).astype(BF16)
        acc_ref[...] += dot(left_ref[...], right_ref[...], NT)
        return carry

    lax.fori_loop(0, 48 // STEP, step, 0)


def lookup_group(group, cells_ref, table_ref, found_ref, back_ref):
    r_iota = iota((128, 128), 0).astype(F32)
    c_iota = iota((512, 128), 0).astype(F32)

    def step(g, carry):
        at = pl.ds(pl.multiple_of(group * 48 + g * 8, 8), 8)
        row8, col8 = row_and_column(cells_ref[at, :])
        found = [[], [], []]
        for pair in range(4):
            right = jnp.concatenate(
                [
                    jnp.where(
                        c_iota == jnp.broadcast_to(col8[r : r + 1], (512, 128)), 1.0, 0.0
                    ).astype(BF16)
                    for r in (2 * pair, 2 * pair + 1)
                ],
                1,
            )
            got = dot(table_ref[...], jnp.concatenate([right, right], 0), NN)
            for k in range(3):
                for h in range(2):
                    r = 2 * pair + h
                    hit = r_iota == jnp.broadcast_to(row8[r : r + 1], (128, 128))
                    part = got[k * 128 : k * 128 + 128, h * 128 : h * 128 + 128]
                    found[k].append(jnp.sum(jnp.where(hit, part, 0.0), axis=0, keepdims=True))
        for k in range(3):
            found_ref[k, pl.ds(pl.multiple_of(g * 8, 8), 8), :] = jnp.concatenate(found[k], 0)
        return carry

    lax.fori_loop(0, 6, step, 0)
    low_half = iota((16, 128), 1) < 64
    first_row = group * PER_GROUP * 8
    tails = [found_ref[k, 32:48, :] for k in range(3)]
    turned = [pltpu.roll(t, 64, 1) for t in tails]
    for k in range(3):
        back_ref[pl.ds(first_row + k, 32, stride=8), :] = found_ref[k, 0:32, :]
    back_ref[pl.ds(first_row + 3, 16, stride=8), :] = jnp.where(low_half, tails[0], turned[1])
    back_ref[pl.ds(first_row + 131, 16, stride=8), :] = jnp.where(low_half, turned[0], tails[1])
    back_ref[pl.ds(first_row + 4, 16, stride=8), :] = tails[2]
    back_ref[pl.ds(first_row + 132, 16, stride=8), :] = turned[2]
    for k in range(5, 8):
        back_ref[pl.ds(first_row + k, 32, stride=8), :] = jnp.zeros((32, 128), F32)


TALL = 136
BROAD = 640


def place_rims(wide_ref, index, f, refs, bases):
    up, down, left, right, *corners = refs
    upper_half = iota((8, 128), 0) < 4
    for b in range(4):
        at = bases[0] + (f * 4 + b) * 8
        wide_ref[index, 128:136, b * 128 : b * 128 + 128] = jnp.where(
            upper_half, down[at : at + 8, :], up[at : at + 8, :]
        )
    to_left = (128 - DEEP - DEEP * f) % 128
    to_right = (128 - DEEP * f) % 128

    def strip(left_part, right_part):
        moved_left = pltpu.roll(left_part, to_left, 1) if to_left else left_part
        moved_right = pltpu.roll(right_part, to_right, 1) if to_right else right_part
        return jnp.where(iota(left_part.shape, 1) < 64, moved_right, moved_left)

    sides = slice(bases[1], bases[1] + 128)
    wide_ref[index, 0:128, 512:640] = strip(left[sides, :], right[sides, :])
    rows = slice(bases[2], bases[2] + 8)
    c = [
        jnp.where(upper_half, corners[2 + side][rows, :], corners[side][rows, :])
        for side in range(2)
    ]
    wide_ref[index, 128:136, 512:640] = strip(c[0], c[1])


def inside_grid(block):
    (a, c), (na, nc) = my_place(), sizes()
    cols = iota((8, BROAD), 1)
    cols = jnp.where(cols < 576, cols, cols - BROAD) + c * 512
    rows = iota((8, BROAD), 0) + block * 8
    rows = jnp.where(rows < 132, rows, rows - TALL) + a * 128
    return (cols >= 0) & (cols < nc * 512) & (rows >= 0) & (rows < na * 128)


def water_step(old_ref, new_ref, depth_ref, source_ref):
    blocks = TALL // 8
    sub = iota((8, BROAD), 0)

    def load(block):
        at = slice(block * 8, block * 8 + 8)
        h, u, v = [old_ref[f, at, :] for f in range(3)]
        fu = depth_ref[0, at, :] * u
        fields = (h, u, v, fu)
        return fields, [pltpu.roll(x, 1, 0) for x in fields], [pltpu.roll(x, 7, 0) for x in fields]

    def left(x):
        return pltpu.roll(x, 1, 1)

    def right(x):
        return pltpu.roll(x, BROAD - 1, 1)

    before, here = load(blocks - 1), load(0)
    for block in range(blocks):
        after = load((block + 1) % blocks)
        at = slice(block * 8, block * 8 + 8)
        (h, u, v, _), down, up = here
        h_w, u_w, v_w, fu_w = [jnp.where(sub == 0, p, q) for p, q in zip(before[1], down)]
        h_e, u_e, v_e, fu_e = [jnp.where(sub == 7, p, q) for p, q in zip(after[2], up)]
        fv = depth_ref[0, at, :] * v
        h_s, h_n = left(h), right(h)
        next_h = 0.25 * (h_e + h_w + h_n + h_s) - 0.5 * courant * (
            fu_e - fu_w + right(fv) - left(fv)
        )
        next_u = 0.25 * (u_e + u_w + right(u) + left(u)) - 0.5 * courant * (h_e - h_w)
        next_v = 0.25 * (v_e + v_w + right(v) + left(v)) - 0.5 * courant * (h_n - h_s)
        inside = inside_grid(block)
        for f, value in enumerate((next_h, next_u, next_v)):
            new_ref[f, at, :] = jnp.where(inside, value + source_ref[f, at, :], 0.0)
        before, here = here, after


def main_kernel(
    pad_ref, present_ref, dest_ref, cell_ref, surface_ref, depth_ref,
    up_ref, down_ref, left_in, right_in, c0_ref, c1_ref, c2_ref, c3_ref,
    dens_ref, state_ref, feed_ref,
    sums_ref, vals_ref, pleft_ref, pslots_ref, pacc_ref, rank_ref, send_ref, got_ref,
    slots_ref, cells_ref, left_ref, right_ref, acc_ref,
    even, odd, deep, wide_source,
    table_ref, found_ref, back_ref, back_got, utable_ref,
    o0, o1, o2, o3, o4, o5, o6, o7, i0, i1, i2, i3, i4, i5, i6, i7,
    rim_send, rim_recv, out_sem, in_sem, back_out_sem, back_in_sem,
):
    (a, c), (na, nc) = my_place(), sizes()
    count = na * nc
    me = a * nc + c

    def device(n):
        return (lax.div(n, nc), lax.rem(n, nc))

    def block(n):
        return pl.ds(pl.multiple_of(n * 8, 8), 8)

    barrier = pltpu.get_barrier_semaphore()

    def greet(step, carry):
        pl.semaphore_signal(
            barrier, inc=1, device_id=device(lax.rem(me + step, count)), device_id_type=MESH
        )
        return carry

    lax.fori_loop(1, count, greet, 0)

    window_sums(pad_ref, present_ref, sums_ref)
    rows, cols = pad_ref.shape[1] - 2, pad_ref.shape[2] - 2
    for i in range(rows):
        at = slice(i * cols, (i + 1) * cols)
        s0 = sums_ref[0, at, :]
        density = s0 / 128.0
        dens_ref[at, :] = density
        volume = pad_ref[4, i + 1, 1 : cols + 1, :] / density
        vals_ref[0, at, :] = cell_ref[at, :].astype(F32)
        vals_ref[1, at, :] = volume
        vals_ref[2, at, :] = volume * (sums_ref[1, at, :] / s0)
        vals_ref[3, at, :] = volume * (sums_ref[2, at, :] / s0)
    pack(dest_ref, vals_ref, rank_ref, send_ref, pleft_ref, pslots_ref, pacc_ref)

    pl.semaphore_wait(barrier, count - 1)

    def send_out(group):
        def start(step, carry):
            to = lax.rem(me + step, count)
            pltpu.make_async_remote_copy(
                src_ref=send_ref.at[block(to), :],
                dst_ref=got_ref.at[block(step), :],
                send_sem=out_sem,
                recv_sem=in_sem.at[group],
                device_id=device(to),
                device_id_type=MESH,
            ).start()
            return carry

        lax.fori_loop(max(1, group * PER_GROUP), (group + 1) * PER_GROUP, start, 0)

    for group in range(GROUPS):
        send_out(group)
    got_ref[0:8, :] = send_ref[block(me), :]

    rims = [up_ref, down_ref, left_in, right_in, c0_ref, c1_ref, c2_ref, c3_ref]
    for f in range(3):
        even[f, 0:128, 0:512] = surface_ref[f]
        place_rims(even, f, f, rims, [0, 0, 0])
    deep[0, 0:128, 0:512] = depth_ref[...]
    place_rims(deep, 0, 3, rims, [0, 0, 0])
    for b in range(TALL // 8):
        at = slice(b * 8, b * 8 + 8)
        for f in range(3):
            even[f, at, :] = jnp.where(inside_grid(b), even[f, at, :], 0.0)

    acc_ref[...] = jnp.zeros_like(acc_ref)
    for group in range(GROUPS):
        landed = got_ref.at[max(8, group * PER_GROUP * 8) : (group + 1) * PER_GROUP * 8, :]
        pltpu.make_async_copy(landed, landed, in_sem.at[group]).wait()
        unfold(got_ref, slots_ref, group)
        deposit_group(group, slots_ref, cells_ref, left_ref, right_ref, acc_ref)
    for k in range(3):
        wide_source[k, 0:128, 0:512] = (
            acc_ref[k * 128 : k * 128 + 128, :] + acc_ref[384 + k * 128 : 512 + k * 128, :]
        )

    outs = [o0, o1, o2, o3, o4, o5, o6, o7]
    ins = [i0, i1, i2, i3, i4, i5, i6, i7]
    write_rims(outs, [0, 0, 0, 0, 0], [
        lambda r, c: wide_source[0, r, c],
        lambda r, c: wide_source[1, r, c],
        lambda r, c: wide_source[2, r, c],
    ])
    copies = rim_copies(outs, ins, rim_send, rim_recv)
    for copy in copies:
        copy.start()
    for copy in copies:
        copy.wait()
    for f in range(3):
        place_rims(wide_source, f, f, ins, [0, 0, 0])

    def two_steps(n, carry):
        water_step(even, odd, deep, wide_source)
        water_step(odd, even, deep, wide_source)
        return carry

    lax.fori_loop(0, SUBSTEPS // 2, two_steps, 0)
    for k in range(3):
        value = even[k, 0:128, 0:512]
        state_ref[k] = value
        hi, lo = split2(value)
        table_ref[k * 128 : k * 128 + 128, 0:512] = hi.astype(BF16)
        table_ref[k * 128 : k * 128 + 128, 512:1024] = lo.astype(BF16)

    for group in range(GROUPS):
        lookup_group(group, cells_ref, table_ref, found_ref, back_ref)

        def start(step, carry):
            pltpu.make_async_remote_copy(
                src_ref=back_ref.at[block(step), :],
                dst_ref=back_got.at[block(me), :],
                send_sem=back_out_sem,
                recv_sem=back_in_sem,
                device_id=device(lax.rem(me - step + count, count)),
                device_id_type=MESH,
            ).start()
            return carry

        lax.fori_loop(max(1, group * PER_GROUP), (group + 1) * PER_GROUP, start, 0)
    back_got[block(me), :] = back_ref[0:8, :]
    others = (count - 1) * 8
    for ref, sem in (
        (back_got, back_in_sem),
        (send_ref, out_sem),
        (back_ref, back_out_sem),
    ):
        pltpu.make_async_copy(ref.at[0:others, :], ref.at[0:others, :], sem).wait()
    unpack(back_got, dest_ref, rank_ref, feed_ref, utable_ref)


def main_call(pad, present, dest, cell, surface, depth, rims):
    heights = [96, 96, 128, 128, 8, 8, 8, 8]
    buffers = [pltpu.VMEM((h, 128), F32) for h in heights]
    dma = pltpu.SemaphoreType.DMA
    return pl.pallas_call(
        main_kernel,
        out_shape=(
            jax.ShapeDtypeStruct((64, 128), F32),
            jax.ShapeDtypeStruct((3, 128, 512), F32),
            jax.ShapeDtypeStruct((3, 64, 128), F32),
        ),
        in_specs=[vmem(), pl.BlockSpec(memory_space=pltpu.SMEM)] + [vmem()] * 12,
        out_specs=(vmem(), vmem(), vmem()),
        scratch_shapes=[
            pltpu.VMEM((3, 64, 128), F32),
            pltpu.VMEM((4, 64, 128), F32),
            pltpu.VMEM((1024, 1024), BF16),
            pltpu.VMEM((192, 1024), BF16),
            pltpu.VMEM((1024, 256), F32),
            pltpu.VMEM((64, 128), F32),
            pltpu.VMEM((1024, 128), F32),
            pltpu.VMEM((1024, 128), F32),
            pltpu.VMEM((4, 48, 128), F32),
            pltpu.VMEM((192, 128), F32),
            pltpu.VMEM((768, STEP * 128), BF16),
            pltpu.VMEM((512, STEP * 128), BF16),
            pltpu.VMEM((768, 512), F32),
            pltpu.VMEM((3, TALL, BROAD), F32),
            pltpu.VMEM((3, TALL, BROAD), F32),
            pltpu.VMEM((1, TALL, BROAD), F32),
            pltpu.VMEM((3, TALL, BROAD), F32),
            pltpu.VMEM((384, 1024), BF16),
            pltpu.VMEM((3, 48, 128), F32),
            pltpu.VMEM((1024, 128), F32),
            pltpu.VMEM((1024, 128), F32),
            pltpu.VMEM((384, 384), BF16),
            *buffers,
            *buffers,
            dma((8,)),
            dma((8,)),
            dma,
            dma((GROUPS,)),
            dma,
            dma,
        ],
        compiler_params=pltpu.CompilerParams(
            vmem_limit_bytes=VMEM_LIMIT, collective_id=1, has_side_effects=True
        ),
        name="main",
    )(pad, present, dest, cell, surface, depth, *rims)


def shards(
    offsets, velocity, particle_mass, neighbours, owner_device, target_cell, surface, water_depth
):
    padded, *rims = rims_call(offsets, velocity, particle_mass, surface, water_depth)
    present = jnp.any(
        neighbours[..., :, None] == jnp.arange(9, dtype=jnp.int32), axis=-2
    ).astype(F32)
    density, water_state, feedback = main_call(
        padded,
        present.reshape(-1),
        owner_device.reshape(64, 128),
        target_cell.reshape(64, 128),
        surface,
        water_depth,
        rims,
    )
    return (
        water_state,
        density.reshape(particle_mass.shape),
        feedback.reshape((3,) + particle_mass.shape),
    )


def solution(mesh):
    in_specs = (
        P(None, "along", "cross", None),
        P(None, "along", "cross", None),
        P("along", "cross", None),
        P("along", "cross", None),
        P("along", "cross", None, None),
        P("along", "cross", None),
        P(None, "along", "cross"),
        P("along", "cross"),
    )
    out_specs = (
        P(None, "along", "cross"),
        P("along", "cross", None),
        P(None, "along", "cross", None),
    )
    return jax.shard_map(shards, mesh=mesh, in_specs=in_specs, out_specs=out_specs, check_vma=False)
```

```python
import math

import jax
import jax.numpy as jnp
from jax import lax
from jax.experimental import pallas as pl
from jax.experimental.pallas import tpu as pltpu
from jax.sharding import PartitionSpec as P

SUBSTEPS = 4
KAPPA = math.sqrt(math.log2(math.e))
F32 = jnp.float32
BF16 = jnp.bfloat16
F8 = jnp.float8_e4m3fn
NN = (((1,), (0,)), ((), ()))
NT = (((1,), (1,)), ((), ()))
VMEM_LIMIT = 56 * 1024 * 1024

courant = 0.4


def dot(a, b, dims):
    return lax.dot_general(a, b, dims, preferred_element_type=F32)


def split2(x):
    hi = x.astype(BF16).astype(F32)
    return hi, x - hi


def split8(x):
    t0 = x.astype(F8).astype(F32)
    r = (x - t0) * 16.0
    t1 = r.astype(F8).astype(F32)
    return t0, t1, (r - t1) * 16.0


def iota(shape, dim):
    return lax.broadcasted_iota(jnp.int32, shape, dim)


def window_sums(pad_ref, near_ref, dest_ref, sums_ref, rank_ref):
    rows, cols = pad_ref.shape[1] - 2, pad_ref.shape[2] - 2
    d_iota = iota((128, 128), 0)
    before = jnp.concatenate(
        [
            (iota((128, 128), 0) < iota((128, 128), 1)).astype(F32),
            jnp.ones((128, 128), F32),
        ],
        1,
    ).astype(BF16)

    def tile(t, running):
        hit = d_iota == jnp.broadcast_to(dest_ref[pl.ds(t, 1), :], (128, 128))
        counts = dot(jnp.where(hit, 1.0, 0.0).astype(BF16), before, NN)
        rank_ref[pl.ds(t, 1), :] = jnp.sum(
            jnp.where(hit, counts[:, :128] + running, 0.0), axis=0, keepdims=True
        )
        running = running + counts[:, 128:]
        i = t // cols
        j = t - i * cols
        x = pad_ref[0, i + 1, pl.ds(j + 1, 1), :] * KAPPA
        y = pad_ref[1, i + 1, pl.ds(j + 1, 1), :] * KAPPA
        x_col = jnp.broadcast_to(x, (128, 128)).T
        y_col = jnp.broadcast_to(y, (128, 128)).T
        listed = jnp.int32(0)
        for slot in range(9):
            listed = listed | lax.shift_left(jnp.int32(1), near_ref[slot, i, j] + 1)
        window = []
        for w in range(9):
            bi, bj = i + w // 3, j + w % 3
            bx = (pad_ref[0, bi, pl.ds(bj, 1), :] + (w // 3 - 1.0)) * KAPPA
            by = (pad_ref[1, bi, pl.ds(bj, 1), :] + (w % 3 - 1.0)) * KAPPA
            c0 = pad_ref[4, bi, pl.ds(bj, 1), :] * jnp.exp2(-bx * bx - by * by)
            c0 = c0 * (lax.shift_right_logical(listed, w + 1) & 1).astype(F32)
            c1 = c0 * pad_ref[2, bi, pl.ds(bj, 1), :]
            c2 = c0 * pad_ref[3, bi, pl.ds(bj, 1), :]
            window.append((2.0 * bx, 2.0 * by, c0, c1, c2))
        acc = [jnp.zeros((128, 128), F32)] * 3
        for bx, by, *carried in window:
            weights = jnp.exp2(x_col * bx + y_col * by)
            acc = [total + weights * c for total, c in zip(acc, carried)]
        scale = jnp.exp2(-x * x - y * y)
        for k in range(3):
            sums_ref[k, pl.ds(t, 1), :] = jnp.sum(acc[k].T, axis=0, keepdims=True) * scale
        return running

    lax.fori_loop(0, rows * cols, tile, jnp.zeros((128, 128), F32), unroll=4)


def pack(dest_ref, vals_ref, rank_ref, send_ref, left_ref, slots_ref, acc_ref):
    groups = dest_ref.shape[0] // 8
    d_iota = iota((128, 128), 0)
    p_iota = iota((192, 128), 0).astype(F32)
    acc_ref[...] = jnp.zeros_like(acc_ref)

    def group(g, carry):
        at = pl.ds(pl.multiple_of(g * 8, 8), 8)
        dest8 = dest_ref[at, :]
        rank8 = rank_ref[at, :]
        vals8 = [split2(vals_ref[k, at, :]) for k in range(4)]
        for r in range(8):
            hit = d_iota == jnp.broadcast_to(dest8[r : r + 1], (128, 128))
            lanes = slice(r * 128, r * 128 + 128)
            slots_ref[:, lanes] = jnp.where(
                p_iota == jnp.broadcast_to(rank8[r : r + 1], (192, 128)), 1.0, 0.0
            ).astype(BF16)
            for part in range(2):
                for k in range(4):
                    v = jnp.broadcast_to(vals8[k][part][r : r + 1], (128, 128))
                    base = (part * 4 + k) * 128
                    left_ref[base : base + 128, lanes] = jnp.where(hit, v, 0.0).astype(BF16)
        acc_ref[:, 0:192] += dot(left_ref[...], slots_ref[...], NT)
        return carry

    lax.fori_loop(0, groups, group, 0)
    tails = []
    for k in range(4):
        send_ref[pl.ds(k, 128, stride=8), :] = acc_ref[k * 128 : k * 128 + 128, 0:128] + acc_ref[
            512 + k * 128 : 640 + k * 128, 0:128
        ]
        tails.append(
            acc_ref[k * 128 : k * 128 + 128, 128:256]
            + acc_ref[512 + k * 128 : 640 + k * 128, 128:256]
        )
    low_half = iota((128, 128), 1) < 64
    for k in range(6, 8):
        send_ref[pl.ds(k, 128, stride=8), :] = jnp.zeros((128, 128), F32)
    for h in range(2):
        send_ref[pl.ds(4 + h, 128, stride=8), :] = jnp.where(
            low_half, tails[2 * h], pltpu.roll(tails[2 * h + 1], 64, 1)
        )


def vmem():
    return pl.BlockSpec(memory_space=pltpu.VMEM)


MESH = pl.DeviceIdType.MESH
AROUND = [(-1, 0), (1, 0), (0, -1), (0, 1), (-1, -1), (-1, 1), (1, -1), (1, 1)]


def my_place():
    return lax.axis_index("along"), lax.axis_index("cross")


def sizes():
    return lax.axis_size("along"), lax.axis_size("cross")


def at_step(step):
    (a, c), (na, nc) = my_place(), sizes()
    return lax.rem(a + step[0] + na, na), lax.rem(c + step[1] + nc, nc)


def rim_copies(out_refs, in_refs, send_sem, recv_sem):
    copies = []
    for n, step in enumerate(AROUND):
        opposite = AROUND.index((-step[0], -step[1]))
        copies.append(
            pltpu.make_async_remote_copy(
                src_ref=out_refs[n],
                dst_ref=in_refs[opposite],
                send_sem=send_sem.at[n],
                recv_sem=recv_sem.at[opposite],
                device_id=at_step(step),
                device_id_type=MESH,
            )
        )
    return copies


DEEP = 4
SIDE_PARTICLES = 24


def column_strip(fields, right):
    lanes = iota((fields[0].shape[0], 128), 1)
    out = jnp.zeros((fields[0].shape[0], 128), F32)
    for f, field in enumerate(fields):
        turn = DEEP * f + (DEEP if right else 0)
        moved = pltpu.roll(field, turn, 1) if turn else field
        out = jnp.where((lanes >= DEEP * f) & (lanes < DEEP * f + DEEP), moved, out)
    return out


def write_rims(out_refs, base, fields):
    top, bottom = slice(0, 8), slice(120, 128)
    for n, rows in ((0, top), (1, bottom)):
        for f, field in enumerate(fields):
            for b in range(4):
                at = base[n] + (f * 4 + b) * 8
                out_refs[n][at : at + 8, :] = field(rows, slice(b * 128, b * 128 + 128))
    for right in range(2):
        lanes = slice(384, 512) if right else slice(0, 128)
        strip = column_strip([field(slice(0, 128), lanes) for field in fields], right == 1)
        at = base[2 + right]
        out_refs[2 + right][at : at + 128, :] = strip
        out_refs[4 + right][base[4] : base[4] + 8, :] = strip[0:8]
        out_refs[6 + right][base[4] : base[4] + 8, :] = strip[120:128]


def rims_kernel(
    off_ref, vel_ref, mass_ref, pad_ref,
    o0, o1, o2, o3, o4, o5, o6, o7, i0, i1, i2, i3, i4, i5, i6, i7, send_sem, recv_sem,
):
    outs = [o0, o1, o2, o3, o4, o5, o6, o7]
    ins = [i0, i1, i2, i3, i4, i5, i6, i7]
    rows, cols = mass_ref.shape[0], mass_ref.shape[1]
    barrier = pltpu.get_barrier_semaphore()
    for step in AROUND:
        pl.semaphore_signal(barrier, inc=1, device_id=at_step(step), device_id_type=MESH)
    particle = [
        (off_ref, 0), (off_ref, 1), (vel_ref, 0), (vel_ref, 1), (mass_ref, None),
    ]

    def tiles(f, i, j):
        ref, part = particle[f]
        return ref[i, j, :] if part is None else ref[part, i, j, :]

    everything = slice(0, cols)
    for f in range(5):
        outs[0][f * cols : (f + 1) * cols, :] = tiles(f, 0, everything)
        outs[1][f * cols : (f + 1) * cols, :] = tiles(f, rows - 1, everything)
        for side, j in ((0, slice(0, 1)), (1, slice(cols - 1, cols))):
            for i in range(rows):
                outs[2 + side][f * rows + i : f * rows + i + 1, :] = tiles(f, i, j)
            outs[4 + side][f : f + 1, :] = tiles(f, 0, j)
            outs[6 + side][f : f + 1, :] = tiles(f, rows - 1, j)
    for side in range(2):
        outs[2 + side][5 * rows : SIDE_PARTICLES, :] = jnp.zeros(
            (SIDE_PARTICLES - 5 * rows, 128), F32
        )
        outs[4 + side][5:8, :] = jnp.zeros((3, 128), F32)
        outs[6 + side][5:8, :] = jnp.zeros((3, 128), F32)
    pl.semaphore_wait(barrier, len(AROUND))
    copies = rim_copies(outs, ins, send_sem, recv_sem)
    for copy in copies:
        copy.start()
    for f in range(5):
        for i in range(rows):
            pad_ref[f, i + 1, 1 : cols + 1, :] = tiles(f, i, everything)
    for copy in copies:
        copy.wait()
    (a, c), (na, nc) = my_place(), sizes()
    inside = [a > 0, a < na - 1, c > 0, c < nc - 1]

    def kept(f, value, *tests):
        if f < 4:
            return value
        for test in tests:
            value = jnp.where(test, value, 0.0)
        return value

    for f in range(5):
        pad_ref[f, 0, 1 : cols + 1, :] = kept(f, ins[0][f * cols : (f + 1) * cols, :], inside[0])
        pad_ref[f, rows + 1, 1 : cols + 1, :] = kept(
            f, ins[1][f * cols : (f + 1) * cols, :], inside[1]
        )
        for side, j in ((0, 0), (1, cols + 1)):
            for i in range(rows):
                pad_ref[f, i + 1, j : j + 1, :] = kept(
                    f, ins[2 + side][f * rows + i : f * rows + i + 1, :], inside[2 + side]
                )
            pad_ref[f, 0, j : j + 1, :] = kept(
                f, ins[4 + side][f : f + 1, :], inside[0], inside[2 + side]
            )
            pad_ref[f, rows + 1, j : j + 1, :] = kept(
                f, ins[6 + side][f : f + 1, :], inside[1], inside[2 + side]
            )


def rims_call(offsets, velocity, mass):
    rows, cols = mass.shape[0], mass.shape[1]
    heights = [5 * cols] * 2 + [SIDE_PARTICLES] * 2 + [8] * 4
    buffers = [pltpu.VMEM((h, 128), F32) for h in heights]
    return pl.pallas_call(
        rims_kernel,
        out_shape=jax.ShapeDtypeStruct((5, rows + 2, cols + 2, 128), F32),
        in_specs=[vmem()] * 3,
        out_specs=vmem(),
        scratch_shapes=[
            *buffers,
            *buffers,
            pltpu.SemaphoreType.DMA((8,)),
            pltpu.SemaphoreType.DMA((8,)),
        ],
        compiler_params=pltpu.CompilerParams(
            vmem_limit_bytes=VMEM_LIMIT, collective_id=0, has_side_effects=True
        ),
        name="rims",
    )(offsets, velocity, mass)


def finish_kernel(
    back_ref, dest_ref, rank_ref, state_in, dens_in, out_ref, state_ref, dens_ref, table_ref, sems
):
    copies = [
        pltpu.make_async_copy(state_in, state_ref, sems.at[0]),
        pltpu.make_async_copy(dens_in, dens_ref, sems.at[1]),
    ]
    for copy in copies:
        copy.start()
    tail = back_ref[pl.ds(3, 128, stride=8), :]
    tails = [tail, pltpu.roll(tail, 64, 1), back_ref[pl.ds(4, 128, stride=8), :]]
    for k in range(3):
        for part, piece in enumerate(split2(back_ref[pl.ds(k, 128, stride=8), :])):
            table_ref[k * 128 : k * 128 + 128, part * 192 : part * 192 + 128] = piece.astype(BF16)
        for part, piece in enumerate(split2(tails[k])):
            table_ref[
                k * 128 : k * 128 + 128, part * 192 + 128 : part * 192 + 192
            ] = piece[:, 0:64].astype(BF16)
    d_iota = iota((128, 128), 0)
    p_iota = iota((192, 128), 0).astype(F32)

    def step(g, carry):
        at = pl.ds(g * 8, 8)
        dest8 = dest_ref[at, :]
        rank8 = rank_ref[at, :]
        found = [[], [], []]
        for pair in range(4):
            slots = jnp.concatenate(
                [
                    jnp.where(
                        p_iota == jnp.broadcast_to(rank8[r : r + 1], (192, 128)), 1.0, 0.0
                    ).astype(BF16)
                    for r in (2 * pair, 2 * pair + 1)
                ],
                1,
            )
            got = dot(table_ref[...], jnp.concatenate([slots, slots], 0), NN)
            for k in range(3):
                for h in range(2):
                    r = 2 * pair + h
                    hit = d_iota == jnp.broadcast_to(dest8[r : r + 1], (128, 128))
                    part = got[k * 128 : k * 128 + 128, h * 128 : h * 128 + 128]
                    found[k].append(jnp.sum(jnp.where(hit, part, 0.0), axis=0, keepdims=True))
        for k in range(3):
            out_ref[k, at, :] = jnp.concatenate(found[k], 0)
        return carry

    lax.fori_loop(0, dest_ref.shape[0] // 8, step, 0, unroll=2)
    for copy in copies:
        copy.wait()


def finish_call(back, dest, rank, state, density):
    anywhere = pl.BlockSpec(memory_space=pl.ANY)
    return pl.pallas_call(
        finish_kernel,
        out_shape=(
            jax.ShapeDtypeStruct((3, 64, 128), F32),
            jax.ShapeDtypeStruct(state.shape, F32),
            jax.ShapeDtypeStruct(density.shape, F32),
        ),
        in_specs=[vmem(), vmem(), vmem(), anywhere, anywhere],
        out_specs=(vmem(), anywhere, anywhere),
        scratch_shapes=[pltpu.VMEM((384, 384), BF16), pltpu.SemaphoreType.DMA((2,))],
        compiler_params=pltpu.CompilerParams(vmem_limit_bytes=VMEM_LIMIT),
        name="finish",
    )(back, dest, rank, state, density)


GROUPS = 4
PER_GROUP = 32
STEP = 16


def row_and_column(cell):
    row = jnp.floor(cell * (1.0 / 512.0))
    return row, cell - row * 512.0


def unfold(got_ref, slots_ref, group):
    low_half = iota((16, 128), 1) < 64
    first_row = group * PER_GROUP * 8
    for k in range(4):
        slots_ref[k, 0:32, :] = got_ref[pl.ds(first_row + k, 32, stride=8), :]
        row = got_ref[pl.ds(first_row + 4 + k // 2, 32, stride=8), :]
        first, second = row[0:16], row[16:32]
        if k % 2 == 0:
            full = jnp.where(low_half, first, pltpu.roll(second, 64, 1))
        else:
            full = jnp.where(low_half, pltpu.roll(first, 64, 1), second)
        slots_ref[k, 32:48, :] = full


def deposit_group(group, slots_ref, cells_ref, left_ref, right_ref, acc_ref):
    r_iota = iota((128, 128), 0).astype(F32)
    c_iota = iota((512, 128), 0).astype(F32)
    cells_ref[pl.ds(pl.multiple_of(group * 48, 8), 48), :] = slots_ref[0]

    def step(g, carry):
        at = pl.ds(pl.multiple_of(g * STEP, STEP), STEP)
        row8, col8 = row_and_column(slots_ref[0, at, :])
        vals8 = [split8(slots_ref[1 + k, at, :] * 0.5) for k in range(3)]
        for r in range(STEP):
            lanes = slice(r * 128, r * 128 + 128)
            hit = r_iota == jnp.broadcast_to(row8[r : r + 1], (128, 128))
            for part in range(3):
                for k in range(3):
                    v = jnp.broadcast_to(vals8[k][part][r : r + 1], (128, 128))
                    base = (part * 3 + k) * 128
                    left_ref[base : base + 128, lanes] = jnp.where(hit, v, 0.0).astype(F8)
            right_ref[:, lanes] = jnp.where(
                c_iota == jnp.broadcast_to(col8[r : r + 1], (512, 128)), 1.0, 0.0
            ).astype(F8)
        acc_ref[...] += dot(left_ref[...], right_ref[...], NT)
        return carry

    lax.fori_loop(0, 48 // STEP, step, 0)


def deposit_sum(acc_ref, k):
    t0, t1, t2 = [
        acc_ref[(part * 3 + k) * 128 : (part * 3 + k) * 128 + 128, :] for part in range(3)
    ]
    return 2.0 * (t0 + (1.0 / 16.0) * t1 + (1.0 / 256.0) * t2)


def lookup_table(state, k, table_ref):
    most = jnp.max(jnp.max(jnp.abs(state), axis=0, keepdims=True), axis=1, keepdims=True)
    most = jnp.maximum(most, 1e-30)
    for part, term in enumerate(split8(state * (256.0 / most))):
        table_ref[k * 128 : k * 128 + 128, part * 512 : part * 512 + 512] = term.astype(F8)
    return most * (1.0 / 256.0)


def lookup_group(group, cells_ref, table_ref, undo, found_ref, back_ref):
    r_iota = iota((128, 128), 0).astype(F32)
    c_iota = iota((512, 128), 0).astype(F32)

    def step(g, carry):
        at = pl.ds(pl.multiple_of(group * 48 + g * 8, 8), 8)
        row8, col8 = row_and_column(cells_ref[at, :])
        found = [[], [], []]
        for pair in range(4):
            rights = [[], [], []]
            for r in (2 * pair, 2 * pair + 1):
                column = c_iota == jnp.broadcast_to(col8[r : r + 1], (512, 128))
                for part, share in enumerate((1.0, 1.0 / 16.0, 1.0 / 256.0)):
                    rights[part].append(jnp.where(column, share, 0.0).astype(F8))
            right = jnp.concatenate([jnp.concatenate(halves, 1) for halves in rights], 0)
            got = dot(table_ref[...], right, NN)
            for k in range(3):
                for h in range(2):
                    r = 2 * pair + h
                    hit = r_iota == jnp.broadcast_to(row8[r : r + 1], (128, 128))
                    part = got[k * 128 : k * 128 + 128, h * 128 : h * 128 + 128]
                    found[k].append(jnp.sum(jnp.where(hit, part, 0.0), axis=0, keepdims=True))
        for k in range(3):
            found_ref[k, pl.ds(pl.multiple_of(g * 8, 8), 8), :] = (
                jnp.concatenate(found[k], 0) * undo[k]
            )
        return carry

    lax.fori_loop(0, 6, step, 0)
    low_half = iota((16, 128), 1) < 64
    first_row = group * PER_GROUP * 8
    tails = [found_ref[k, 32:48, :] for k in range(3)]
    turned = [pltpu.roll(t, 64, 1) for t in tails]
    for k in range(3):
        back_ref[pl.ds(first_row + k, 32, stride=8), :] = found_ref[k, 0:32, :]
    back_ref[pl.ds(first_row + 3, 16, stride=8), :] = jnp.where(low_half, tails[0], turned[1])
    back_ref[pl.ds(first_row + 131, 16, stride=8), :] = jnp.where(low_half, turned[0], tails[1])
    back_ref[pl.ds(first_row + 4, 16, stride=8), :] = tails[2]
    back_ref[pl.ds(first_row + 132, 16, stride=8), :] = turned[2]
    for k in range(5, 8):
        back_ref[pl.ds(first_row + k, 32, stride=8), :] = jnp.zeros((32, 128), F32)


TALL = 136
BROAD = 640


def place_rims(wide_ref, index, f, refs, bases):
    up, down, left, right, *corners = refs
    upper_half = iota((8, 128), 0) < 4
    for b in range(4):
        at = bases[0] + (f * 4 + b) * 8
        wide_ref[index, 128:136, b * 128 : b * 128 + 128] = jnp.where(
            upper_half, down[at : at + 8, :], up[at : at + 8, :]
        )
    to_left = (128 - DEEP - DEEP * f) % 128
    to_right = (128 - DEEP * f) % 128

    def strip(left_part, right_part):
        moved_left = pltpu.roll(left_part, to_left, 1) if to_left else left_part
        moved_right = pltpu.roll(right_part, to_right, 1) if to_right else right_part
        return jnp.where(iota(left_part.shape, 1) < 64, moved_right, moved_left)

    sides = slice(bases[1], bases[1] + 128)
    wide_ref[index, 0:128, 512:640] = strip(left[sides, :], right[sides, :])
    rows = slice(bases[2], bases[2] + 8)
    c = [
        jnp.where(upper_half, corners[2 + side][rows, :], corners[side][rows, :])
        for side in range(2)
    ]
    wide_ref[index, 128:136, 512:640] = strip(c[0], c[1])


def inside_grid(block):
    (a, c), (na, nc) = my_place(), sizes()
    cols = iota((8, BROAD), 1)
    cols = jnp.where(cols < 576, cols, cols - BROAD) + c * 512
    rows = iota((8, BROAD), 0) + block * 8
    rows = jnp.where(rows < 132, rows, rows - TALL) + a * 128
    return (cols >= 0) & (cols < nc * 512) & (rows >= 0) & (rows < na * 128)


def water_step(old_ref, new_ref, depth_ref, source_ref):
    blocks = TALL // 8
    sub = iota((8, BROAD), 0)

    def load(block):
        at = slice(block * 8, block * 8 + 8)
        h, u, v = [old_ref[f, at, :] for f in range(3)]
        fu = depth_ref[0, at, :] * u
        fields = (h, u, v, fu)
        return fields, [pltpu.roll(x, 1, 0) for x in fields], [pltpu.roll(x, 7, 0) for x in fields]

    def left(x):
        return pltpu.roll(x, 1, 1)

    def right(x):
        return pltpu.roll(x, BROAD - 1, 1)

    before, here = load(blocks - 1), load(0)
    for block in range(blocks):
        after = load((block + 1) % blocks)
        at = slice(block * 8, block * 8 + 8)
        (h, u, v, _), down, up = here
        h_w, u_w, v_w, fu_w = [jnp.where(sub == 0, p, q) for p, q in zip(before[1], down)]
        h_e, u_e, v_e, fu_e = [jnp.where(sub == 7, p, q) for p, q in zip(after[2], up)]
        fv = depth_ref[0, at, :] * v
        h_s, h_n = left(h), right(h)
        next_h = 0.25 * (h_e + h_w + h_n + h_s) - 0.5 * courant * (
            fu_e - fu_w + right(fv) - left(fv)
        )
        next_u = 0.25 * (u_e + u_w + right(u) + left(u)) - 0.5 * courant * (h_e - h_w)
        next_v = 0.25 * (v_e + v_w + right(v) + left(v)) - 0.5 * courant * (h_n - h_s)
        inside = inside_grid(block)
        for f, value in enumerate((next_h, next_u, next_v)):
            new_ref[f, at, :] = jnp.where(inside, value + source_ref[f, at, :], 0.0)
        before, here = here, after


def main_kernel(
    pad_ref, near_ref, dest_ref, cell_ref, surface_ref, depth_ref,
    dens_ref, rank_ref, state_ref, back_got,
    sums_ref, vals_ref, pleft_ref, pslots_ref, pacc_ref, send_ref, got_ref,
    slots_ref, cells_ref, left_ref, right_ref, acc_ref,
    even, odd, deep, wide_source,
    table_ref, found_ref, back_ref,
    o0, o1, o2, o3, o4, o5, o6, o7, i0, i1, i2, i3, i4, i5, i6, i7,
    q0, q1, q2, q3, q4, q5, q6, q7, g0, g1, g2, g3, g4, g5, g6, g7,
    rim_send, rim_recv, first_send, first_recv,
    out_sem, in_sem, back_out_sem, back_in_sem, state_sem,
):
    (a, c), (na, nc) = my_place(), sizes()
    count = na * nc
    me = a * nc + c

    def device(n):
        return (lax.div(n, nc), lax.rem(n, nc))

    def block(n):
        return pl.ds(pl.multiple_of(n * 8, 8), 8)

    barrier = pltpu.get_barrier_semaphore()

    def greet(step, carry):
        pl.semaphore_signal(
            barrier, inc=1, device_id=device(lax.rem(me + step, count)), device_id_type=MESH
        )
        return carry

    lax.fori_loop(1, count, greet, 0)

    window_sums(pad_ref, near_ref, dest_ref, sums_ref, rank_ref)
    rows, cols = pad_ref.shape[1] - 2, pad_ref.shape[2] - 2
    for i in range(rows):
        at = slice(i * cols, (i + 1) * cols)
        s0 = sums_ref[0, at, :]
        density = s0 / 128.0
        dens_ref[at, :] = density
        volume = pad_ref[4, i + 1, 1 : cols + 1, :] / density
        vals_ref[0, at, :] = cell_ref[at, :].astype(F32)
        vals_ref[1, at, :] = volume
        vals_ref[2, at, :] = volume * (sums_ref[1, at, :] / s0)
        vals_ref[3, at, :] = volume * (sums_ref[2, at, :] / s0)
    pack(dest_ref, vals_ref, rank_ref, send_ref, pleft_ref, pslots_ref, pacc_ref)

    pl.semaphore_wait(barrier, count - 1)

    def send_out(group):
        def start(step, carry):
            to = lax.rem(me + step, count)
            pltpu.make_async_remote_copy(
                src_ref=send_ref.at[block(to), :],
                dst_ref=got_ref.at[block(step), :],
                send_sem=out_sem,
                recv_sem=in_sem.at[group],
                device_id=device(to),
                device_id_type=MESH,
            ).start()
            return carry

        lax.fori_loop(max(1, group * PER_GROUP), (group + 1) * PER_GROUP, start, 0)

    for group in range(GROUPS):
        send_out(group)
    got_ref[0:8, :] = send_ref[block(me), :]

    first_outs = [q0, q1, q2, q3, q4, q5, q6, q7]
    first_ins = [g0, g1, g2, g3, g4, g5, g6, g7]
    write_rims(first_outs, [0, 0, 0, 0, 0], [
        lambda r, c: surface_ref[0, r, c],
        lambda r, c: surface_ref[1, r, c],
        lambda r, c: surface_ref[2, r, c],
        lambda r, c: depth_ref[r, c],
    ])
    copies = rim_copies(first_outs, first_ins, first_send, first_recv)
    for copy in copies:
        copy.start()
    for f in range(3):
        even[f, 0:128, 0:512] = surface_ref[f]
    deep[0, 0:128, 0:512] = depth_ref[...]
    acc_ref[...] = jnp.zeros_like(acc_ref)
    for copy in copies:
        copy.wait()
    for f in range(3):
        place_rims(even, f, f, first_ins, [0, 0, 0])
    place_rims(deep, 0, 3, first_ins, [0, 0, 0])
    for b in range(TALL // 8):
        at = slice(b * 8, b * 8 + 8)
        for f in range(3):
            even[f, at, :] = jnp.where(inside_grid(b), even[f, at, :], 0.0)

    for group in range(GROUPS):
        landed = got_ref.at[max(8, group * PER_GROUP * 8) : (group + 1) * PER_GROUP * 8, :]
        pltpu.make_async_copy(landed, landed, in_sem.at[group]).wait()
        unfold(got_ref, slots_ref, group)
        deposit_group(group, slots_ref, cells_ref, left_ref, right_ref, acc_ref)
    for k in range(3):
        wide_source[k, 0:128, 0:512] = deposit_sum(acc_ref, k)

    outs = [o0, o1, o2, o3, o4, o5, o6, o7]
    ins = [i0, i1, i2, i3, i4, i5, i6, i7]
    write_rims(outs, [0, 0, 0, 0, 0], [
        lambda r, c: wide_source[0, r, c],
        lambda r, c: wide_source[1, r, c],
        lambda r, c: wide_source[2, r, c],
    ])
    copies = rim_copies(outs, ins, rim_send, rim_recv)
    for copy in copies:
        copy.start()
    for copy in copies:
        copy.wait()
    for f in range(3):
        place_rims(wide_source, f, f, ins, [0, 0, 0])

    def two_steps(n, carry):
        water_step(even, odd, deep, wide_source)
        water_step(odd, even, deep, wide_source)
        return carry

    lax.fori_loop(0, SUBSTEPS // 2, two_steps, 0)
    keep = pltpu.make_async_copy(even.at[:, 0:128, 0:512], state_ref, state_sem)
    keep.start()
    undo = [lookup_table(even[k, 0:128, 0:512], k, table_ref) for k in range(3)]

    for group in range(GROUPS):
        lookup_group(group, cells_ref, table_ref, undo, found_ref, back_ref)

        def start(step, carry):
            pltpu.make_async_remote_copy(
                src_ref=back_ref.at[block(step), :],
                dst_ref=back_got.at[block(me), :],
                send_sem=back_out_sem,
                recv_sem=back_in_sem,
                device_id=device(lax.rem(me - step + count, count)),
                device_id_type=MESH,
            ).start()
            return carry

        lax.fori_loop(max(1, group * PER_GROUP), (group + 1) * PER_GROUP, start, 0)
    back_got[block(me), :] = back_ref[0:8, :]
    others = (count - 1) * 8
    for ref, sem in (
        (back_got, back_in_sem),
        (send_ref, out_sem),
        (back_ref, back_out_sem),
    ):
        pltpu.make_async_copy(ref.at[0:others, :], ref.at[0:others, :], sem).wait()
    keep.wait()


def main_call(pad, near, dest, cell, surface, depth):
    def buffers(heights):
        return [pltpu.VMEM((h, 128), F32) for h in heights + [8, 8, 8, 8]]

    dma = pltpu.SemaphoreType.DMA
    anywhere = pl.BlockSpec(memory_space=pl.ANY)
    return pl.pallas_call(
        main_kernel,
        out_shape=(
            jax.ShapeDtypeStruct((64, 128), F32),
            jax.ShapeDtypeStruct((64, 128), F32),
            jax.ShapeDtypeStruct((3, 128, 512), F32),
            jax.ShapeDtypeStruct((1024, 128), F32),
        ),
        in_specs=[vmem(), pl.BlockSpec(memory_space=pltpu.SMEM)] + [vmem()] * 4,
        out_specs=(vmem(), vmem(), anywhere, vmem()),
        scratch_shapes=[
            pltpu.VMEM((3, 64, 128), F32),
            pltpu.VMEM((4, 64, 128), F32),
            pltpu.VMEM((1024, 1024), BF16),
            pltpu.VMEM((192, 1024), BF16),
            pltpu.VMEM((1024, 256), F32),
            pltpu.VMEM((1024, 128), F32),
            pltpu.VMEM((1024, 128), F32),
            pltpu.VMEM((4, 48, 128), F32),
            pltpu.VMEM((192, 128), F32),
            pltpu.VMEM((1152, STEP * 128), F8),
            pltpu.VMEM((512, STEP * 128), F8),
            pltpu.VMEM((1152, 512), F32),
            pltpu.VMEM((3, TALL, BROAD), F32),
            pltpu.VMEM((3, TALL, BROAD), F32),
            pltpu.VMEM((1, TALL, BROAD), F32),
            pltpu.VMEM((3, TALL, BROAD), F32),
            pltpu.VMEM((384, 1536), F8),
            pltpu.VMEM((3, 48, 128), F32),
            pltpu.VMEM((1024, 128), F32),
            *buffers([96, 96, 128, 128]),
            *buffers([96, 96, 128, 128]),
            *buffers([128, 128, 128, 128]),
            *buffers([128, 128, 128, 128]),
            dma((8,)),
            dma((8,)),
            dma((8,)),
            dma((8,)),
            dma,
            dma((GROUPS,)),
            dma,
            dma,
            dma,
        ],
        compiler_params=pltpu.CompilerParams(
            vmem_limit_bytes=VMEM_LIMIT, collective_id=1, has_side_effects=True
        ),
        name="main",
    )(pad, near, dest, cell, surface, depth)


def shards(
    offsets, velocity, particle_mass, neighbours, owner_device, target_cell, surface, water_depth
):
    padded = rims_call(offsets, velocity, particle_mass)
    dest = owner_device.reshape(64, 128)
    density, rank, water_state, back = main_call(
        padded, jnp.transpose(neighbours, (2, 0, 1)), dest, target_cell.reshape(64, 128), surface, water_depth
    )
    feedback, water_state, density = finish_call(back, dest, rank, water_state, density)
    return (
        water_state,
        density.reshape(particle_mass.shape),
        feedback.reshape((3,) + particle_mass.shape),
    )


def solution(mesh):
    in_specs = (
        P(None, "along", "cross", None),
        P(None, "along", "cross", None),
        P("along", "cross", None),
        P("along", "cross", None),
        P("along", "cross", None, None),
        P("along", "cross", None),
        P(None, "along", "cross"),
        P("along", "cross"),
    )
    out_specs = (
        P(None, "along", "cross"),
        P("along", "cross", None),
        P(None, "along", "cross", None),
    )
    return jax.shard_map(shards, mesh=mesh, in_specs=in_specs, out_specs=out_specs, check_vma=False)
```

```python
import math

import jax
import jax.numpy as jnp
from jax import lax
from jax.experimental import pallas as pl
from jax.experimental.pallas import tpu as pltpu
from jax.sharding import PartitionSpec as P

SUBSTEPS = 4
KAPPA = math.sqrt(math.log2(math.e))
F32 = jnp.float32
BF16 = jnp.bfloat16
F8 = jnp.float8_e4m3fn
NN = (((1,), (0,)), ((), ()))
NT = (((1,), (1,)), ((), ()))
VMEM_LIMIT = 56 * 1024 * 1024

courant = 0.4


def dot(a, b, dims):
    return lax.dot_general(a, b, dims, preferred_element_type=F32)


def split2(x):
    hi = x.astype(BF16).astype(F32)
    return hi, x - hi


def split8(x):
    t0 = x.astype(F8).astype(F32)
    r = (x - t0) * 16.0
    t1 = r.astype(F8).astype(F32)
    return t0, t1, (r - t1) * 16.0


def iota(shape, dim):
    return lax.broadcasted_iota(jnp.int32, shape, dim)


def window_sums(pad_ref, near_ref, dest_ref, sums_ref, rank_ref):
    cols = pad_ref.shape[2] - 2
    d_iota = iota((128, 128), 0)
    before = jnp.concatenate(
        [
            (iota((128, 128), 0) < iota((128, 128), 1)).astype(F32),
            jnp.ones((128, 128), F32),
        ],
        1,
    ).astype(BF16)

    def tile(i, j, row, running):
        hit = d_iota == jnp.broadcast_to(dest_ref[pl.ds(row, 1), :], (128, 128))
        counts = dot(jnp.where(hit, 1.0, 0.0).astype(BF16), before, NN)
        rank_ref[pl.ds(row, 1), :] = jnp.sum(
            jnp.where(hit, counts[:, :128] + running, 0.0), axis=0, keepdims=True
        )
        running = running + counts[:, 128:]
        x = pad_ref[0, i + 1, pl.ds(j + 1, 1), :] * KAPPA
        y = pad_ref[1, i + 1, pl.ds(j + 1, 1), :] * KAPPA
        x_col = jnp.broadcast_to(x, (128, 128)).T
        y_col = jnp.broadcast_to(y, (128, 128)).T
        listed = jnp.int32(0)
        for slot in range(9):
            listed = listed | lax.shift_left(jnp.int32(1), near_ref[slot, i, j] + 1)
        window = []
        for w in range(9):
            bi, bj = i + w // 3, j + w % 3
            bx = (pad_ref[0, bi, pl.ds(bj, 1), :] + (w // 3 - 1.0)) * KAPPA
            by = (pad_ref[1, bi, pl.ds(bj, 1), :] + (w % 3 - 1.0)) * KAPPA
            c0 = pad_ref[4, bi, pl.ds(bj, 1), :] * jnp.exp2(-bx * bx - by * by)
            c0 = c0 * (lax.shift_right_logical(listed, w + 1) & 1).astype(F32)
            c1 = c0 * pad_ref[2, bi, pl.ds(bj, 1), :]
            c2 = c0 * pad_ref[3, bi, pl.ds(bj, 1), :]
            window.append((2.0 * bx, 2.0 * by, c0, c1, c2))
        acc = [jnp.zeros((128, 128), F32)] * 3
        for bx, by, *carried in window:
            weights = jnp.exp2(x_col * bx + y_col * by)
            acc = [total + weights * c for total, c in zip(acc, carried)]
        scale = jnp.exp2(-x * x - y * y)
        for k in range(3):
            sums_ref[k, pl.ds(i * cols + j, 1), :] = jnp.sum(acc[k].T, axis=0, keepdims=True) * scale
        return running

    return tile


def pack(dest_ref, vals_ref, rank_ref, send_ref, left_ref, slots_ref, acc_ref):
    groups = dest_ref.shape[0] // 8
    d_iota = iota((128, 128), 0)
    p_iota = iota((192, 128), 0).astype(F32)
    acc_ref[...] = jnp.zeros_like(acc_ref)

    def group(g, carry):
        at = pl.ds(pl.multiple_of(g * 8, 8), 8)
        dest8 = dest_ref[at, :]
        rank8 = rank_ref[at, :]
        vals8 = [split2(vals_ref[k, at, :]) for k in range(4)]
        for r in range(8):
            hit = d_iota == jnp.broadcast_to(dest8[r : r + 1], (128, 128))
            lanes = slice(r * 128, r * 128 + 128)
            slots_ref[:, lanes] = jnp.where(
                p_iota == jnp.broadcast_to(rank8[r : r + 1], (192, 128)), 1.0, 0.0
            ).astype(BF16)
            for part in range(2):
                for k in range(4):
                    v = jnp.broadcast_to(vals8[k][part][r : r + 1], (128, 128))
                    base = (part * 4 + k) * 128
                    left_ref[base : base + 128, lanes] = jnp.where(hit, v, 0.0).astype(BF16)
        acc_ref[:, 0:192] += dot(left_ref[...], slots_ref[...], NT)
        return carry

    lax.fori_loop(0, groups, group, 0)
    tails = []
    for k in range(4):
        send_ref[pl.ds(k, 128, stride=8), :] = acc_ref[k * 128 : k * 128 + 128, 0:128] + acc_ref[
            512 + k * 128 : 640 + k * 128, 0:128
        ]
        tails.append(
            acc_ref[k * 128 : k * 128 + 128, 128:256]
            + acc_ref[512 + k * 128 : 640 + k * 128, 128:256]
        )
    low_half = iota((128, 128), 1) < 64
    for k in range(6, 8):
        send_ref[pl.ds(k, 128, stride=8), :] = jnp.zeros((128, 128), F32)
    for h in range(2):
        send_ref[pl.ds(4 + h, 128, stride=8), :] = jnp.where(
            low_half, tails[2 * h], pltpu.roll(tails[2 * h + 1], 64, 1)
        )


def vmem():
    return pl.BlockSpec(memory_space=pltpu.VMEM)


MESH = pl.DeviceIdType.MESH
AROUND = [(-1, 0), (1, 0), (0, -1), (0, 1), (-1, -1), (-1, 1), (1, -1), (1, 1)]


def my_place():
    return lax.axis_index("along"), lax.axis_index("cross")


def sizes():
    return lax.axis_size("along"), lax.axis_size("cross")


def at_step(step):
    (a, c), (na, nc) = my_place(), sizes()
    return lax.rem(a + step[0] + na, na), lax.rem(c + step[1] + nc, nc)


def rim_copies(out_refs, in_refs, send_sem, recv_sem):
    copies = []
    for n, step in enumerate(AROUND):
        opposite = AROUND.index((-step[0], -step[1]))
        copies.append(
            pltpu.make_async_remote_copy(
                src_ref=out_refs[n],
                dst_ref=in_refs[opposite],
                send_sem=send_sem.at[n],
                recv_sem=recv_sem.at[opposite],
                device_id=at_step(step),
                device_id_type=MESH,
            )
        )
    return copies


DEEP = 4
SIDE_PARTICLES = 24


def column_strip(fields, right):
    lanes = iota((fields[0].shape[0], 128), 1)
    out = jnp.zeros((fields[0].shape[0], 128), F32)
    for f, field in enumerate(fields):
        turn = DEEP * f + (DEEP if right else 0)
        moved = pltpu.roll(field, turn, 1) if turn else field
        out = jnp.where((lanes >= DEEP * f) & (lanes < DEEP * f + DEEP), moved, out)
    return out


def write_rims(out_refs, base, fields):
    top, bottom = slice(0, 8), slice(120, 128)
    for n, rows in ((0, top), (1, bottom)):
        for f, field in enumerate(fields):
            for b in range(4):
                at = base[n] + (f * 4 + b) * 8
                out_refs[n][at : at + 8, :] = field(rows, slice(b * 128, b * 128 + 128))
    for right in range(2):
        lanes = slice(384, 512) if right else slice(0, 128)
        strip = column_strip([field(slice(0, 128), lanes) for field in fields], right == 1)
        at = base[2 + right]
        out_refs[2 + right][at : at + 128, :] = strip
        out_refs[4 + right][base[4] : base[4] + 8, :] = strip[0:8]
        out_refs[6 + right][base[4] : base[4] + 8, :] = strip[120:128]


def stage_particles(particle, rows, cols, outs, pad_ref):
    def tiles(f, i, j):
        ref, part = particle[f]
        return ref[i, j, :] if part is None else ref[part, i, j, :]

    everything = slice(0, cols)
    for f in range(5):
        outs[0][f * cols : (f + 1) * cols, :] = tiles(f, 0, everything)
        outs[1][f * cols : (f + 1) * cols, :] = tiles(f, rows - 1, everything)
        for side, j in ((0, slice(0, 1)), (1, slice(cols - 1, cols))):
            for i in range(rows):
                outs[2 + side][f * rows + i : f * rows + i + 1, :] = tiles(f, i, j)
            outs[4 + side][f : f + 1, :] = tiles(f, 0, j)
            outs[6 + side][f : f + 1, :] = tiles(f, rows - 1, j)
    for side in range(2):
        outs[2 + side][5 * rows : SIDE_PARTICLES, :] = jnp.zeros(
            (SIDE_PARTICLES - 5 * rows, 128), F32
        )
        outs[4 + side][5:8, :] = jnp.zeros((3, 128), F32)
        outs[6 + side][5:8, :] = jnp.zeros((3, 128), F32)
    for f in range(5):
        for i in range(rows):
            pad_ref[f, i + 1, 1 : cols + 1, :] = tiles(f, i, everything)


def place_particles(ins, rows, cols, pad_ref):
    (a, c), (na, nc) = my_place(), sizes()
    inside = [a > 0, a < na - 1, c > 0, c < nc - 1]

    def kept(f, value, *tests):
        if f < 4:
            return value
        for test in tests:
            value = jnp.where(test, value, 0.0)
        return value

    for f in range(5):
        pad_ref[f, 0, 1 : cols + 1, :] = kept(f, ins[0][f * cols : (f + 1) * cols, :], inside[0])
        pad_ref[f, rows + 1, 1 : cols + 1, :] = kept(
            f, ins[1][f * cols : (f + 1) * cols, :], inside[1]
        )
        for side, j in ((0, 0), (1, cols + 1)):
            for i in range(rows):
                pad_ref[f, i + 1, j : j + 1, :] = kept(
                    f, ins[2 + side][f * rows + i : f * rows + i + 1, :], inside[2 + side]
                )
            pad_ref[f, 0, j : j + 1, :] = kept(
                f, ins[4 + side][f : f + 1, :], inside[0], inside[2 + side]
            )
            pad_ref[f, rows + 1, j : j + 1, :] = kept(
                f, ins[6 + side][f : f + 1, :], inside[1], inside[2 + side]
            )


def finish_kernel(
    back_ref, dest_ref, rank_ref, state_in, dens_in, out_ref, state_ref, dens_ref, table_ref
):
    state_ref[...] = state_in[...]
    dens_ref[...] = dens_in[...]
    tail = back_ref[pl.ds(3, 128, stride=8), :]
    tails = [tail, pltpu.roll(tail, 64, 1), back_ref[pl.ds(4, 128, stride=8), :]]
    for k in range(3):
        for part, piece in enumerate(split2(back_ref[pl.ds(k, 128, stride=8), :])):
            table_ref[k * 128 : k * 128 + 128, part * 192 : part * 192 + 128] = piece.astype(BF16)
        for part, piece in enumerate(split2(tails[k])):
            table_ref[
                k * 128 : k * 128 + 128, part * 192 + 128 : part * 192 + 192
            ] = piece[:, 0:64].astype(BF16)
    d_iota = iota((128, 128), 0)
    p_iota = iota((192, 128), 0).astype(F32)

    def step(g, carry):
        at = pl.ds(g * 8, 8)
        dest8 = dest_ref[at, :]
        rank8 = rank_ref[at, :]
        found = [[], [], []]
        for pair in range(4):
            slots = jnp.concatenate(
                [
                    jnp.where(
                        p_iota == jnp.broadcast_to(rank8[r : r + 1], (192, 128)), 1.0, 0.0
                    ).astype(BF16)
                    for r in (2 * pair, 2 * pair + 1)
                ],
                1,
            )
            got = dot(table_ref[...], jnp.concatenate([slots, slots], 0), NN)
            for k in range(3):
                for h in range(2):
                    r = 2 * pair + h
                    hit = d_iota == jnp.broadcast_to(dest8[r : r + 1], (128, 128))
                    part = got[k * 128 : k * 128 + 128, h * 128 : h * 128 + 128]
                    found[k].append(jnp.sum(jnp.where(hit, part, 0.0), axis=0, keepdims=True))
        for k in range(3):
            out_ref[k, at, :] = jnp.concatenate(found[k], 0)
        return carry

    lax.fori_loop(0, dest_ref.shape[0] // 8, step, 0, unroll=2)


def finish_call(back, dest, rank, state, density):
    return pl.pallas_call(
        finish_kernel,
        out_shape=(
            jax.ShapeDtypeStruct((3, 64, 128), F32),
            jax.ShapeDtypeStruct(state.shape, F32),
            jax.ShapeDtypeStruct(density.shape, F32),
        ),
        in_specs=[vmem()] * 5,
        out_specs=(vmem(), vmem(), vmem()),
        scratch_shapes=[pltpu.VMEM((384, 384), BF16)],
        compiler_params=pltpu.CompilerParams(vmem_limit_bytes=VMEM_LIMIT),
        name="finish",
    )(back, dest, rank, state, density)


GROUPS = 4
PER_GROUP = 32
STEP = 16


def row_and_column(cell):
    row = jnp.floor(cell * (1.0 / 512.0))
    return row, cell - row * 512.0


def unfold(got_ref, slots_ref, group):
    low_half = iota((16, 128), 1) < 64
    first_row = group * PER_GROUP * 8
    for k in range(4):
        slots_ref[k, 0:32, :] = got_ref[pl.ds(first_row + k, 32, stride=8), :]
        row = got_ref[pl.ds(first_row + 4 + k // 2, 32, stride=8), :]
        first, second = row[0:16], row[16:32]
        if k % 2 == 0:
            full = jnp.where(low_half, first, pltpu.roll(second, 64, 1))
        else:
            full = jnp.where(low_half, pltpu.roll(first, 64, 1), second)
        slots_ref[k, 32:48, :] = full


def deposit_group(group, slots_ref, cells_ref, left_ref, right_ref, acc_ref):
    r_iota = iota((128, 128), 0).astype(F32)
    c_iota = iota((512, 128), 0).astype(F32)
    cells_ref[pl.ds(pl.multiple_of(group * 48, 8), 48), :] = slots_ref[0]

    def step(g, carry):
        at = pl.ds(pl.multiple_of(g * STEP, STEP), STEP)
        row8, col8 = row_and_column(slots_ref[0, at, :])
        vals8 = [split8(slots_ref[1 + k, at, :] * 0.5) for k in range(3)]
        for r in range(STEP):
            lanes = slice(r * 128, r * 128 + 128)
            hit = r_iota == jnp.broadcast_to(row8[r : r + 1], (128, 128))
            for part in range(3):
                for k in range(3):
                    v = jnp.broadcast_to(vals8[k][part][r : r + 1], (128, 128))
                    base = (part * 3 + k) * 128
                    left_ref[base : base + 128, lanes] = jnp.where(hit, v, 0.0).astype(F8)
            right_ref[:, lanes] = jnp.where(
                c_iota == jnp.broadcast_to(col8[r : r + 1], (512, 128)), 1.0, 0.0
            ).astype(F8)
        acc_ref[...] += dot(left_ref[...], right_ref[...], NT)
        return carry

    lax.fori_loop(0, 48 // STEP, step, 0)


def deposit_sum(acc_ref, k):
    t0, t1, t2 = [
        acc_ref[(part * 3 + k) * 128 : (part * 3 + k) * 128 + 128, :] for part in range(3)
    ]
    return 2.0 * (t0 + (1.0 / 16.0) * t1 + (1.0 / 256.0) * t2)


def lookup_table(state, k, high_ref, low_ref):
    most = jnp.max(jnp.max(jnp.abs(state), axis=0, keepdims=True), axis=1, keepdims=True)
    most = jnp.maximum(most, 1e-30)
    hi, lo = split2(state * (1024.0 / most))
    high_ref[k * 128 : k * 128 + 128, :] = hi.astype(BF16)
    low_ref[k * 128 : k * 128 + 128, :] = (lo * 64.0).astype(F8)
    return most * (1.0 / 1024.0)


def lookup_group(group, cells_ref, high_ref, low_ref, undo, found_ref, back_ref):
    r_iota = iota((128, 128), 0).astype(F32)
    c_iota = iota((512, 128), 0).astype(F32)

    def step(g, carry):
        at = pl.ds(pl.multiple_of(group * 48 + g * 8, 8), 8)
        row8, col8 = row_and_column(cells_ref[at, :])
        found = [[], [], []]
        for pair in range(4):
            high, low = [], []
            for r in (2 * pair, 2 * pair + 1):
                column = c_iota == jnp.broadcast_to(col8[r : r + 1], (512, 128))
                high.append(jnp.where(column, 1.0, 0.0).astype(BF16))
                low.append(jnp.where(column, 1.0 / 64.0, 0.0).astype(F8))
            got = dot(high_ref[...], jnp.concatenate(high, 1), NN) + dot(
                low_ref[...], jnp.concatenate(low, 1), NN
            )
            for k in range(3):
                for h in range(2):
                    r = 2 * pair + h
                    hit = r_iota == jnp.broadcast_to(row8[r : r + 1], (128, 128))
                    part = got[k * 128 : k * 128 + 128, h * 128 : h * 128 + 128]
                    found[k].append(jnp.sum(jnp.where(hit, part, 0.0), axis=0, keepdims=True))
        for k in range(3):
            found_ref[k, pl.ds(pl.multiple_of(g * 8, 8), 8), :] = (
                jnp.concatenate(found[k], 0) * undo[k]
            )
        return carry

    lax.fori_loop(0, 6, step, 0)
    low_half = iota((16, 128), 1) < 64
    first_row = group * PER_GROUP * 8
    tails = [found_ref[k, 32:48, :] for k in range(3)]
    turned = [pltpu.roll(t, 64, 1) for t in tails]
    for k in range(3):
        back_ref[pl.ds(first_row + k, 32, stride=8), :] = found_ref[k, 0:32, :]
    back_ref[pl.ds(first_row + 3, 16, stride=8), :] = jnp.where(low_half, tails[0], turned[1])
    back_ref[pl.ds(first_row + 131, 16, stride=8), :] = jnp.where(low_half, turned[0], tails[1])
    back_ref[pl.ds(first_row + 4, 16, stride=8), :] = tails[2]
    back_ref[pl.ds(first_row + 132, 16, stride=8), :] = turned[2]
    for k in range(5, 8):
        back_ref[pl.ds(first_row + k, 32, stride=8), :] = jnp.zeros((32, 128), F32)


TALL = 136
BROAD = 640


def place_rims(wide_ref, index, f, refs, bases):
    up, down, left, right, *corners = refs
    upper_half = iota((8, 128), 0) < 4
    for b in range(4):
        at = bases[0] + (f * 4 + b) * 8
        wide_ref[index, 128:136, b * 128 : b * 128 + 128] = jnp.where(
            upper_half, down[at : at + 8, :], up[at : at + 8, :]
        )
    to_left = (128 - DEEP - DEEP * f) % 128
    to_right = (128 - DEEP * f) % 128

    def strip(left_part, right_part):
        moved_left = pltpu.roll(left_part, to_left, 1) if to_left else left_part
        moved_right = pltpu.roll(right_part, to_right, 1) if to_right else right_part
        return jnp.where(iota(left_part.shape, 1) < 64, moved_right, moved_left)

    sides = slice(bases[1], bases[1] + 128)
    wide_ref[index, 0:128, 512:640] = strip(left[sides, :], right[sides, :])
    rows = slice(bases[2], bases[2] + 8)
    c = [
        jnp.where(upper_half, corners[2 + side][rows, :], corners[side][rows, :])
        for side in range(2)
    ]
    wide_ref[index, 128:136, 512:640] = strip(c[0], c[1])


def inside_grid(block):
    (a, c), (na, nc) = my_place(), sizes()
    cols = iota((8, BROAD), 1)
    cols = jnp.where(cols < 576, cols, cols - BROAD) + c * 512
    rows = iota((8, BROAD), 0) + block * 8
    rows = jnp.where(rows < 132, rows, rows - TALL) + a * 128
    return (cols >= 0) & (cols < nc * 512) & (rows >= 0) & (rows < na * 128)


def water_step(old_ref, new_ref, depth_ref, source_ref):
    blocks = TALL // 8
    sub = iota((8, BROAD), 0)

    def load(block):
        at = slice(block * 8, block * 8 + 8)
        h, u, v = [old_ref[f, at, :] for f in range(3)]
        fu = depth_ref[0, at, :] * u
        fields = (h, u, v, fu)
        return fields, [pltpu.roll(x, 1, 0) for x in fields], [pltpu.roll(x, 7, 0) for x in fields]

    def left(x):
        return pltpu.roll(x, 1, 1)

    def right(x):
        return pltpu.roll(x, BROAD - 1, 1)

    before, here = load(blocks - 1), load(0)
    for block in range(blocks):
        after = load((block + 1) % blocks)
        at = slice(block * 8, block * 8 + 8)
        (h, u, v, _), down, up = here
        h_w, u_w, v_w, fu_w = [jnp.where(sub == 0, p, q) for p, q in zip(before[1], down)]
        h_e, u_e, v_e, fu_e = [jnp.where(sub == 7, p, q) for p, q in zip(after[2], up)]
        fv = depth_ref[0, at, :] * v
        h_s, h_n = left(h), right(h)
        next_h = 0.25 * (h_e + h_w + h_n + h_s) - 0.5 * courant * (
            fu_e - fu_w + right(fv) - left(fv)
        )
        next_u = 0.25 * (u_e + u_w + right(u) + left(u)) - 0.5 * courant * (h_e - h_w)
        next_v = 0.25 * (v_e + v_w + right(v) + left(v)) - 0.5 * courant * (h_n - h_s)
        inside = inside_grid(block)
        for f, value in enumerate((next_h, next_u, next_v)):
            new_ref[f, at, :] = jnp.where(inside, value + source_ref[f, at, :], 0.0)
        before, here = here, after


def main_kernel(
    off_ref, vel_ref, mass_ref, near_ref, dest_ref, cell_ref, surface_ref, depth_ref,
    dens_ref, rank_ref, state_ref, back_got,
    pad_ref,
    sums_ref, vals_ref, pleft_ref, pslots_ref, pacc_ref, send_ref, got_ref,
    slots_ref, cells_ref, left_ref, right_ref, acc_ref,
    even, odd, deep, wide_source,
    high_ref, low_ref, found_ref, back_ref,
    o0, o1, o2, o3, o4, o5, o6, o7, i0, i1, i2, i3, i4, i5, i6, i7,
    q0, q1, q2, q3, q4, q5, q6, q7, g0, g1, g2, g3, g4, g5, g6, g7,
    r0, r1, r2, r3, r4, r5, r6, r7, t0, t1, t2, t3, t4, t5, t6, t7,
    rim_send, rim_recv, first_send, first_recv, tile_send, tile_recv,
    out_sem, in_sem, back_out_sem, back_in_sem, state_sem,
):
    (a, c), (na, nc) = my_place(), sizes()
    count = na * nc
    me = a * nc + c
    rows, cols = mass_ref.shape[0], mass_ref.shape[1]
    ahead = [lax.rem(c + step, nc) for step in range(nc)]
    behind = [lax.rem(c - step + nc, nc) for step in range(nc)]

    def block(n):
        return pl.ds(pl.multiple_of(n * 8, 8), 8)

    def each_other(first, last, act):
        if first == 0:
            for across in range(1, nc):
                act(0, across)

        def along(step, carry):
            for across in range(nc):
                act(step, across)
            return carry

        lax.fori_loop(max(first, 1), last, along, 0)

    barrier = pltpu.get_barrier_semaphore()

    def greet(along, across):
        pl.semaphore_signal(
            barrier,
            inc=1,
            device_id=(lax.rem(a + along, na), ahead[across]),
            device_id_type=MESH,
        )

    each_other(0, na, greet)

    particle = [
        (off_ref, 0), (off_ref, 1), (vel_ref, 0), (vel_ref, 1), (mass_ref, None),
    ]
    tile_outs = [r0, r1, r2, r3, r4, r5, r6, r7]
    tile_ins = [t0, t1, t2, t3, t4, t5, t6, t7]
    stage_particles(particle, rows, cols, tile_outs, pad_ref)
    tile = window_sums(pad_ref, near_ref, dest_ref, sums_ref, rank_ref)
    inner = cols - 2
    half = rows // 2 - 1

    def inner_tiles(base, row0, running):
        def one(n, running):
            return tile(row0 + n // inner, 1 + n % inner, base + n, running)

        return lax.fori_loop(0, half * inner, one, running, unroll=2)

    running = inner_tiles(0, 1, jnp.zeros((128, 128), F32))
    pl.semaphore_wait(barrier, count - 1)
    copies = rim_copies(tile_outs, tile_ins, tile_send, tile_recv)
    for copy in copies:
        copy.start()
    running = inner_tiles(half * inner, 1 + half, running)
    for copy in copies:
        copy.wait()
    place_particles(tile_ins, rows, cols, pad_ref)
    done = 2 * half * inner

    def end_rows(n, running):
        i = (n // cols) * (rows - 1)
        return tile(i, n % cols, done + n, running)

    running = lax.fori_loop(0, 2 * cols, end_rows, running, unroll=4)
    done = done + 2 * cols

    def end_columns(n, running):
        return tile(1 + n // 2, (n % 2) * (cols - 1), done + n, running)

    lax.fori_loop(0, 2 * (rows - 2), end_columns, running, unroll=2)

    for i in range(rows):
        at = slice(i * cols, (i + 1) * cols)
        s0 = sums_ref[0, at, :]
        density = s0 / 128.0
        dens_ref[at, :] = density
        volume = mass_ref[i] / density
        vals_ref[0, at, :] = cell_ref[at, :].astype(F32)
        vals_ref[1, at, :] = volume
        vals_ref[2, at, :] = volume * (sums_ref[1, at, :] / s0)
        vals_ref[3, at, :] = volume * (sums_ref[2, at, :] / s0)
    pack(dest_ref, vals_ref, rank_ref, send_ref, pleft_ref, pslots_ref, pacc_ref)

    per_group = na // GROUPS

    def send_out(group):
        def start(along, across):
            to = (lax.rem(a + along, na), ahead[across])
            pltpu.make_async_remote_copy(
                src_ref=send_ref.at[block(to[0] * nc + to[1]), :],
                dst_ref=got_ref.at[block(along * nc + across), :],
                send_sem=out_sem,
                recv_sem=in_sem.at[group],
                device_id=to,
                device_id_type=MESH,
            ).start()

        each_other(group * per_group, (group + 1) * per_group, start)

    for group in range(GROUPS):
        send_out(group)
    got_ref[0:8, :] = send_ref[block(me), :]

    first_outs = [q0, q1, q2, q3, q4, q5, q6, q7]
    first_ins = [g0, g1, g2, g3, g4, g5, g6, g7]
    write_rims(first_outs, [0, 0, 0, 0, 0], [
        lambda r, c: surface_ref[0, r, c],
        lambda r, c: surface_ref[1, r, c],
        lambda r, c: surface_ref[2, r, c],
        lambda r, c: depth_ref[r, c],
    ])
    copies = rim_copies(first_outs, first_ins, first_send, first_recv)
    for copy in copies:
        copy.start()
    for f in range(3):
        even[f, 0:128, 0:512] = surface_ref[f]
    deep[0, 0:128, 0:512] = depth_ref[...]
    acc_ref[...] = jnp.zeros_like(acc_ref)
    for copy in copies:
        copy.wait()
    for f in range(3):
        place_rims(even, f, f, first_ins, [0, 0, 0])
    place_rims(deep, 0, 3, first_ins, [0, 0, 0])
    for b in range(TALL // 8):
        at = slice(b * 8, b * 8 + 8)
        for f in range(3):
            even[f, at, :] = jnp.where(inside_grid(b), even[f, at, :], 0.0)

    for group in range(GROUPS):
        landed = got_ref.at[max(8, group * PER_GROUP * 8) : (group + 1) * PER_GROUP * 8, :]
        pltpu.make_async_copy(landed, landed, in_sem.at[group]).wait()
        unfold(got_ref, slots_ref, group)
        deposit_group(group, slots_ref, cells_ref, left_ref, right_ref, acc_ref)
    for k in range(3):
        wide_source[k, 0:128, 0:512] = deposit_sum(acc_ref, k)

    outs = [o0, o1, o2, o3, o4, o5, o6, o7]
    ins = [i0, i1, i2, i3, i4, i5, i6, i7]
    write_rims(outs, [0, 0, 0, 0, 0], [
        lambda r, c: wide_source[0, r, c],
        lambda r, c: wide_source[1, r, c],
        lambda r, c: wide_source[2, r, c],
    ])
    copies = rim_copies(outs, ins, rim_send, rim_recv)
    for copy in copies:
        copy.start()
    for copy in copies:
        copy.wait()
    for f in range(3):
        place_rims(wide_source, f, f, ins, [0, 0, 0])

    def two_steps(n, carry):
        water_step(even, odd, deep, wide_source)
        water_step(odd, even, deep, wide_source)
        return carry

    lax.fori_loop(0, SUBSTEPS // 2, two_steps, 0)
    keep = pltpu.make_async_copy(even.at[:, 0:128, 0:512], state_ref, state_sem)
    keep.start()
    undo = [lookup_table(even[k, 0:128, 0:512], k, high_ref, low_ref) for k in range(3)]

    for group in range(GROUPS):
        lookup_group(group, cells_ref, high_ref, low_ref, undo, found_ref, back_ref)

        def start(along, across):
            pltpu.make_async_remote_copy(
                src_ref=back_ref.at[block(along * nc + across), :],
                dst_ref=back_got.at[block(me), :],
                send_sem=back_out_sem,
                recv_sem=back_in_sem,
                device_id=(lax.rem(a - along + na, na), behind[across]),
                device_id_type=MESH,
            ).start()

        each_other(group * per_group, (group + 1) * per_group, start)
    back_got[block(me), :] = back_ref[0:8, :]
    others = (count - 1) * 8
    for ref, sem in (
        (back_got, back_in_sem),
        (send_ref, out_sem),
        (back_ref, back_out_sem),
    ):
        pltpu.make_async_copy(ref.at[0:others, :], ref.at[0:others, :], sem).wait()
    keep.wait()


def main_call(offsets, velocity, mass, near, dest, cell, surface, depth):
    def buffers(heights):
        return [pltpu.VMEM((h, 128), F32) for h in heights + [8, 8, 8, 8]]

    rows, cols = mass.shape[0], mass.shape[1]
    dma = pltpu.SemaphoreType.DMA
    anywhere = pl.BlockSpec(memory_space=pl.ANY)
    return pl.pallas_call(
        main_kernel,
        out_shape=(
            jax.ShapeDtypeStruct((64, 128), F32),
            jax.ShapeDtypeStruct((64, 128), F32),
            jax.ShapeDtypeStruct((3, 128, 512), F32),
            jax.ShapeDtypeStruct((1024, 128), F32),
        ),
        in_specs=[vmem()] * 3 + [pl.BlockSpec(memory_space=pltpu.SMEM)] + [vmem()] * 4,
        out_specs=(vmem(), vmem(), anywhere, vmem()),
        scratch_shapes=[
            pltpu.VMEM((5, rows + 2, cols + 2, 128), F32),
            pltpu.VMEM((3, 64, 128), F32),
            pltpu.VMEM((4, 64, 128), F32),
            pltpu.VMEM((1024, 1024), BF16),
            pltpu.VMEM((192, 1024), BF16),
            pltpu.VMEM((1024, 256), F32),
            pltpu.VMEM((1024, 128), F32),
            pltpu.VMEM((1024, 128), F32),
            pltpu.VMEM((4, 48, 128), F32),
            pltpu.VMEM((192, 128), F32),
            pltpu.VMEM((1152, STEP * 128), F8),
            pltpu.VMEM((512, STEP * 128), F8),
            pltpu.VMEM((1152, 512), F32),
            pltpu.VMEM((3, TALL, BROAD), F32),
            pltpu.VMEM((3, TALL, BROAD), F32),
            pltpu.VMEM((1, TALL, BROAD), F32),
            pltpu.VMEM((3, TALL, BROAD), F32),
            pltpu.VMEM((384, 512), BF16),
            pltpu.VMEM((384, 512), F8),
            pltpu.VMEM((3, 48, 128), F32),
            pltpu.VMEM((1024, 128), F32),
            *buffers([96, 96, 128, 128]),
            *buffers([96, 96, 128, 128]),
            *buffers([128, 128, 128, 128]),
            *buffers([128, 128, 128, 128]),
            *buffers([5 * cols, 5 * cols, SIDE_PARTICLES, SIDE_PARTICLES]),
            *buffers([5 * cols, 5 * cols, SIDE_PARTICLES, SIDE_PARTICLES]),
            dma((8,)),
            dma((8,)),
            dma((8,)),
            dma((8,)),
            dma((8,)),
            dma((8,)),
            dma,
            dma((GROUPS,)),
            dma,
            dma,
            dma,
        ],
        compiler_params=pltpu.CompilerParams(
            vmem_limit_bytes=VMEM_LIMIT, collective_id=1, has_side_effects=True
        ),
        name="main",
    )(offsets, velocity, mass, near, dest, cell, surface, depth)


def shards(
    offsets, velocity, particle_mass, neighbours, owner_device, target_cell, surface, water_depth
):
    dest = owner_device.reshape(64, 128)
    density, rank, water_state, back = main_call(
        offsets,
        velocity,
        particle_mass,
        jnp.transpose(neighbours, (2, 0, 1)),
        dest,
        target_cell.reshape(64, 128),
        surface,
        water_depth,
    )
    feedback, water_state, density = finish_call(back, dest, rank, water_state, density)
    return (
        water_state,
        density.reshape(particle_mass.shape),
        feedback.reshape((3,) + particle_mass.shape),
    )


def solution(mesh):
    in_specs = (
        P(None, "along", "cross", None),
        P(None, "along", "cross", None),
        P("along", "cross", None),
        P("along", "cross", None),
        P("along", "cross", None, None),
        P("along", "cross", None),
        P(None, "along", "cross"),
        P("along", "cross"),
    )
    out_specs = (
        P(None, "along", "cross"),
        P("along", "cross", None),
        P(None, "along", "cross", None),
    )
    return jax.shard_map(shards, mesh=mesh, in_specs=in_specs, out_specs=out_specs, check_vma=False)
```

```python
import math

import jax
import jax.numpy as jnp
from jax import lax
from jax.experimental import pallas as pl
from jax.experimental.pallas import tpu as pltpu
from jax.sharding import PartitionSpec as P

SUBSTEPS = 4
KAPPA = math.sqrt(math.log2(math.e))
F32 = jnp.float32
BF16 = jnp.bfloat16
F8 = jnp.float8_e4m3fn
NN = (((1,), (0,)), ((), ()))
NT = (((1,), (1,)), ((), ()))
VMEM_LIMIT = 56 * 1024 * 1024

courant = 0.4


def dot(a, b, dims):
    return lax.dot_general(a, b, dims, preferred_element_type=F32)


def split2(x):
    hi = x.astype(BF16).astype(F32)
    return hi, x - hi


def split8(x):
    t0 = x.astype(F8).astype(F32)
    r = (x - t0) * 16.0
    t1 = r.astype(F8).astype(F32)
    return t0, t1, (r - t1) * 16.0


def iota(shape, dim):
    return lax.broadcasted_iota(jnp.int32, shape, dim)


def window_sums(pad_ref, near_ref, dest_ref, sums_ref, rank_ref):
    cols = pad_ref.shape[2] - 2
    d_iota = iota((128, 128), 0)
    before = jnp.concatenate(
        [
            (iota((128, 128), 0) < iota((128, 128), 1)).astype(F32),
            jnp.ones((128, 128), F32),
        ],
        1,
    ).astype(BF16)

    q16 = iota((16, 128), 0)
    kind = jnp.where(q16 >= 3, q16 - 3, q16)

    def tile(i, j, row, running):
        hit = d_iota == jnp.broadcast_to(dest_ref[pl.ds(row, 1), :], (128, 128))
        counts = dot(jnp.where(hit, 1.0, 0.0).astype(BF16), before, NN)
        rank_ref[pl.ds(row, 1), :] = jnp.sum(
            jnp.where(hit, counts[:, :128] + running, 0.0), axis=0, keepdims=True
        )
        running = running + counts[:, 128:]
        x = pad_ref[0, i + 1, pl.ds(j + 1, 1), :] * KAPPA
        y = pad_ref[1, i + 1, pl.ds(j + 1, 1), :] * KAPPA
        x_col = jnp.broadcast_to(x, (128, 128)).T
        y_col = jnp.broadcast_to(y, (128, 128)).T
        listed = jnp.int32(0)
        for slot in range(9):
            listed = listed | lax.shift_left(jnp.int32(1), near_ref[slot, i, j] + 1)
        window = []
        for w in range(9):
            bi, bj = i + w // 3, j + w % 3
            bx = (pad_ref[0, bi, pl.ds(bj, 1), :] + (w // 3 - 1.0)) * KAPPA
            by = (pad_ref[1, bi, pl.ds(bj, 1), :] + (w % 3 - 1.0)) * KAPPA
            c0 = pad_ref[4, bi, pl.ds(bj, 1), :] * jnp.exp2(-bx * bx - by * by)
            c0 = c0 * (lax.shift_right_logical(listed, w + 1) & 1).astype(F32)
            vx = pad_ref[2, bi, pl.ds(bj, 1), :]
            vy = pad_ref[3, bi, pl.ds(bj, 1), :]
            c_hi, c_lo = split2(
                jnp.broadcast_to(c0, (16, 128))
                * jnp.where(kind == 0, 1.0, jnp.where(kind == 1, vx, vy))
            )
            carried = jnp.where(q16 < 3, c_hi, jnp.where(q16 < 6, c_lo, 0.0)).astype(BF16)
            window.append((2.0 * bx, 2.0 * by, carried))
        left, right = [], []
        for bx, by, carried in window:
            weights = jnp.exp2(x_col * bx + y_col * by)
            hi = weights.astype(BF16)
            left += [hi, (weights - hi.astype(F32)).astype(BF16)]
            right += [carried, carried]
        total = dot(jnp.concatenate(left, 1), jnp.concatenate(right, 1), NT)
        total = jnp.concatenate([total, jnp.zeros((128, 112), F32)], 1).T
        scale = jnp.exp2(-x * x - y * y)
        for k in range(3):
            sums_ref[k, pl.ds(i * cols + j, 1), :] = (total[k : k + 1] + total[k + 3 : k + 4]) * scale
        return running

    return tile


def pack(dest_ref, vals_ref, rank_ref, send_ref, left_ref, slots_ref, acc_ref):
    groups = dest_ref.shape[0] // 8
    d_iota = iota((128, 128), 0)
    p_iota = iota((192, 128), 0).astype(F32)
    acc_ref[...] = jnp.zeros_like(acc_ref)

    def group(g, carry):
        at = pl.ds(pl.multiple_of(g * 8, 8), 8)
        dest8 = dest_ref[at, :]
        rank8 = rank_ref[at, :]
        vals8 = [split2(vals_ref[k, at, :]) for k in range(4)]
        for r in range(8):
            hit = d_iota == jnp.broadcast_to(dest8[r : r + 1], (128, 128))
            lanes = slice(r * 128, r * 128 + 128)
            slots_ref[:, lanes] = jnp.where(
                p_iota == jnp.broadcast_to(rank8[r : r + 1], (192, 128)), 1.0, 0.0
            ).astype(BF16)
            for part in range(2):
                for k in range(4):
                    v = jnp.broadcast_to(vals8[k][part][r : r + 1], (128, 128))
                    base = (part * 4 + k) * 128
                    left_ref[base : base + 128, lanes] = jnp.where(hit, v, 0.0).astype(BF16)
        acc_ref[:, 0:192] += dot(left_ref[...], slots_ref[...], NT)
        return carry

    lax.fori_loop(0, groups, group, 0)
    tails = []
    for k in range(4):
        send_ref[pl.ds(k, 128, stride=8), :] = acc_ref[k * 128 : k * 128 + 128, 0:128] + acc_ref[
            512 + k * 128 : 640 + k * 128, 0:128
        ]
        tails.append(
            acc_ref[k * 128 : k * 128 + 128, 128:256]
            + acc_ref[512 + k * 128 : 640 + k * 128, 128:256]
        )
    low_half = iota((128, 128), 1) < 64
    for k in range(6, 8):
        send_ref[pl.ds(k, 128, stride=8), :] = jnp.zeros((128, 128), F32)
    for h in range(2):
        send_ref[pl.ds(4 + h, 128, stride=8), :] = jnp.where(
            low_half, tails[2 * h], pltpu.roll(tails[2 * h + 1], 64, 1)
        )


def vmem():
    return pl.BlockSpec(memory_space=pltpu.VMEM)


MESH = pl.DeviceIdType.MESH
AROUND = [(-1, 0), (1, 0), (0, -1), (0, 1), (-1, -1), (-1, 1), (1, -1), (1, 1)]


def my_place():
    return lax.axis_index("along"), lax.axis_index("cross")


def sizes():
    return lax.axis_size("along"), lax.axis_size("cross")


def at_step(step):
    (a, c), (na, nc) = my_place(), sizes()
    return lax.rem(a + step[0] + na, na), lax.rem(c + step[1] + nc, nc)


def rim_copies(out_refs, in_refs, send_sem, recv_sem):
    copies = []
    for n, step in enumerate(AROUND):
        opposite = AROUND.index((-step[0], -step[1]))
        copies.append(
            pltpu.make_async_remote_copy(
                src_ref=out_refs[n],
                dst_ref=in_refs[opposite],
                send_sem=send_sem.at[n],
                recv_sem=recv_sem.at[opposite],
                device_id=at_step(step),
                device_id_type=MESH,
            )
        )
    return copies


DEEP = 4
SIDE_PARTICLES = 24


def column_strip(fields, right):
    lanes = iota((fields[0].shape[0], 128), 1)
    out = jnp.zeros((fields[0].shape[0], 128), F32)
    for f, field in enumerate(fields):
        turn = DEEP * f + (DEEP if right else 0)
        moved = pltpu.roll(field, turn, 1) if turn else field
        out = jnp.where((lanes >= DEEP * f) & (lanes < DEEP * f + DEEP), moved, out)
    return out


def write_rims(out_refs, base, fields):
    top, bottom = slice(0, 8), slice(120, 128)
    for n, rows in ((0, top), (1, bottom)):
        for f, field in enumerate(fields):
            for b in range(4):
                at = base[n] + (f * 4 + b) * 8
                out_refs[n][at : at + 8, :] = field(rows, slice(b * 128, b * 128 + 128))
    for right in range(2):
        lanes = slice(384, 512) if right else slice(0, 128)
        strip = column_strip([field(slice(0, 128), lanes) for field in fields], right == 1)
        at = base[2 + right]
        out_refs[2 + right][at : at + 128, :] = strip
        out_refs[4 + right][base[4] : base[4] + 8, :] = strip[0:8]
        out_refs[6 + right][base[4] : base[4] + 8, :] = strip[120:128]


def stage_particles(particle, rows, cols, outs, pad_ref):
    def tiles(f, i, j):
        ref, part = particle[f]
        return ref[i, j, :] if part is None else ref[part, i, j, :]

    everything = slice(0, cols)
    for f in range(5):
        outs[0][f * cols : (f + 1) * cols, :] = tiles(f, 0, everything)
        outs[1][f * cols : (f + 1) * cols, :] = tiles(f, rows - 1, everything)
        for side, j in ((0, slice(0, 1)), (1, slice(cols - 1, cols))):
            for i in range(rows):
                outs[2 + side][f * rows + i : f * rows + i + 1, :] = tiles(f, i, j)
            outs[4 + side][f : f + 1, :] = tiles(f, 0, j)
            outs[6 + side][f : f + 1, :] = tiles(f, rows - 1, j)
    for side in range(2):
        outs[2 + side][5 * rows : SIDE_PARTICLES, :] = jnp.zeros(
            (SIDE_PARTICLES - 5 * rows, 128), F32
        )
        outs[4 + side][5:8, :] = jnp.zeros((3, 128), F32)
        outs[6 + side][5:8, :] = jnp.zeros((3, 128), F32)
    for f in range(5):
        for i in range(rows):
            pad_ref[f, i + 1, 1 : cols + 1, :] = tiles(f, i, everything)


def place_particles(ins, rows, cols, pad_ref):
    (a, c), (na, nc) = my_place(), sizes()
    inside = [a > 0, a < na - 1, c > 0, c < nc - 1]

    def kept(f, value, *tests):
        if f < 4:
            return value
        for test in tests:
            value = jnp.where(test, value, 0.0)
        return value

    for f in range(5):
        pad_ref[f, 0, 1 : cols + 1, :] = kept(f, ins[0][f * cols : (f + 1) * cols, :], inside[0])
        pad_ref[f, rows + 1, 1 : cols + 1, :] = kept(
            f, ins[1][f * cols : (f + 1) * cols, :], inside[1]
        )
        for side, j in ((0, 0), (1, cols + 1)):
            for i in range(rows):
                pad_ref[f, i + 1, j : j + 1, :] = kept(
                    f, ins[2 + side][f * rows + i : f * rows + i + 1, :], inside[2 + side]
                )
            pad_ref[f, 0, j : j + 1, :] = kept(
                f, ins[4 + side][f : f + 1, :], inside[0], inside[2 + side]
            )
            pad_ref[f, rows + 1, j : j + 1, :] = kept(
                f, ins[6 + side][f : f + 1, :], inside[1], inside[2 + side]
            )


def finish_kernel(
    back_ref, dest_ref, rank_ref, state_in, dens_in, out_ref, state_ref, dens_ref, table_ref
):
    state_ref[...] = state_in[...]
    dens_ref[...] = dens_in[...]
    tail = back_ref[pl.ds(3, 128, stride=8), :]
    tails = [tail, pltpu.roll(tail, 64, 1), back_ref[pl.ds(4, 128, stride=8), :]]
    for k in range(3):
        for part, piece in enumerate(split2(back_ref[pl.ds(k, 128, stride=8), :])):
            table_ref[k * 128 : k * 128 + 128, part * 192 : part * 192 + 128] = piece.astype(BF16)
        for part, piece in enumerate(split2(tails[k])):
            table_ref[
                k * 128 : k * 128 + 128, part * 192 + 128 : part * 192 + 192
            ] = piece[:, 0:64].astype(BF16)
    d_iota = iota((128, 128), 0)
    p_iota = iota((192, 128), 0).astype(F32)

    def step(g, carry):
        at = pl.ds(g * 8, 8)
        dest8 = dest_ref[at, :]
        rank8 = rank_ref[at, :]
        found = [[], [], []]
        for pair in range(4):
            slots = jnp.concatenate(
                [
                    jnp.where(
                        p_iota == jnp.broadcast_to(rank8[r : r + 1], (192, 128)), 1.0, 0.0
                    ).astype(BF16)
                    for r in (2 * pair, 2 * pair + 1)
                ],
                1,
            )
            got = dot(table_ref[...], jnp.concatenate([slots, slots], 0), NN)
            for k in range(3):
                for h in range(2):
                    r = 2 * pair + h
                    hit = d_iota == jnp.broadcast_to(dest8[r : r + 1], (128, 128))
                    part = got[k * 128 : k * 128 + 128, h * 128 : h * 128 + 128]
                    found[k].append(jnp.sum(jnp.where(hit, part, 0.0), axis=0, keepdims=True))
        for k in range(3):
            out_ref[k, at, :] = jnp.concatenate(found[k], 0)
        return carry

    lax.fori_loop(0, dest_ref.shape[0] // 8, step, 0, unroll=4)


def finish_call(back, dest, rank, state, density):
    return pl.pallas_call(
        finish_kernel,
        out_shape=(
            jax.ShapeDtypeStruct((3, 64, 128), F32),
            jax.ShapeDtypeStruct(state.shape, F32),
            jax.ShapeDtypeStruct(density.shape, F32),
        ),
        in_specs=[vmem()] * 5,
        out_specs=(vmem(), vmem(), vmem()),
        scratch_shapes=[pltpu.VMEM((384, 384), BF16)],
        compiler_params=pltpu.CompilerParams(vmem_limit_bytes=VMEM_LIMIT),
        name="finish",
    )(back, dest, rank, state, density)


GROUPS = 4
PER_GROUP = 32
STEP = 16


def row_and_column(cell):
    row = jnp.floor(cell * (1.0 / 512.0))
    return row, cell - row * 512.0


def unfold(got_ref, slots_ref, group):
    low_half = iota((16, 128), 1) < 64
    first_row = group * PER_GROUP * 8
    for k in range(4):
        slots_ref[k, 0:32, :] = got_ref[pl.ds(first_row + k, 32, stride=8), :]
        row = got_ref[pl.ds(first_row + 4 + k // 2, 32, stride=8), :]
        first, second = row[0:16], row[16:32]
        if k % 2 == 0:
            full = jnp.where(low_half, first, pltpu.roll(second, 64, 1))
        else:
            full = jnp.where(low_half, pltpu.roll(first, 64, 1), second)
        slots_ref[k, 32:48, :] = full


def deposit_group(group, slots_ref, cells_ref, left_ref, right_ref, acc_ref):
    r_iota = iota((128, 128), 0).astype(F32)
    c_iota = iota((512, 128), 0).astype(F32)
    cells_ref[pl.ds(pl.multiple_of(group * 48, 8), 48), :] = slots_ref[0]

    def step(g, carry):
        at = pl.ds(pl.multiple_of(g * STEP, STEP), STEP)
        row8, col8 = row_and_column(slots_ref[0, at, :])
        vals8 = [split8(slots_ref[1 + k, at, :] * 0.5) for k in range(3)]
        for r in range(STEP):
            lanes = slice(r * 128, r * 128 + 128)
            hit = r_iota == jnp.broadcast_to(row8[r : r + 1], (128, 128))
            for part in range(3):
                for k in range(3):
                    v = jnp.broadcast_to(vals8[k][part][r : r + 1], (128, 128))
                    base = (part * 3 + k) * 128
                    left_ref[base : base + 128, lanes] = jnp.where(hit, v, 0.0).astype(F8)
            right_ref[:, lanes] = jnp.where(
                c_iota == jnp.broadcast_to(col8[r : r + 1], (512, 128)), 1.0, 0.0
            ).astype(F8)
        acc_ref[...] += dot(left_ref[...], right_ref[...], NT)
        return carry

    lax.fori_loop(0, 48 // STEP, step, 0)


def deposit_sum(acc_ref, k):
    t0, t1, t2 = [
        acc_ref[(part * 3 + k) * 128 : (part * 3 + k) * 128 + 128, :] for part in range(3)
    ]
    return 2.0 * (t0 + (1.0 / 16.0) * t1 + (1.0 / 256.0) * t2)


def lookup_table(state, k, high_ref, low_ref):
    most = jnp.max(jnp.max(jnp.abs(state), axis=0, keepdims=True), axis=1, keepdims=True)
    most = jnp.maximum(most, 1e-30)
    hi, lo = split2(state * (1024.0 / most))
    high_ref[k * 128 : k * 128 + 128, :] = hi.astype(BF16)
    low_ref[k * 128 : k * 128 + 128, :] = (lo * 64.0).astype(F8)
    return most * (1.0 / 1024.0)


def lookup_group(group, cells_ref, high_ref, low_ref, undo, found_ref, back_ref):
    r_iota = iota((128, 128), 0).astype(F32)
    c_iota = iota((512, 128), 0).astype(F32)

    def step(g, carry):
        at = pl.ds(pl.multiple_of(group * 48 + g * 8, 8), 8)
        row8, col8 = row_and_column(cells_ref[at, :])
        found = [[], [], []]
        for pair in range(4):
            high, low = [], []
            for r in (2 * pair, 2 * pair + 1):
                column = c_iota == jnp.broadcast_to(col8[r : r + 1], (512, 128))
                high.append(jnp.where(column, 1.0, 0.0).astype(BF16))
                low.append(jnp.where(column, 1.0 / 64.0, 0.0).astype(F8))
            got = dot(high_ref[...], jnp.concatenate(high, 1), NN) + dot(
                low_ref[...], jnp.concatenate(low, 1), NN
            )
            for k in range(3):
                for h in range(2):
                    r = 2 * pair + h
                    hit = r_iota == jnp.broadcast_to(row8[r : r + 1], (128, 128))
                    part = got[k * 128 : k * 128 + 128, h * 128 : h * 128 + 128]
                    found[k].append(jnp.sum(jnp.where(hit, part, 0.0), axis=0, keepdims=True))
        for k in range(3):
            found_ref[k, pl.ds(pl.multiple_of(g * 8, 8), 8), :] = (
                jnp.concatenate(found[k], 0) * undo[k]
            )
        return carry

    lax.fori_loop(0, 6, step, 0)
    low_half = iota((16, 128), 1) < 64
    first_row = group * PER_GROUP * 8
    tails = [found_ref[k, 32:48, :] for k in range(3)]
    turned = [pltpu.roll(t, 64, 1) for t in tails]
    for k in range(3):
        back_ref[pl.ds(first_row + k, 32, stride=8), :] = found_ref[k, 0:32, :]
    back_ref[pl.ds(first_row + 3, 16, stride=8), :] = jnp.where(low_half, tails[0], turned[1])
    back_ref[pl.ds(first_row + 131, 16, stride=8), :] = jnp.where(low_half, turned[0], tails[1])
    back_ref[pl.ds(first_row + 4, 16, stride=8), :] = tails[2]
    back_ref[pl.ds(first_row + 132, 16, stride=8), :] = turned[2]
    for k in range(5, 8):
        back_ref[pl.ds(first_row + k, 32, stride=8), :] = jnp.zeros((32, 128), F32)


TALL = 136
BROAD = 640


def place_rims(wide_ref, index, f, refs, bases):
    up, down, left, right, *corners = refs
    upper_half = iota((8, 128), 0) < 4
    for b in range(4):
        at = bases[0] + (f * 4 + b) * 8
        wide_ref[index, 128:136, b * 128 : b * 128 + 128] = jnp.where(
            upper_half, down[at : at + 8, :], up[at : at + 8, :]
        )
    to_left = (128 - DEEP - DEEP * f) % 128
    to_right = (128 - DEEP * f) % 128

    def strip(left_part, right_part):
        moved_left = pltpu.roll(left_part, to_left, 1) if to_left else left_part
        moved_right = pltpu.roll(right_part, to_right, 1) if to_right else right_part
        return jnp.where(iota(left_part.shape, 1) < 64, moved_right, moved_left)

    sides = slice(bases[1], bases[1] + 128)
    wide_ref[index, 0:128, 512:640] = strip(left[sides, :], right[sides, :])
    rows = slice(bases[2], bases[2] + 8)
    c = [
        jnp.where(upper_half, corners[2 + side][rows, :], corners[side][rows, :])
        for side in range(2)
    ]
    wide_ref[index, 128:136, 512:640] = strip(c[0], c[1])


def inside_grid(block):
    (a, c), (na, nc) = my_place(), sizes()
    cols = iota((8, BROAD), 1)
    cols = jnp.where(cols < 576, cols, cols - BROAD) + c * 512
    rows = iota((8, BROAD), 0) + block * 8
    rows = jnp.where(rows < 132, rows, rows - TALL) + a * 128
    return (cols >= 0) & (cols < nc * 512) & (rows >= 0) & (rows < na * 128)


def water_step(old_ref, new_ref, depth_ref, source_ref=None):
    blocks = TALL // 8
    sub = iota((8, BROAD), 0)

    def load(block):
        at = slice(block * 8, block * 8 + 8)
        h, u, v = [old_ref[f, at, :] for f in range(3)]
        fu = depth_ref[0, at, :] * u
        fields = (h, u, v, fu)
        return fields, [pltpu.roll(x, 1, 0) for x in fields], [pltpu.roll(x, 7, 0) for x in fields]

    def left(x):
        return pltpu.roll(x, 1, 1)

    def right(x):
        return pltpu.roll(x, BROAD - 1, 1)

    before, here = load(blocks - 1), load(0)
    for block in range(blocks):
        after = load((block + 1) % blocks)
        at = slice(block * 8, block * 8 + 8)
        (h, u, v, _), down, up = here
        h_w, u_w, v_w, fu_w = [jnp.where(sub == 0, p, q) for p, q in zip(before[1], down)]
        h_e, u_e, v_e, fu_e = [jnp.where(sub == 7, p, q) for p, q in zip(after[2], up)]
        fv = depth_ref[0, at, :] * v
        h_s, h_n = left(h), right(h)
        next_h = 0.25 * (h_e + h_w + h_n + h_s) - 0.5 * courant * (
            fu_e - fu_w + right(fv) - left(fv)
        )
        next_u = 0.25 * (u_e + u_w + right(u) + left(u)) - 0.5 * courant * (h_e - h_w)
        next_v = 0.25 * (v_e + v_w + right(v) + left(v)) - 0.5 * courant * (h_n - h_s)
        inside = inside_grid(block)
        for f, value in enumerate((next_h, next_u, next_v)):
            if source_ref is not None:
                value = value + source_ref[f, at, :]
            new_ref[f, at, :] = jnp.where(inside, value, 0.0)
        before, here = here, after


def main_kernel(
    off_ref, vel_ref, mass_ref, near_ref, dest_ref, cell_ref, surface_ref, depth_ref,
    dens_ref, rank_ref, state_ref, back_got,
    pad_ref,
    sums_ref, vals_ref, pleft_ref, pslots_ref, pacc_ref, send_ref, got_ref,
    slots_ref, cells_ref, left_ref, right_ref, acc_ref,
    even, odd, deep, wide_source,
    high_ref, low_ref, found_ref, back_ref,
    o0, o1, o2, o3, o4, o5, o6, o7, i0, i1, i2, i3, i4, i5, i6, i7,
    q0, q1, q2, q3, q4, q5, q6, q7, g0, g1, g2, g3, g4, g5, g6, g7,
    r0, r1, r2, r3, r4, r5, r6, r7, t0, t1, t2, t3, t4, t5, t6, t7,
    rim_send, rim_recv, first_send, first_recv, tile_send, tile_recv,
    out_sem, in_sem, back_out_sem, back_in_sem, state_sem,
):
    (a, c), (na, nc) = my_place(), sizes()
    count = na * nc
    me = a * nc + c
    rows, cols = mass_ref.shape[0], mass_ref.shape[1]
    ahead = [lax.rem(c + step, nc) for step in range(nc)]
    behind = [lax.rem(c - step + nc, nc) for step in range(nc)]

    def block(n):
        return pl.ds(pl.multiple_of(n * 8, 8), 8)

    def each_other(first, last, act):
        if first == 0:
            for across in range(1, nc):
                act(0, across)

        def along(step, carry):
            for across in range(nc):
                act(step, across)
            return carry

        lax.fori_loop(max(first, 1), last, along, 0)

    barrier = pltpu.get_barrier_semaphore()

    def greet(along, across):
        pl.semaphore_signal(
            barrier,
            inc=1,
            device_id=(lax.rem(a + along, na), ahead[across]),
            device_id_type=MESH,
        )

    each_other(0, na, greet)

    particle = [
        (off_ref, 0), (off_ref, 1), (vel_ref, 0), (vel_ref, 1), (mass_ref, None),
    ]
    tile_outs = [r0, r1, r2, r3, r4, r5, r6, r7]
    tile_ins = [t0, t1, t2, t3, t4, t5, t6, t7]
    stage_particles(particle, rows, cols, tile_outs, pad_ref)
    tile = window_sums(pad_ref, near_ref, dest_ref, sums_ref, rank_ref)
    inner = cols - 2
    half = rows // 2 - 1

    def inner_tiles(base, row0, running):
        def one(n, running):
            return tile(row0 + n // inner, 1 + n % inner, base + n, running)

        return lax.fori_loop(0, half * inner, one, running, unroll=7)

    running = inner_tiles(0, 1, jnp.zeros((128, 128), F32))
    pl.semaphore_wait(barrier, count - 1)
    copies = rim_copies(tile_outs, tile_ins, tile_send, tile_recv)
    for copy in copies:
        copy.start()
    running = inner_tiles(half * inner, 1 + half, running)
    for copy in copies:
        copy.wait()
    place_particles(tile_ins, rows, cols, pad_ref)
    done = 2 * half * inner

    ends = 2 * cols

    def outer_tiles(n, running):
        late = n // ends
        i = (1 - late) * (n // cols) * (rows - 1) + late * (1 + (n - ends) // 2)
        j = (1 - late) * (n % cols) + late * (n % 2) * (cols - 1)
        return tile(i, j, done + n, running)

    lax.fori_loop(0, ends + 2 * (rows - 2), outer_tiles, running, unroll=6)

    for i in range(rows):
        at = slice(i * cols, (i + 1) * cols)
        s0 = sums_ref[0, at, :]
        density = s0 / 128.0
        dens_ref[at, :] = density
        volume = mass_ref[i] / density
        vals_ref[0, at, :] = cell_ref[at, :].astype(F32)
        vals_ref[1, at, :] = volume
        vals_ref[2, at, :] = volume * (sums_ref[1, at, :] / s0)
        vals_ref[3, at, :] = volume * (sums_ref[2, at, :] / s0)
    pack(dest_ref, vals_ref, rank_ref, send_ref, pleft_ref, pslots_ref, pacc_ref)

    per_group = na // GROUPS

    def send_out(group):
        def start(along, across):
            to = (lax.rem(a + along, na), ahead[across])
            pltpu.make_async_remote_copy(
                src_ref=send_ref.at[block(to[0] * nc + to[1]), :],
                dst_ref=got_ref.at[block(along * nc + across), :],
                send_sem=out_sem,
                recv_sem=in_sem.at[group],
                device_id=to,
                device_id_type=MESH,
            ).start()

        each_other(group * per_group, (group + 1) * per_group, start)

    for group in range(GROUPS):
        send_out(group)
    got_ref[0:8, :] = send_ref[block(me), :]

    first_outs = [q0, q1, q2, q3, q4, q5, q6, q7]
    first_ins = [g0, g1, g2, g3, g4, g5, g6, g7]
    write_rims(first_outs, [0, 0, 0, 0, 0], [
        lambda r, c: surface_ref[0, r, c],
        lambda r, c: surface_ref[1, r, c],
        lambda r, c: surface_ref[2, r, c],
        lambda r, c: depth_ref[r, c],
    ])
    copies = rim_copies(first_outs, first_ins, first_send, first_recv)
    for copy in copies:
        copy.start()
    for f in range(3):
        even[f, 0:128, 0:512] = surface_ref[f]
    deep[0, 0:128, 0:512] = depth_ref[...]
    acc_ref[...] = jnp.zeros_like(acc_ref)
    for copy in copies:
        copy.wait()
    for f in range(3):
        place_rims(even, f, f, first_ins, [0, 0, 0])
    place_rims(deep, 0, 3, first_ins, [0, 0, 0])
    for b in range(TALL // 8):
        at = slice(b * 8, b * 8 + 8)
        for f in range(3):
            even[f, at, :] = jnp.where(inside_grid(b), even[f, at, :], 0.0)

    water_step(even, odd, deep)
    for group in range(GROUPS):
        landed = got_ref.at[max(8, group * PER_GROUP * 8) : (group + 1) * PER_GROUP * 8, :]
        pltpu.make_async_copy(landed, landed, in_sem.at[group]).wait()
        unfold(got_ref, slots_ref, group)
        deposit_group(group, slots_ref, cells_ref, left_ref, right_ref, acc_ref)
    for k in range(3):
        wide_source[k, 0:128, 0:512] = deposit_sum(acc_ref, k)

    outs = [o0, o1, o2, o3, o4, o5, o6, o7]
    ins = [i0, i1, i2, i3, i4, i5, i6, i7]
    write_rims(outs, [0, 0, 0, 0, 0], [
        lambda r, c: wide_source[0, r, c],
        lambda r, c: wide_source[1, r, c],
        lambda r, c: wide_source[2, r, c],
    ])
    copies = rim_copies(outs, ins, rim_send, rim_recv)
    for copy in copies:
        copy.start()
    for copy in copies:
        copy.wait()
    for f in range(3):
        place_rims(wide_source, f, f, ins, [0, 0, 0])

    for b in range(TALL // 8):
        at = slice(b * 8, b * 8 + 8)
        for f in range(3):
            odd[f, at, :] = jnp.where(inside_grid(b), odd[f, at, :] + wide_source[f, at, :], 0.0)
    water_step(odd, even, deep, wide_source)
    for _ in range(SUBSTEPS // 2 - 1):
        water_step(even, odd, deep, wide_source)
        water_step(odd, even, deep, wide_source)
    keep = pltpu.make_async_copy(even.at[:, 0:128, 0:512], state_ref, state_sem)
    keep.start()
    undo = [lookup_table(even[k, 0:128, 0:512], k, high_ref, low_ref) for k in range(3)]

    for group in range(GROUPS):
        lookup_group(group, cells_ref, high_ref, low_ref, undo, found_ref, back_ref)

        def start(along, across):
            pltpu.make_async_remote_copy(
                src_ref=back_ref.at[block(along * nc + across), :],
                dst_ref=back_got.at[block(me), :],
                send_sem=back_out_sem,
                recv_sem=back_in_sem,
                device_id=(lax.rem(a - along + na, na), behind[across]),
                device_id_type=MESH,
            ).start()

        each_other(group * per_group, (group + 1) * per_group, start)
    back_got[block(me), :] = back_ref[0:8, :]
    others = (count - 1) * 8
    for ref, sem in (
        (back_got, back_in_sem),
        (send_ref, out_sem),
        (back_ref, back_out_sem),
    ):
        pltpu.make_async_copy(ref.at[0:others, :], ref.at[0:others, :], sem).wait()
    keep.wait()


def main_call(offsets, velocity, mass, near, dest, cell, surface, depth):
    def buffers(heights):
        return [pltpu.VMEM((h, 128), F32) for h in heights + [8, 8, 8, 8]]

    rows, cols = mass.shape[0], mass.shape[1]
    dma = pltpu.SemaphoreType.DMA
    anywhere = pl.BlockSpec(memory_space=pl.ANY)
    return pl.pallas_call(
        main_kernel,
        out_shape=(
            jax.ShapeDtypeStruct((64, 128), F32),
            jax.ShapeDtypeStruct((64, 128), F32),
            jax.ShapeDtypeStruct((3, 128, 512), F32),
            jax.ShapeDtypeStruct((1024, 128), F32),
        ),
        in_specs=[vmem()] * 3 + [pl.BlockSpec(memory_space=pltpu.SMEM)] + [vmem()] * 4,
        out_specs=(vmem(), vmem(), anywhere, vmem()),
        scratch_shapes=[
            pltpu.VMEM((5, rows + 2, cols + 2, 128), F32),
            pltpu.VMEM((3, 64, 128), F32),
            pltpu.VMEM((4, 64, 128), F32),
            pltpu.VMEM((1024, 1024), BF16),
            pltpu.VMEM((192, 1024), BF16),
            pltpu.VMEM((1024, 256), F32),
            pltpu.VMEM((1024, 128), F32),
            pltpu.VMEM((1024, 128), F32),
            pltpu.VMEM((4, 48, 128), F32),
            pltpu.VMEM((192, 128), F32),
            pltpu.VMEM((1152, STEP * 128), F8),
            pltpu.VMEM((512, STEP * 128), F8),
            pltpu.VMEM((1152, 512), F32),
            pltpu.VMEM((3, TALL, BROAD), F32),
            pltpu.VMEM((3, TALL, BROAD), F32),
            pltpu.VMEM((1, TALL, BROAD), F32),
            pltpu.VMEM((3, TALL, BROAD), F32),
            pltpu.VMEM((384, 512), BF16),
            pltpu.VMEM((384, 512), F8),
            pltpu.VMEM((3, 48, 128), F32),
            pltpu.VMEM((1024, 128), F32),
            *buffers([96, 96, 128, 128]),
            *buffers([96, 96, 128, 128]),
            *buffers([128, 128, 128, 128]),
            *buffers([128, 128, 128, 128]),
            *buffers([5 * cols, 5 * cols, SIDE_PARTICLES, SIDE_PARTICLES]),
            *buffers([5 * cols, 5 * cols, SIDE_PARTICLES, SIDE_PARTICLES]),
            dma((8,)),
            dma((8,)),
            dma((8,)),
            dma((8,)),
            dma((8,)),
            dma((8,)),
            dma,
            dma((GROUPS,)),
            dma,
            dma,
            dma,
        ],
        compiler_params=pltpu.CompilerParams(
            vmem_limit_bytes=VMEM_LIMIT, collective_id=1, has_side_effects=True
        ),
        name="main",
    )(offsets, velocity, mass, near, dest, cell, surface, depth)


def shards(
    offsets, velocity, particle_mass, neighbours, owner_device, target_cell, surface, water_depth
):
    dest = owner_device.reshape(64, 128)
    density, rank, water_state, back = main_call(
        offsets,
        velocity,
        particle_mass,
        jnp.transpose(neighbours, (2, 0, 1)),
        dest,
        target_cell.reshape(64, 128),
        surface,
        water_depth,
    )
    feedback, water_state, density = finish_call(back, dest, rank, water_state, density)
    return (
        water_state,
        density.reshape(particle_mass.shape),
        feedback.reshape((3,) + particle_mass.shape),
    )


def solution(mesh):
    in_specs = (
        P(None, "along", "cross", None),
        P(None, "along", "cross", None),
        P("along", "cross", None),
        P("along", "cross", None),
        P("along", "cross", None, None),
        P("along", "cross", None),
        P(None, "along", "cross"),
        P("along", "cross"),
    )
    out_specs = (
        P(None, "along", "cross"),
        P("along", "cross", None),
        P(None, "along", "cross", None),
    )
    return jax.shard_map(shards, mesh=mesh, in_specs=in_specs, out_specs=out_specs, check_vma=False)
```

```python
import math

import jax
import jax.numpy as jnp
from jax import lax
from jax.experimental import pallas as pl
from jax.experimental.pallas import tpu as pltpu
from jax.sharding import PartitionSpec as P

SUBSTEPS = 4
KAPPA = math.sqrt(math.log2(math.e))
F32 = jnp.float32
BF16 = jnp.bfloat16
F8 = jnp.float8_e4m3fn
NN = (((1,), (0,)), ((), ()))
NT = (((1,), (1,)), ((), ()))
VMEM_LIMIT = 56 * 1024 * 1024

courant = 0.4


def dot(a, b, dims):
    return lax.dot_general(a, b, dims, preferred_element_type=F32)


def split2(x):
    hi = x.astype(BF16).astype(F32)
    return hi, x - hi


def split8(x):
    t0 = x.astype(F8).astype(F32)
    r = (x - t0) * 16.0
    t1 = r.astype(F8).astype(F32)
    return t0, t1, (r - t1) * 16.0


def iota(shape, dim):
    return lax.broadcasted_iota(jnp.int32, shape, dim)


def window_sums(pad_ref, near_ref, dest_ref, sums_ref, rank_ref):
    cols = pad_ref.shape[2] - 2
    d_iota = iota((128, 128), 0)
    before = jnp.concatenate(
        [
            (iota((128, 128), 0) < iota((128, 128), 1)).astype(F32),
            jnp.ones((128, 128), F32),
        ],
        1,
    ).astype(BF16)

    q16 = iota((16, 128), 0)
    kind = jnp.where(q16 >= 3, q16 - 3, q16)

    def tile(i, j, row, running):
        hit = d_iota == jnp.broadcast_to(dest_ref[pl.ds(row, 1), :], (128, 128))
        counts = dot(jnp.where(hit, 1.0, 0.0).astype(BF16), before, NN)
        rank_ref[pl.ds(row, 1), :] = jnp.sum(
            jnp.where(hit, counts[:, :128] + running, 0.0), axis=0, keepdims=True
        )
        running = running + counts[:, 128:]
        x = pad_ref[0, i + 1, pl.ds(j + 1, 1), :] * KAPPA
        y = pad_ref[1, i + 1, pl.ds(j + 1, 1), :] * KAPPA
        x_col = jnp.broadcast_to(x, (128, 128)).T
        y_col = jnp.broadcast_to(y, (128, 128)).T
        listed = jnp.int32(0)
        for slot in range(9):
            listed = listed | lax.shift_left(jnp.int32(1), near_ref[slot, i, j] + 1)
        window = []
        for w in range(9):
            bi, bj = i + w // 3, j + w % 3
            bx = (pad_ref[0, bi, pl.ds(bj, 1), :] + (w // 3 - 1.0)) * KAPPA
            by = (pad_ref[1, bi, pl.ds(bj, 1), :] + (w % 3 - 1.0)) * KAPPA
            c0 = pad_ref[4, bi, pl.ds(bj, 1), :] * jnp.exp2(-bx * bx - by * by)
            c0 = c0 * (lax.shift_right_logical(listed, w + 1) & 1).astype(F32)
            vx = pad_ref[2, bi, pl.ds(bj, 1), :]
            vy = pad_ref[3, bi, pl.ds(bj, 1), :]
            c_hi, c_lo = split2(
                jnp.broadcast_to(c0, (16, 128))
                * jnp.where(kind == 0, 1.0, jnp.where(kind == 1, vx, vy))
            )
            carried = jnp.where(q16 < 3, c_hi, jnp.where(q16 < 6, c_lo, 0.0)).astype(BF16)
            window.append((2.0 * bx, 2.0 * by, carried))
        left, right = [], []
        for bx, by, carried in window:
            weights = jnp.exp2(x_col * bx + y_col * by)
            hi = weights.astype(BF16)
            left += [hi, (weights - hi.astype(F32)).astype(BF16)]
            right += [carried, carried]
        total = dot(jnp.concatenate(left, 1), jnp.concatenate(right, 1), NT)
        total = jnp.concatenate([total, jnp.zeros((128, 112), F32)], 1).T
        scale = jnp.exp2(-x * x - y * y)
        for k in range(3):
            sums_ref[k, pl.ds(i * cols + j, 1), :] = (total[k : k + 1] + total[k + 3 : k + 4]) * scale
        return running

    return tile


def pack(dest_ref, vals_ref, rank_ref, send_ref, left_ref, slots_ref, acc_ref):
    groups = dest_ref.shape[0] // 8
    d_iota = iota((128, 128), 0)
    p_iota = iota((192, 128), 0).astype(F32)
    acc_ref[...] = jnp.zeros_like(acc_ref)

    def group(g, carry):
        at = pl.ds(pl.multiple_of(g * 8, 8), 8)
        dest8 = dest_ref[at, :]
        rank8 = rank_ref[at, :]
        vals8 = [split2(vals_ref[k, at, :]) for k in range(4)]
        for r in range(8):
            hit = d_iota == jnp.broadcast_to(dest8[r : r + 1], (128, 128))
            lanes = slice(r * 128, r * 128 + 128)
            slots_ref[:, lanes] = jnp.where(
                p_iota == jnp.broadcast_to(rank8[r : r + 1], (192, 128)), 1.0, 0.0
            ).astype(BF16)
            for part in range(2):
                for k in range(4):
                    v = jnp.broadcast_to(vals8[k][part][r : r + 1], (128, 128))
                    base = (part * 4 + k) * 128
                    left_ref[base : base + 128, lanes] = jnp.where(hit, v, 0.0).astype(BF16)
        acc_ref[:, 0:192] += dot(left_ref[...], slots_ref[...], NT)
        return carry

    lax.fori_loop(0, groups, group, 0)
    tails = []
    for k in range(4):
        send_ref[pl.ds(k, 128, stride=8), :] = acc_ref[k * 128 : k * 128 + 128, 0:128] + acc_ref[
            512 + k * 128 : 640 + k * 128, 0:128
        ]
        tails.append(
            acc_ref[k * 128 : k * 128 + 128, 128:256]
            + acc_ref[512 + k * 128 : 640 + k * 128, 128:256]
        )
    low_half = iota((128, 128), 1) < 64
    for k in range(6, 8):
        send_ref[pl.ds(k, 128, stride=8), :] = jnp.zeros((128, 128), F32)
    for h in range(2):
        send_ref[pl.ds(4 + h, 128, stride=8), :] = jnp.where(
            low_half, tails[2 * h], pltpu.roll(tails[2 * h + 1], 64, 1)
        )


def vmem():
    return pl.BlockSpec(memory_space=pltpu.VMEM)


MESH = pl.DeviceIdType.MESH
AROUND = [(-1, 0), (1, 0), (0, -1), (0, 1), (-1, -1), (-1, 1), (1, -1), (1, 1)]


def my_place():
    return lax.axis_index("along"), lax.axis_index("cross")


def sizes():
    return lax.axis_size("along"), lax.axis_size("cross")


def at_step(step):
    (a, c), (na, nc) = my_place(), sizes()
    return lax.rem(a + step[0] + na, na), lax.rem(c + step[1] + nc, nc)


def rim_copies(out_refs, in_refs, send_sem, recv_sem):
    copies = []
    for n, step in enumerate(AROUND):
        opposite = AROUND.index((-step[0], -step[1]))
        copies.append(
            pltpu.make_async_remote_copy(
                src_ref=out_refs[n],
                dst_ref=in_refs[opposite],
                send_sem=send_sem.at[n],
                recv_sem=recv_sem.at[opposite],
                device_id=at_step(step),
                device_id_type=MESH,
            )
        )
    return copies


DEEP = 4
SIDE_PARTICLES = 24


def column_strip(fields, right):
    lanes = iota((fields[0].shape[0], 128), 1)
    out = jnp.zeros((fields[0].shape[0], 128), F32)
    for f, field in enumerate(fields):
        turn = DEEP * f + (DEEP if right else 0)
        moved = pltpu.roll(field, turn, 1) if turn else field
        out = jnp.where((lanes >= DEEP * f) & (lanes < DEEP * f + DEEP), moved, out)
    return out


def write_rims(out_refs, base, fields):
    top, bottom = slice(0, 8), slice(120, 128)
    for n, rows in ((0, top), (1, bottom)):
        for f, field in enumerate(fields):
            for b in range(4):
                at = base[n] + (f * 4 + b) * 8
                out_refs[n][at : at + 8, :] = field(rows, slice(b * 128, b * 128 + 128))
    for right in range(2):
        lanes = slice(384, 512) if right else slice(0, 128)
        strip = column_strip([field(slice(0, 128), lanes) for field in fields], right == 1)
        at = base[2 + right]
        out_refs[2 + right][at : at + 128, :] = strip
        out_refs[4 + right][base[4] : base[4] + 8, :] = strip[0:8]
        out_refs[6 + right][base[4] : base[4] + 8, :] = strip[120:128]


def stage_particles(particle, rows, cols, outs, pad_ref):
    def tiles(f, i, j):
        ref, part = particle[f]
        return ref[i, j, :] if part is None else ref[part, i, j, :]

    everything = slice(0, cols)
    for f in range(5):
        outs[0][f * cols : (f + 1) * cols, :] = tiles(f, 0, everything)
        outs[1][f * cols : (f + 1) * cols, :] = tiles(f, rows - 1, everything)
        for side, j in ((0, slice(0, 1)), (1, slice(cols - 1, cols))):
            for i in range(rows):
                outs[2 + side][f * rows + i : f * rows + i + 1, :] = tiles(f, i, j)
            outs[4 + side][f : f + 1, :] = tiles(f, 0, j)
            outs[6 + side][f : f + 1, :] = tiles(f, rows - 1, j)
    for side in range(2):
        outs[2 + side][5 * rows : SIDE_PARTICLES, :] = jnp.zeros(
            (SIDE_PARTICLES - 5 * rows, 128), F32
        )
        outs[4 + side][5:8, :] = jnp.zeros((3, 128), F32)
        outs[6 + side][5:8, :] = jnp.zeros((3, 128), F32)
    for f in range(5):
        for i in range(rows):
            pad_ref[f, i + 1, 1 : cols + 1, :] = tiles(f, i, everything)


def place_particles(ins, rows, cols, pad_ref):
    (a, c), (na, nc) = my_place(), sizes()
    inside = [a > 0, a < na - 1, c > 0, c < nc - 1]

    def kept(f, value, *tests):
        if f < 4:
            return value
        for test in tests:
            value = jnp.where(test, value, 0.0)
        return value

    for f in range(5):
        pad_ref[f, 0, 1 : cols + 1, :] = kept(f, ins[0][f * cols : (f + 1) * cols, :], inside[0])
        pad_ref[f, rows + 1, 1 : cols + 1, :] = kept(
            f, ins[1][f * cols : (f + 1) * cols, :], inside[1]
        )
        for side, j in ((0, 0), (1, cols + 1)):
            for i in range(rows):
                pad_ref[f, i + 1, j : j + 1, :] = kept(
                    f, ins[2 + side][f * rows + i : f * rows + i + 1, :], inside[2 + side]
                )
            pad_ref[f, 0, j : j + 1, :] = kept(
                f, ins[4 + side][f : f + 1, :], inside[0], inside[2 + side]
            )
            pad_ref[f, rows + 1, j : j + 1, :] = kept(
                f, ins[6 + side][f : f + 1, :], inside[1], inside[2 + side]
            )


def finish_kernel(
    back_ref, dest_ref, rank_ref, state_in, dens_in, out_ref, state_ref, dens_ref, table_ref
):
    state_ref[...] = state_in[...]
    dens_ref[...] = dens_in[...]
    tail = back_ref[pl.ds(3, 128, stride=8), :]
    tails = [tail, pltpu.roll(tail, 64, 1), back_ref[pl.ds(4, 128, stride=8), :]]
    for k in range(3):
        for part, piece in enumerate(split2(back_ref[pl.ds(k, 128, stride=8), :])):
            table_ref[k * 128 : k * 128 + 128, part * 192 : part * 192 + 128] = piece.astype(BF16)
        for part, piece in enumerate(split2(tails[k])):
            table_ref[
                k * 128 : k * 128 + 128, part * 192 + 128 : part * 192 + 192
            ] = piece[:, 0:64].astype(BF16)
    d_iota = iota((128, 128), 0)
    p_iota = iota((192, 128), 0).astype(F32)

    def step(g, carry):
        at = pl.ds(g * 8, 8)
        dest8 = dest_ref[at, :]
        rank8 = rank_ref[at, :]
        found = [[], [], []]
        for pair in range(4):
            slots = jnp.concatenate(
                [
                    jnp.where(
                        p_iota == jnp.broadcast_to(rank8[r : r + 1], (192, 128)), 1.0, 0.0
                    ).astype(BF16)
                    for r in (2 * pair, 2 * pair + 1)
                ],
                1,
            )
            got = dot(table_ref[...], jnp.concatenate([slots, slots], 0), NN)
            for k in range(3):
                for h in range(2):
                    r = 2 * pair + h
                    hit = d_iota == jnp.broadcast_to(dest8[r : r + 1], (128, 128))
                    part = got[k * 128 : k * 128 + 128, h * 128 : h * 128 + 128]
                    found[k].append(jnp.sum(jnp.where(hit, part, 0.0), axis=0, keepdims=True))
        for k in range(3):
            out_ref[k, at, :] = jnp.concatenate(found[k], 0)
        return carry

    lax.fori_loop(0, dest_ref.shape[0] // 8, step, 0, unroll=4)


def finish_call(back, dest, rank, state, density):
    return pl.pallas_call(
        finish_kernel,
        out_shape=(
            jax.ShapeDtypeStruct((3, 64, 128), F32),
            jax.ShapeDtypeStruct(state.shape, F32),
            jax.ShapeDtypeStruct(density.shape, F32),
        ),
        in_specs=[vmem()] * 5,
        out_specs=(vmem(), vmem(), vmem()),
        scratch_shapes=[pltpu.VMEM((384, 384), BF16)],
        compiler_params=pltpu.CompilerParams(vmem_limit_bytes=VMEM_LIMIT),
        name="finish",
    )(back, dest, rank, state, density)


GROUPS = 4
PER_GROUP = 32
STEP = 16


def row_and_column(cell):
    row = jnp.floor(cell * (1.0 / 512.0))
    return row, cell - row * 512.0


def unfold(got_ref, slots_ref, group):
    low_half = iota((16, 128), 1) < 64
    first_row = group * PER_GROUP * 8
    for k in range(4):
        slots_ref[k, 0:32, :] = got_ref[pl.ds(first_row + k, 32, stride=8), :]
        row = got_ref[pl.ds(first_row + 4 + k // 2, 32, stride=8), :]
        first, second = row[0:16], row[16:32]
        if k % 2 == 0:
            full = jnp.where(low_half, first, pltpu.roll(second, 64, 1))
        else:
            full = jnp.where(low_half, pltpu.roll(first, 64, 1), second)
        slots_ref[k, 32:48, :] = full


def deposit_group(group, slots_ref, cells_ref, left_refs, right_refs, acc_ref):
    r_iota = iota((128, 128), 0).astype(F32)
    c_iota = iota((512, 128), 0).astype(F32)
    cells_ref[pl.ds(pl.multiple_of(group * 48, 8), 48), :] = slots_ref[0]
    for g in range(48 // STEP):
        left_ref, right_ref = left_refs[g % 2], right_refs[g % 2]
        at = slice(g * STEP, g * STEP + STEP)
        row8, col8 = row_and_column(slots_ref[0, at, :])
        vals8 = [split8(slots_ref[1 + k, at, :] * 0.5) for k in range(3)]
        for r in range(STEP):
            lanes = slice(r * 128, r * 128 + 128)
            hit = r_iota == jnp.broadcast_to(row8[r : r + 1], (128, 128))
            for part in range(3):
                for k in range(3):
                    v = jnp.broadcast_to(vals8[k][part][r : r + 1], (128, 128))
                    base = (part * 3 + k) * 128
                    left_ref[base : base + 128, lanes] = jnp.where(hit, v, 0.0).astype(F8)
            right_ref[:, lanes] = jnp.where(
                c_iota == jnp.broadcast_to(col8[r : r + 1], (512, 128)), 1.0, 0.0
            ).astype(F8)
        acc_ref[...] += dot(left_ref[...], right_ref[...], NT)


def deposit_sum(acc_ref, k):
    t0, t1, t2 = [
        acc_ref[(part * 3 + k) * 128 : (part * 3 + k) * 128 + 128, :] for part in range(3)
    ]
    return 2.0 * (t0 + (1.0 / 16.0) * t1 + (1.0 / 256.0) * t2)


def lookup_table(state, k, high_ref, low_ref):
    most = jnp.max(jnp.max(jnp.abs(state), axis=0, keepdims=True), axis=1, keepdims=True)
    most = jnp.maximum(most, 1e-30)
    hi, lo = split2(state * (1024.0 / most))
    high_ref[k * 128 : k * 128 + 128, :] = hi.astype(BF16)
    low_ref[k * 128 : k * 128 + 128, :] = (lo * 64.0).astype(F8)
    return most * (1.0 / 1024.0)


def lookup_group(group, cells_ref, high_ref, low_ref, undo, found_ref, back_ref):
    r_iota = iota((128, 128), 0).astype(F32)
    c_iota = iota((512, 128), 0).astype(F32)

    def step(g, carry):
        at = pl.ds(pl.multiple_of(group * 48 + g * 8, 8), 8)
        row8, col8 = row_and_column(cells_ref[at, :])
        found = [[], [], []]
        for pair in range(4):
            high, low = [], []
            for r in (2 * pair, 2 * pair + 1):
                column = c_iota == jnp.broadcast_to(col8[r : r + 1], (512, 128))
                high.append(jnp.where(column, 1.0, 0.0).astype(BF16))
                low.append(jnp.where(column, 1.0 / 64.0, 0.0).astype(F8))
            got = dot(high_ref[...], jnp.concatenate(high, 1), NN) + dot(
                low_ref[...], jnp.concatenate(low, 1), NN
            )
            for k in range(3):
                for h in range(2):
                    r = 2 * pair + h
                    hit = r_iota == jnp.broadcast_to(row8[r : r + 1], (128, 128))
                    part = got[k * 128 : k * 128 + 128, h * 128 : h * 128 + 128]
                    found[k].append(jnp.sum(jnp.where(hit, part, 0.0), axis=0, keepdims=True))
        for k in range(3):
            found_ref[k, pl.ds(pl.multiple_of(g * 8, 8), 8), :] = (
                jnp.concatenate(found[k], 0) * undo[k]
            )
        return carry

    lax.fori_loop(0, 6, step, 0)
    low_half = iota((16, 128), 1) < 64
    first_row = group * PER_GROUP * 8
    tails = [found_ref[k, 32:48, :] for k in range(3)]
    turned = [pltpu.roll(t, 64, 1) for t in tails]
    for k in range(3):
        back_ref[pl.ds(first_row + k, 32, stride=8), :] = found_ref[k, 0:32, :]
    back_ref[pl.ds(first_row + 3, 16, stride=8), :] = jnp.where(low_half, tails[0], turned[1])
    back_ref[pl.ds(first_row + 131, 16, stride=8), :] = jnp.where(low_half, turned[0], tails[1])
    back_ref[pl.ds(first_row + 4, 16, stride=8), :] = tails[2]
    back_ref[pl.ds(first_row + 132, 16, stride=8), :] = turned[2]
    for k in range(5, 8):
        back_ref[pl.ds(first_row + k, 32, stride=8), :] = jnp.zeros((32, 128), F32)


TALL = 136
BROAD = 640


def place_rims(wide_ref, index, f, refs, bases):
    up, down, left, right, *corners = refs
    upper_half = iota((8, 128), 0) < 4
    for b in range(4):
        at = bases[0] + (f * 4 + b) * 8
        wide_ref[index, 128:136, b * 128 : b * 128 + 128] = jnp.where(
            upper_half, down[at : at + 8, :], up[at : at + 8, :]
        )
    to_left = (128 - DEEP - DEEP * f) % 128
    to_right = (128 - DEEP * f) % 128

    def strip(left_part, right_part):
        moved_left = pltpu.roll(left_part, to_left, 1) if to_left else left_part
        moved_right = pltpu.roll(right_part, to_right, 1) if to_right else right_part
        return jnp.where(iota(left_part.shape, 1) < 64, moved_right, moved_left)

    sides = slice(bases[1], bases[1] + 128)
    wide_ref[index, 0:128, 512:640] = strip(left[sides, :], right[sides, :])
    rows = slice(bases[2], bases[2] + 8)
    c = [
        jnp.where(upper_half, corners[2 + side][rows, :], corners[side][rows, :])
        for side in range(2)
    ]
    wide_ref[index, 128:136, 512:640] = strip(c[0], c[1])


def inside_grid(block):
    (a, c), (na, nc) = my_place(), sizes()
    cols = iota((8, BROAD), 1)
    cols = jnp.where(cols < 576, cols, cols - BROAD) + c * 512
    rows = iota((8, BROAD), 0) + block * 8
    rows = jnp.where(rows < 132, rows, rows - TALL) + a * 128
    return (cols >= 0) & (cols < nc * 512) & (rows >= 0) & (rows < na * 128)


def water_step(old_ref, new_ref, depth_ref, source_ref=None):
    blocks = TALL // 8
    sub = iota((8, BROAD), 0)

    def load(block):
        at = slice(block * 8, block * 8 + 8)
        h, u, v = [old_ref[f, at, :] for f in range(3)]
        fu = depth_ref[0, at, :] * u
        fields = (h, u, v, fu)
        return fields, [pltpu.roll(x, 1, 0) for x in fields], [pltpu.roll(x, 7, 0) for x in fields]

    def left(x):
        return pltpu.roll(x, 1, 1)

    def right(x):
        return pltpu.roll(x, BROAD - 1, 1)

    before, here = load(blocks - 1), load(0)
    for block in range(blocks):
        after = load((block + 1) % blocks)
        at = slice(block * 8, block * 8 + 8)
        (h, u, v, _), down, up = here
        h_w, u_w, v_w, fu_w = [jnp.where(sub == 0, p, q) for p, q in zip(before[1], down)]
        h_e, u_e, v_e, fu_e = [jnp.where(sub == 7, p, q) for p, q in zip(after[2], up)]
        fv = depth_ref[0, at, :] * v
        h_s, h_n = left(h), right(h)
        next_h = 0.25 * (h_e + h_w + h_n + h_s) - 0.5 * courant * (
            fu_e - fu_w + right(fv) - left(fv)
        )
        next_u = 0.25 * (u_e + u_w + right(u) + left(u)) - 0.5 * courant * (h_e - h_w)
        next_v = 0.25 * (v_e + v_w + right(v) + left(v)) - 0.5 * courant * (h_n - h_s)
        inside = inside_grid(block)
        for f, value in enumerate((next_h, next_u, next_v)):
            if source_ref is not None:
                value = value + source_ref[f, at, :]
            new_ref[f, at, :] = jnp.where(inside, value, 0.0)
        before, here = here, after


def main_kernel(
    off_ref, vel_ref, mass_ref, near_ref, dest_ref, cell_ref, surface_ref, depth_ref,
    dens_ref, rank_ref, state_ref, back_got,
    pad_ref,
    sums_ref, vals_ref, pleft_ref, pslots_ref, pacc_ref, send_ref, got_ref,
    slots_ref, cells_ref, left0, left1, right0, right1, acc_ref,
    even, odd, deep, wide_source,
    high_ref, low_ref, found_ref, back_ref,
    o0, o1, o2, o3, o4, o5, o6, o7, i0, i1, i2, i3, i4, i5, i6, i7,
    q0, q1, q2, q3, q4, q5, q6, q7, g0, g1, g2, g3, g4, g5, g6, g7,
    r0, r1, r2, r3, r4, r5, r6, r7, t0, t1, t2, t3, t4, t5, t6, t7,
    rim_send, rim_recv, first_send, first_recv, tile_send, tile_recv,
    out_sem, in_sem, back_out_sem, back_in_sem, state_sem, fill_sem,
):
    (a, c), (na, nc) = my_place(), sizes()
    count = na * nc
    me = a * nc + c
    rows, cols = mass_ref.shape[0], mass_ref.shape[1]
    ahead = [lax.rem(c + step, nc) for step in range(nc)]
    behind = [lax.rem(c - step + nc, nc) for step in range(nc)]

    def block(n):
        return pl.ds(pl.multiple_of(n * 8, 8), 8)

    def each_other(first, last, act):
        if first == 0:
            for across in range(1, nc):
                act(0, across)

        def along(step, carry):
            for across in range(nc):
                act(step, across)
            return carry

        lax.fori_loop(max(first, 1), last, along, 0)

    fill = [
        pltpu.make_async_copy(surface_ref, even.at[:, 0:128, 0:512], fill_sem.at[0]),
        pltpu.make_async_copy(depth_ref, deep.at[0, 0:128, 0:512], fill_sem.at[1]),
    ]
    for copy in fill:
        copy.start()
    barrier = pltpu.get_barrier_semaphore()

    def greet(along, across):
        pl.semaphore_signal(
            barrier,
            inc=1,
            device_id=(lax.rem(a + along, na), ahead[across]),
            device_id_type=MESH,
        )

    each_other(0, na, greet)

    particle = [
        (off_ref, 0), (off_ref, 1), (vel_ref, 0), (vel_ref, 1), (mass_ref, None),
    ]
    tile_outs = [r0, r1, r2, r3, r4, r5, r6, r7]
    tile_ins = [t0, t1, t2, t3, t4, t5, t6, t7]
    stage_particles(particle, rows, cols, tile_outs, pad_ref)
    tile = window_sums(pad_ref, near_ref, dest_ref, sums_ref, rank_ref)
    inner = cols - 2
    half = rows // 2 - 1

    def inner_tiles(base, row0, running):
        def one(n, running):
            return tile(row0 + n // inner, 1 + n % inner, base + n, running)

        return lax.fori_loop(0, half * inner, one, running, unroll=7)

    running = inner_tiles(0, 1, jnp.zeros((128, 128), F32))
    pl.semaphore_wait(barrier, count - 1)
    copies = rim_copies(tile_outs, tile_ins, tile_send, tile_recv)
    for copy in copies:
        copy.start()
    running = inner_tiles(half * inner, 1 + half, running)
    for copy in copies:
        copy.wait()
    place_particles(tile_ins, rows, cols, pad_ref)
    done = 2 * half * inner

    ends = 2 * cols

    def outer_tiles(n, running):
        late = n // ends
        i = (1 - late) * (n // cols) * (rows - 1) + late * (1 + (n - ends) // 2)
        j = (1 - late) * (n % cols) + late * (n % 2) * (cols - 1)
        return tile(i, j, done + n, running)

    lax.fori_loop(0, ends + 2 * (rows - 2), outer_tiles, running, unroll=6)

    for i in range(rows):
        at = slice(i * cols, (i + 1) * cols)
        s0 = sums_ref[0, at, :]
        density = s0 / 128.0
        dens_ref[at, :] = density
        volume = mass_ref[i] / density
        vals_ref[0, at, :] = cell_ref[at, :].astype(F32)
        vals_ref[1, at, :] = volume
        vals_ref[2, at, :] = volume * (sums_ref[1, at, :] / s0)
        vals_ref[3, at, :] = volume * (sums_ref[2, at, :] / s0)
    pack(dest_ref, vals_ref, rank_ref, send_ref, pleft_ref, pslots_ref, pacc_ref)

    per_group = na // GROUPS

    def send_out(group):
        def start(along, across):
            to = (lax.rem(a + along, na), ahead[across])
            pltpu.make_async_remote_copy(
                src_ref=send_ref.at[block(to[0] * nc + to[1]), :],
                dst_ref=got_ref.at[block(along * nc + across), :],
                send_sem=out_sem,
                recv_sem=in_sem.at[group],
                device_id=to,
                device_id_type=MESH,
            ).start()

        each_other(group * per_group, (group + 1) * per_group, start)

    for group in range(GROUPS):
        send_out(group)
    pltpu.make_async_copy(send_ref.at[block(me), :], got_ref.at[0:8, :], in_sem.at[0]).start()

    first_outs = [q0, q1, q2, q3, q4, q5, q6, q7]
    first_ins = [g0, g1, g2, g3, g4, g5, g6, g7]
    for copy in fill:
        copy.wait()
    write_rims(first_outs, [0, 0, 0, 0, 0], [
        lambda r, c: even[0, r, c],
        lambda r, c: even[1, r, c],
        lambda r, c: even[2, r, c],
        lambda r, c: deep[0, r, c],
    ])
    copies = rim_copies(first_outs, first_ins, first_send, first_recv)
    for copy in copies:
        copy.start()
    acc_ref[...] = jnp.zeros_like(acc_ref)
    for copy in copies:
        copy.wait()
    for f in range(3):
        place_rims(even, f, f, first_ins, [0, 0, 0])
    place_rims(deep, 0, 3, first_ins, [0, 0, 0])
    for b in range(TALL // 8):
        at = slice(b * 8, b * 8 + 8)
        for f in range(3):
            even[f, at, :] = jnp.where(inside_grid(b), even[f, at, :], 0.0)

    water_step(even, odd, deep)
    def take_group(group, carry):
        span = PER_GROUP * 8
        landed = got_ref.at[pl.ds(pl.multiple_of(group * span, span), span), :]
        pltpu.make_async_copy(landed, landed, in_sem.at[group]).wait()
        unfold(got_ref, slots_ref, group)
        deposit_group(group, slots_ref, cells_ref, [left0, left1], [right0, right1], acc_ref)
        return carry

    lax.fori_loop(0, GROUPS, take_group, 0)
    for k in range(3):
        wide_source[k, 0:128, 0:512] = deposit_sum(acc_ref, k)

    outs = [o0, o1, o2, o3, o4, o5, o6, o7]
    ins = [i0, i1, i2, i3, i4, i5, i6, i7]
    write_rims(outs, [0, 0, 0, 0, 0], [
        lambda r, c: wide_source[0, r, c],
        lambda r, c: wide_source[1, r, c],
        lambda r, c: wide_source[2, r, c],
    ])
    copies = rim_copies(outs, ins, rim_send, rim_recv)
    for copy in copies:
        copy.start()
    for copy in copies:
        copy.wait()
    for f in range(3):
        place_rims(wide_source, f, f, ins, [0, 0, 0])

    for b in range(TALL // 8):
        at = slice(b * 8, b * 8 + 8)
        for f in range(3):
            odd[f, at, :] = jnp.where(inside_grid(b), odd[f, at, :] + wide_source[f, at, :], 0.0)
    water_step(odd, even, deep, wide_source)
    for _ in range(SUBSTEPS // 2 - 1):
        water_step(even, odd, deep, wide_source)
        water_step(odd, even, deep, wide_source)
    keep = pltpu.make_async_copy(even.at[:, 0:128, 0:512], state_ref, state_sem)
    keep.start()
    undo = [lookup_table(even[k, 0:128, 0:512], k, high_ref, low_ref) for k in range(3)]

    for group in range(GROUPS):
        lookup_group(group, cells_ref, high_ref, low_ref, undo, found_ref, back_ref)

        def start(along, across):
            pltpu.make_async_remote_copy(
                src_ref=back_ref.at[block(along * nc + across), :],
                dst_ref=back_got.at[block(me), :],
                send_sem=back_out_sem,
                recv_sem=back_in_sem,
                device_id=(lax.rem(a - along + na, na), behind[across]),
                device_id_type=MESH,
            ).start()

        each_other(group * per_group, (group + 1) * per_group, start)
    back_got[block(me), :] = back_ref[0:8, :]
    others = (count - 1) * 8
    for ref, sem in (
        (back_got, back_in_sem),
        (send_ref, out_sem),
        (back_ref, back_out_sem),
    ):
        pltpu.make_async_copy(ref.at[0:others, :], ref.at[0:others, :], sem).wait()
    keep.wait()


def main_call(offsets, velocity, mass, near, dest, cell, surface, depth):
    def buffers(heights):
        return [pltpu.VMEM((h, 128), F32) for h in heights + [8, 8, 8, 8]]

    rows, cols = mass.shape[0], mass.shape[1]
    dma = pltpu.SemaphoreType.DMA
    anywhere = pl.BlockSpec(memory_space=pl.ANY)
    return pl.pallas_call(
        main_kernel,
        out_shape=(
            jax.ShapeDtypeStruct((64, 128), F32),
            jax.ShapeDtypeStruct((64, 128), F32),
            jax.ShapeDtypeStruct((3, 128, 512), F32),
            jax.ShapeDtypeStruct((1024, 128), F32),
        ),
        in_specs=[vmem()] * 3
        + [pl.BlockSpec(memory_space=pltpu.SMEM)]
        + [vmem()] * 2
        + [anywhere] * 2,
        out_specs=(vmem(), vmem(), anywhere, vmem()),
        scratch_shapes=[
            pltpu.VMEM((5, rows + 2, cols + 2, 128), F32),
            pltpu.VMEM((3, 64, 128), F32),
            pltpu.VMEM((4, 64, 128), F32),
            pltpu.VMEM((1024, 1024), BF16),
            pltpu.VMEM((192, 1024), BF16),
            pltpu.VMEM((1024, 256), F32),
            pltpu.VMEM((1024, 128), F32),
            pltpu.VMEM((1024, 128), F32),
            pltpu.VMEM((4, 48, 128), F32),
            pltpu.VMEM((192, 128), F32),
            pltpu.VMEM((1152, STEP * 128), F8),
            pltpu.VMEM((1152, STEP * 128), F8),
            pltpu.VMEM((512, STEP * 128), F8),
            pltpu.VMEM((512, STEP * 128), F8),
            pltpu.VMEM((1152, 512), F32),
            pltpu.VMEM((3, TALL, BROAD), F32),
            pltpu.VMEM((3, TALL, BROAD), F32),
            pltpu.VMEM((1, TALL, BROAD), F32),
            pltpu.VMEM((3, TALL, BROAD), F32),
            pltpu.VMEM((384, 512), BF16),
            pltpu.VMEM((384, 512), F8),
            pltpu.VMEM((3, 48, 128), F32),
            pltpu.VMEM((1024, 128), F32),
            *buffers([96, 96, 128, 128]),
            *buffers([96, 96, 128, 128]),
            *buffers([128, 128, 128, 128]),
            *buffers([128, 128, 128, 128]),
            *buffers([5 * cols, 5 * cols, SIDE_PARTICLES, SIDE_PARTICLES]),
            *buffers([5 * cols, 5 * cols, SIDE_PARTICLES, SIDE_PARTICLES]),
            dma((8,)),
            dma((8,)),
            dma((8,)),
            dma((8,)),
            dma((8,)),
            dma((8,)),
            dma,
            dma((GROUPS,)),
            dma,
            dma,
            dma,
            dma((2,)),
        ],
        compiler_params=pltpu.CompilerParams(
            vmem_limit_bytes=VMEM_LIMIT, collective_id=1, has_side_effects=True
        ),
        name="main",
    )(offsets, velocity, mass, near, dest, cell, surface, depth)


def shards(
    offsets, velocity, particle_mass, neighbours, owner_device, target_cell, surface, water_depth
):
    dest = owner_device.reshape(64, 128)
    density, rank, water_state, back = main_call(
        offsets,
        velocity,
        particle_mass,
        jnp.transpose(neighbours, (2, 0, 1)),
        dest,
        target_cell.reshape(64, 128),
        surface,
        water_depth,
    )
    feedback, water_state, density = finish_call(back, dest, rank, water_state, density)
    return (
        water_state,
        density.reshape(particle_mass.shape),
        feedback.reshape((3,) + particle_mass.shape),
    )


def solution(mesh):
    in_specs = (
        P(None, "along", "cross", None),
        P(None, "along", "cross", None),
        P("along", "cross", None),
        P("along", "cross", None),
        P("along", "cross", None, None),
        P("along", "cross", None),
        P(None, "along", "cross"),
        P("along", "cross"),
    )
    out_specs = (
        P(None, "along", "cross"),
        P("along", "cross", None),
        P(None, "along", "cross", None),
    )
    return jax.shard_map(shards, mesh=mesh, in_specs=in_specs, out_specs=out_specs, check_vma=False)
```

```python
import math

import jax
import jax.numpy as jnp
from jax import lax
from jax.experimental import pallas as pl
from jax.experimental.pallas import tpu as pltpu
from jax.sharding import PartitionSpec as P

SUBSTEPS = 4
KAPPA = math.sqrt(math.log2(math.e))
F32 = jnp.float32
BF16 = jnp.bfloat16
F8 = jnp.float8_e4m3fn
NN = (((1,), (0,)), ((), ()))
NT = (((1,), (1,)), ((), ()))
VMEM_LIMIT = 56 * 1024 * 1024

courant = 0.4


def dot(a, b, dims):
    return lax.dot_general(a, b, dims, preferred_element_type=F32)


def split2(x):
    hi = x.astype(BF16).astype(F32)
    return hi, x - hi


def split8(x):
    t0 = x.astype(F8).astype(F32)
    r = (x - t0) * 16.0
    t1 = r.astype(F8).astype(F32)
    return t0, t1, (r - t1) * 16.0


def iota(shape, dim):
    return lax.broadcasted_iota(jnp.int32, shape, dim)


def window_sums(pad_ref, near_ref, dest_ref, sums_ref, rank_ref):
    cols = pad_ref.shape[2] - 2
    d_iota = iota((128, 128), 0)
    before = jnp.concatenate(
        [
            (iota((128, 128), 0) < iota((128, 128), 1)).astype(F32),
            jnp.ones((128, 128), F32),
        ],
        1,
    ).astype(BF16)

    q16 = iota((16, 128), 0)
    kind = jnp.where(q16 >= 3, q16 - 3, q16)

    def tile(i, j, row, running):
        hit = d_iota == jnp.broadcast_to(dest_ref[pl.ds(row, 1), :], (128, 128))
        counts = dot(jnp.where(hit, 1.0, 0.0).astype(BF16), before, NN)
        rank_ref[pl.ds(row, 1), :] = jnp.sum(
            jnp.where(hit, counts[:, :128] + running, 0.0), axis=0, keepdims=True
        )
        running = running + counts[:, 128:]
        x = pad_ref[0, i + 1, pl.ds(j + 1, 1), :] * KAPPA
        y = pad_ref[1, i + 1, pl.ds(j + 1, 1), :] * KAPPA
        x_col = jnp.broadcast_to(x, (128, 128)).T
        y_col = jnp.broadcast_to(y, (128, 128)).T
        listed = jnp.int32(0)
        for slot in range(9):
            listed = listed | lax.shift_left(jnp.int32(1), near_ref[slot, i, j] + 1)
        window = []
        for w in range(9):
            bi, bj = i + w // 3, j + w % 3
            bx = (pad_ref[0, bi, pl.ds(bj, 1), :] + (w // 3 - 1.0)) * KAPPA
            by = (pad_ref[1, bi, pl.ds(bj, 1), :] + (w % 3 - 1.0)) * KAPPA
            c0 = pad_ref[4, bi, pl.ds(bj, 1), :] * jnp.exp2(-bx * bx - by * by)
            c0 = c0 * (lax.shift_right_logical(listed, w + 1) & 1).astype(F32)
            vx = pad_ref[2, bi, pl.ds(bj, 1), :]
            vy = pad_ref[3, bi, pl.ds(bj, 1), :]
            c_hi, c_lo = split2(
                jnp.broadcast_to(c0, (16, 128))
                * jnp.where(kind == 0, 1.0, jnp.where(kind == 1, vx, vy))
            )
            carried = jnp.where(q16 < 3, c_hi, jnp.where(q16 < 6, c_lo, 0.0)).astype(BF16)
            window.append((2.0 * bx, 2.0 * by, carried))
        left, right = [], []
        for bx, by, carried in window:
            weights = jnp.exp2(x_col * bx + y_col * by)
            hi = weights.astype(BF16)
            left += [hi, (weights - hi.astype(F32)).astype(BF16)]
            right += [carried, carried]
        total = dot(jnp.concatenate(left, 1), jnp.concatenate(right, 1), NT)
        total = jnp.concatenate([total, jnp.zeros((128, 112), F32)], 1).T
        scale = jnp.exp2(-x * x - y * y)
        for k in range(3):
            sums_ref[k, pl.ds(i * cols + j, 1), :] = (total[k : k + 1] + total[k + 3 : k + 4]) * scale
        return running

    return tile


def pack(dest_ref, vals_ref, rank_ref, send_ref, left_ref, slots_ref, acc_ref):
    groups = dest_ref.shape[0] // 8
    d_iota = iota((128, 128), 0)
    p_iota = iota((192, 128), 0).astype(F32)
    acc_ref[...] = jnp.zeros_like(acc_ref)

    def group(g, carry):
        at = pl.ds(pl.multiple_of(g * 8, 8), 8)
        dest8 = dest_ref[at, :]
        rank8 = rank_ref[at, :]
        vals8 = [split2(vals_ref[k, at, :]) for k in range(4)]
        for r in range(8):
            hit = d_iota == jnp.broadcast_to(dest8[r : r + 1], (128, 128))
            lanes = slice(r * 128, r * 128 + 128)
            slots_ref[:, lanes] = jnp.where(
                p_iota == jnp.broadcast_to(rank8[r : r + 1], (192, 128)), 1.0, 0.0
            ).astype(BF16)
            for part in range(2):
                for k in range(4):
                    v = jnp.broadcast_to(vals8[k][part][r : r + 1], (128, 128))
                    base = (part * 4 + k) * 128
                    left_ref[base : base + 128, lanes] = jnp.where(hit, v, 0.0).astype(BF16)
        acc_ref[:, 0:192] += dot(left_ref[...], slots_ref[...], NT)
        return carry

    lax.fori_loop(0, groups, group, 0)
    tails = []
    for k in range(4):
        send_ref[pl.ds(k, 128, stride=8), :] = acc_ref[k * 128 : k * 128 + 128, 0:128] + acc_ref[
            512 + k * 128 : 640 + k * 128, 0:128
        ]
        tails.append(
            acc_ref[k * 128 : k * 128 + 128, 128:256]
            + acc_ref[512 + k * 128 : 640 + k * 128, 128:256]
        )
    low_half = iota((128, 128), 1) < 64
    for k in range(6, 8):
        send_ref[pl.ds(k, 128, stride=8), :] = jnp.zeros((128, 128), F32)
    for h in range(2):
        send_ref[pl.ds(4 + h, 128, stride=8), :] = jnp.where(
            low_half, tails[2 * h], pltpu.roll(tails[2 * h + 1], 64, 1)
        )


def vmem():
    return pl.BlockSpec(memory_space=pltpu.VMEM)


MESH = pl.DeviceIdType.MESH
AROUND = [(-1, 0), (1, 0), (0, -1), (0, 1), (-1, -1), (-1, 1), (1, -1), (1, 1)]


def my_place():
    return lax.axis_index("along"), lax.axis_index("cross")


def sizes():
    return lax.axis_size("along"), lax.axis_size("cross")


def at_step(step):
    (a, c), (na, nc) = my_place(), sizes()
    return lax.rem(a + step[0] + na, na), lax.rem(c + step[1] + nc, nc)


def rim_copies(out_refs, in_refs, send_sem, recv_sem):
    copies = []
    for n, step in enumerate(AROUND):
        opposite = AROUND.index((-step[0], -step[1]))
        copies.append(
            pltpu.make_async_remote_copy(
                src_ref=out_refs[n],
                dst_ref=in_refs[opposite],
                send_sem=send_sem.at[n],
                recv_sem=recv_sem.at[opposite],
                device_id=at_step(step),
                device_id_type=MESH,
            )
        )
    return copies


DEEP = 4
SIDE_PARTICLES = 24


def column_strip(fields, right):
    lanes = iota((fields[0].shape[0], 128), 1)
    out = jnp.zeros((fields[0].shape[0], 128), F32)
    for f, field in enumerate(fields):
        turn = DEEP * f + (DEEP if right else 0)
        moved = pltpu.roll(field, turn, 1) if turn else field
        out = jnp.where((lanes >= DEEP * f) & (lanes < DEEP * f + DEEP), moved, out)
    return out


def write_rims(out_refs, base, fields):
    top, bottom = slice(0, 8), slice(120, 128)
    for n, rows in ((0, top), (1, bottom)):
        for f, field in enumerate(fields):
            for b in range(4):
                at = base[n] + (f * 4 + b) * 8
                out_refs[n][at : at + 8, :] = field(rows, slice(b * 128, b * 128 + 128))
    for right in range(2):
        lanes = slice(384, 512) if right else slice(0, 128)
        strip = column_strip([field(slice(0, 128), lanes) for field in fields], right == 1)
        at = base[2 + right]
        out_refs[2 + right][at : at + 128, :] = strip
        out_refs[4 + right][base[4] : base[4] + 8, :] = strip[0:8]
        out_refs[6 + right][base[4] : base[4] + 8, :] = strip[120:128]


def stage_particles(particle, rows, cols, outs, pad_ref):
    def tiles(f, i, j):
        ref, part = particle[f]
        return ref[i, j, :] if part is None else ref[part, i, j, :]

    everything = slice(0, cols)
    for f in range(5):
        outs[0][f * cols : (f + 1) * cols, :] = tiles(f, 0, everything)
        outs[1][f * cols : (f + 1) * cols, :] = tiles(f, rows - 1, everything)
        for side, j in ((0, slice(0, 1)), (1, slice(cols - 1, cols))):
            for i in range(rows):
                outs[2 + side][f * rows + i : f * rows + i + 1, :] = tiles(f, i, j)
            outs[4 + side][f : f + 1, :] = tiles(f, 0, j)
            outs[6 + side][f : f + 1, :] = tiles(f, rows - 1, j)
    for side in range(2):
        outs[2 + side][5 * rows : SIDE_PARTICLES, :] = jnp.zeros(
            (SIDE_PARTICLES - 5 * rows, 128), F32
        )
        outs[4 + side][5:8, :] = jnp.zeros((3, 128), F32)
        outs[6 + side][5:8, :] = jnp.zeros((3, 128), F32)
    for f in range(5):
        for i in range(rows):
            pad_ref[f, i + 1, 1 : cols + 1, :] = tiles(f, i, everything)


def place_particles(ins, rows, cols, pad_ref):
    (a, c), (na, nc) = my_place(), sizes()
    inside = [a > 0, a < na - 1, c > 0, c < nc - 1]

    def kept(f, value, *tests):
        if f < 4:
            return value
        for test in tests:
            value = jnp.where(test, value, 0.0)
        return value

    for f in range(5):
        pad_ref[f, 0, 1 : cols + 1, :] = kept(f, ins[0][f * cols : (f + 1) * cols, :], inside[0])
        pad_ref[f, rows + 1, 1 : cols + 1, :] = kept(
            f, ins[1][f * cols : (f + 1) * cols, :], inside[1]
        )
        for side, j in ((0, 0), (1, cols + 1)):
            for i in range(rows):
                pad_ref[f, i + 1, j : j + 1, :] = kept(
                    f, ins[2 + side][f * rows + i : f * rows + i + 1, :], inside[2 + side]
                )
            pad_ref[f, 0, j : j + 1, :] = kept(
                f, ins[4 + side][f : f + 1, :], inside[0], inside[2 + side]
            )
            pad_ref[f, rows + 1, j : j + 1, :] = kept(
                f, ins[6 + side][f : f + 1, :], inside[1], inside[2 + side]
            )


def finish_kernel(
    back_ref, dest_ref, rank_ref, state_in, dens_in, out_ref, state_ref, dens_ref, table_ref
):
    state_ref[...] = state_in[...]
    dens_ref[...] = dens_in[...]
    tail = back_ref[pl.ds(3, 128, stride=8), :]
    tails = [tail, pltpu.roll(tail, 64, 1), back_ref[pl.ds(4, 128, stride=8), :]]
    for k in range(3):
        for part, piece in enumerate(split2(back_ref[pl.ds(k, 128, stride=8), :])):
            table_ref[k * 128 : k * 128 + 128, part * 192 : part * 192 + 128] = piece.astype(BF16)
        for part, piece in enumerate(split2(tails[k])):
            table_ref[
                k * 128 : k * 128 + 128, part * 192 + 128 : part * 192 + 192
            ] = piece[:, 0:64].astype(BF16)
    d_iota = iota((128, 128), 0)
    p_iota = iota((192, 128), 0).astype(F32)

    def step(g, carry):
        at = pl.ds(g * 8, 8)
        dest8 = dest_ref[at, :]
        rank8 = rank_ref[at, :]
        found = [[], [], []]
        for pair in range(4):
            slots = jnp.concatenate(
                [
                    jnp.where(
                        p_iota == jnp.broadcast_to(rank8[r : r + 1], (192, 128)), 1.0, 0.0
                    ).astype(BF16)
                    for r in (2 * pair, 2 * pair + 1)
                ],
                1,
            )
            got = dot(table_ref[...], jnp.concatenate([slots, slots], 0), NN)
            for k in range(3):
                for h in range(2):
                    r = 2 * pair + h
                    hit = d_iota == jnp.broadcast_to(dest8[r : r + 1], (128, 128))
                    part = got[k * 128 : k * 128 + 128, h * 128 : h * 128 + 128]
                    found[k].append(jnp.sum(jnp.where(hit, part, 0.0), axis=0, keepdims=True))
        for k in range(3):
            out_ref[k, at, :] = jnp.concatenate(found[k], 0)
        return carry

    lax.fori_loop(0, dest_ref.shape[0] // 8, step, 0, unroll=8)


def finish_call(back, dest, rank, state, density):
    return pl.pallas_call(
        finish_kernel,
        out_shape=(
            jax.ShapeDtypeStruct((3, 64, 128), F32),
            jax.ShapeDtypeStruct(state.shape, F32),
            jax.ShapeDtypeStruct(density.shape, F32),
        ),
        in_specs=[vmem()] * 5,
        out_specs=(vmem(), vmem(), vmem()),
        scratch_shapes=[pltpu.VMEM((384, 384), BF16)],
        compiler_params=pltpu.CompilerParams(vmem_limit_bytes=VMEM_LIMIT),
        name="finish",
    )(back, dest, rank, state, density)


GROUPS = 4
PER_GROUP = 32
STEP = 16


def row_and_column(cell):
    row = jnp.floor(cell * (1.0 / 512.0))
    return row, cell - row * 512.0


def unfold(got_ref, slots_ref, group):
    low_half = iota((16, 128), 1) < 64
    first_row = group * PER_GROUP * 8
    for k in range(4):
        slots_ref[k, 0:32, :] = got_ref[pl.ds(first_row + k, 32, stride=8), :]
        row = got_ref[pl.ds(first_row + 4 + k // 2, 32, stride=8), :]
        first, second = row[0:16], row[16:32]
        if k % 2 == 0:
            full = jnp.where(low_half, first, pltpu.roll(second, 64, 1))
        else:
            full = jnp.where(low_half, pltpu.roll(first, 64, 1), second)
        slots_ref[k, 32:48, :] = full


def deposit_group(group, slots_ref, cells_ref, left_refs, right_refs, acc_ref):
    r_iota = iota((128, 128), 0).astype(F32)
    c_iota = iota((512, 128), 0).astype(F32)
    cells_ref[pl.ds(pl.multiple_of(group * 48, 8), 48), :] = slots_ref[0]
    for g in range(48 // STEP):
        left_ref, right_ref = left_refs[g % 2], right_refs[g % 2]
        at = slice(g * STEP, g * STEP + STEP)
        row8, col8 = row_and_column(slots_ref[0, at, :])
        vals8 = [split8(slots_ref[1 + k, at, :] * 0.5) for k in range(3)]
        for r in range(STEP):
            lanes = slice(r * 128, r * 128 + 128)
            hit = r_iota == jnp.broadcast_to(row8[r : r + 1], (128, 128))
            for part in range(3):
                for k in range(3):
                    v = jnp.broadcast_to(vals8[k][part][r : r + 1], (128, 128))
                    base = (part * 3 + k) * 128
                    left_ref[base : base + 128, lanes] = jnp.where(hit, v, 0.0).astype(F8)
            right_ref[:, lanes] = jnp.where(
                c_iota == jnp.broadcast_to(col8[r : r + 1], (512, 128)), 1.0, 0.0
            ).astype(F8)
        acc_ref[...] += dot(left_ref[...], right_ref[...], NT)


def deposit_sum(acc_ref, k):
    t0, t1, t2 = [
        acc_ref[(part * 3 + k) * 128 : (part * 3 + k) * 128 + 128, :] for part in range(3)
    ]
    return 2.0 * (t0 + (1.0 / 16.0) * t1 + (1.0 / 256.0) * t2)


def lookup_table(state, k, high_ref, low_ref):
    most = jnp.max(jnp.max(jnp.abs(state), axis=0, keepdims=True), axis=1, keepdims=True)
    most = jnp.maximum(most, 1e-30)
    hi, lo = split2(state * (1024.0 / most))
    high_ref[k * 128 : k * 128 + 128, :] = hi.astype(BF16)
    low_ref[k * 128 : k * 128 + 128, :] = (lo * 64.0).astype(F8)
    return most * (1.0 / 1024.0)


def lookup_group(group, cells_ref, high_ref, low_ref, undo, found_ref, back_ref, beside, steps):
    r_iota = iota((128, 128), 0).astype(F32)
    c_iota = iota((512, 128), 0).astype(F32)

    def step(g, carry):
        at = pl.ds(pl.multiple_of(group * 48 + g * 8, 8), 8)
        row8, col8 = row_and_column(cells_ref[at, :])
        found = [[], [], []]
        for pair in range(4):
            high, low = [], []
            for r in (2 * pair, 2 * pair + 1):
                column = c_iota == jnp.broadcast_to(col8[r : r + 1], (512, 128))
                high.append(jnp.where(column, 1.0, 0.0).astype(BF16))
                low.append(jnp.where(column, 1.0 / 64.0, 0.0).astype(F8))
            got = dot(high_ref[...], jnp.concatenate(high, 1), NN) + dot(
                low_ref[...], jnp.concatenate(low, 1), NN
            )
            for k in range(3):
                for h in range(2):
                    r = 2 * pair + h
                    hit = r_iota == jnp.broadcast_to(row8[r : r + 1], (128, 128))
                    part = got[k * 128 : k * 128 + 128, h * 128 : h * 128 + 128]
                    found[k].append(jnp.sum(jnp.where(hit, part, 0.0), axis=0, keepdims=True))
        for k in range(3):
            found_ref[k, pl.ds(pl.multiple_of(g * 8, 8), 8), :] = (
                jnp.concatenate(found[k], 0) * undo[k]
            )
        return carry

    def step_beside(g, carry):
        beside(g)
        return step(g, carry)

    if steps:
        lax.fori_loop(0, steps, step_beside, 0)
    lax.fori_loop(steps, 6, step, 0)
    low_half = iota((16, 128), 1) < 64
    first_row = group * PER_GROUP * 8
    tails = [found_ref[k, 32:48, :] for k in range(3)]
    turned = [pltpu.roll(t, 64, 1) for t in tails]
    for k in range(3):
        back_ref[pl.ds(first_row + k, 32, stride=8), :] = found_ref[k, 0:32, :]
    back_ref[pl.ds(first_row + 3, 16, stride=8), :] = jnp.where(low_half, tails[0], turned[1])
    back_ref[pl.ds(first_row + 131, 16, stride=8), :] = jnp.where(low_half, turned[0], tails[1])
    back_ref[pl.ds(first_row + 4, 16, stride=8), :] = tails[2]
    back_ref[pl.ds(first_row + 132, 16, stride=8), :] = turned[2]
    for k in range(5, 8):
        back_ref[pl.ds(first_row + k, 32, stride=8), :] = jnp.zeros((32, 128), F32)


TALL = 136
BROAD = 640


def place_rims(wide_ref, index, f, refs, bases):
    up, down, left, right, *corners = refs
    upper_half = iota((8, 128), 0) < 4
    for b in range(4):
        at = bases[0] + (f * 4 + b) * 8
        wide_ref[index, 128:136, b * 128 : b * 128 + 128] = jnp.where(
            upper_half, down[at : at + 8, :], up[at : at + 8, :]
        )
    to_left = (128 - DEEP - DEEP * f) % 128
    to_right = (128 - DEEP * f) % 128

    def strip(left_part, right_part):
        moved_left = pltpu.roll(left_part, to_left, 1) if to_left else left_part
        moved_right = pltpu.roll(right_part, to_right, 1) if to_right else right_part
        return jnp.where(iota(left_part.shape, 1) < 64, moved_right, moved_left)

    sides = slice(bases[1], bases[1] + 128)
    wide_ref[index, 0:128, 512:640] = strip(left[sides, :], right[sides, :])
    rows = slice(bases[2], bases[2] + 8)
    c = [
        jnp.where(upper_half, corners[2 + side][rows, :], corners[side][rows, :])
        for side in range(2)
    ]
    wide_ref[index, 128:136, 512:640] = strip(c[0], c[1])


def inside_grid(block):
    (a, c), (na, nc) = my_place(), sizes()
    cols = iota((8, BROAD), 1)
    cols = jnp.where(cols < 576, cols, cols - BROAD) + c * 512
    rows = iota((8, BROAD), 0) + block * 8
    rows = jnp.where(rows < 132, rows, rows - TALL) + a * 128
    return (cols >= 0) & (cols < nc * 512) & (rows >= 0) & (rows < na * 128)


def water_step(old_ref, new_ref, depth_ref, source_ref=None):
    blocks = TALL // 8
    sub = iota((8, BROAD), 0)

    def load(block):
        at = slice(block * 8, block * 8 + 8)
        h, u, v = [old_ref[f, at, :] for f in range(3)]
        fu = depth_ref[0, at, :] * u
        fields = (h, u, v, fu)
        return fields, [pltpu.roll(x, 1, 0) for x in fields], [pltpu.roll(x, 7, 0) for x in fields]

    def left(x):
        return pltpu.roll(x, 1, 1)

    def right(x):
        return pltpu.roll(x, BROAD - 1, 1)

    before, here = load(blocks - 1), load(0)
    for block in range(blocks):
        after = load((block + 1) % blocks)
        at = slice(block * 8, block * 8 + 8)
        (h, u, v, _), down, up = here
        h_w, u_w, v_w, fu_w = [jnp.where(sub == 0, p, q) for p, q in zip(before[1], down)]
        h_e, u_e, v_e, fu_e = [jnp.where(sub == 7, p, q) for p, q in zip(after[2], up)]
        fv = depth_ref[0, at, :] * v
        h_s, h_n = left(h), right(h)
        next_h = 0.25 * (h_e + h_w + h_n + h_s) - 0.5 * courant * (
            fu_e - fu_w + right(fv) - left(fv)
        )
        next_u = 0.25 * (u_e + u_w + right(u) + left(u)) - 0.5 * courant * (h_e - h_w)
        next_v = 0.25 * (v_e + v_w + right(v) + left(v)) - 0.5 * courant * (h_n - h_s)
        inside = inside_grid(block)
        for f, value in enumerate((next_h, next_u, next_v)):
            if source_ref is not None:
                value = value + source_ref[f, at, :]
            new_ref[f, at, :] = jnp.where(inside, value, 0.0)
        before, here = here, after


def main_kernel(
    off_ref, vel_ref, mass_ref, near_ref, dest_ref, cell_ref, surface_ref, depth_ref,
    dens_ref, rank_ref, state_ref, back_got,
    pad_ref,
    sums_ref, vals_ref, pleft_ref, pslots_ref, pacc_ref, send_ref, got_ref,
    slots_ref, cells_ref, left0, left1, right0, right1, acc_ref,
    even, odd, deep, wide_source,
    high_ref, low_ref, found_ref, back_ref,
    o0, o1, o2, o3, o4, o5, o6, o7, i0, i1, i2, i3, i4, i5, i6, i7,
    q0, q1, q2, q3, q4, q5, q6, q7, g0, g1, g2, g3, g4, g5, g6, g7,
    r0, r1, r2, r3, r4, r5, r6, r7, t0, t1, t2, t3, t4, t5, t6, t7,
    rim_send, rim_recv, first_send, first_recv, tile_send, tile_recv,
    out_sem, in_sem, back_out_sem, back_in_sem, state_sem, fill_sem,
):
    (a, c), (na, nc) = my_place(), sizes()
    count = na * nc
    me = a * nc + c
    rows, cols = mass_ref.shape[0], mass_ref.shape[1]
    ahead = [lax.rem(c + step, nc) for step in range(nc)]
    behind = [lax.rem(c - step + nc, nc) for step in range(nc)]

    def block(n):
        return pl.ds(pl.multiple_of(n * 8, 8), 8)

    def each_other(first, last, act):
        if first == 0:
            for across in range(1, nc):
                act(0, across)

        def along(step, carry):
            for across in range(nc):
                act(step, across)
            return carry

        lax.fori_loop(max(first, 1), last, along, 0)

    fill = [
        pltpu.make_async_copy(surface_ref, even.at[:, 0:128, 0:512], fill_sem.at[0]),
        pltpu.make_async_copy(depth_ref, deep.at[0, 0:128, 0:512], fill_sem.at[1]),
    ]
    for copy in fill:
        copy.start()
    barrier = pltpu.get_barrier_semaphore()

    def greet(along, across):
        pl.semaphore_signal(
            barrier,
            inc=1,
            device_id=(lax.rem(a + along, na), ahead[across]),
            device_id_type=MESH,
        )

    each_other(0, na, greet)

    particle = [
        (off_ref, 0), (off_ref, 1), (vel_ref, 0), (vel_ref, 1), (mass_ref, None),
    ]
    tile_outs = [r0, r1, r2, r3, r4, r5, r6, r7]
    tile_ins = [t0, t1, t2, t3, t4, t5, t6, t7]
    stage_particles(particle, rows, cols, tile_outs, pad_ref)
    tile = window_sums(pad_ref, near_ref, dest_ref, sums_ref, rank_ref)
    inner = cols - 2
    half = rows // 2 - 1

    def inner_tiles(base, row0, running):
        def one(n, running):
            return tile(row0 + n // inner, 1 + n % inner, base + n, running)

        return lax.fori_loop(0, half * inner, one, running, unroll=7)

    running = inner_tiles(0, 1, jnp.zeros((128, 128), F32))
    pl.semaphore_wait(barrier, count - 1)
    copies = rim_copies(tile_outs, tile_ins, tile_send, tile_recv)
    for copy in copies:
        copy.start()
    running = inner_tiles(half * inner, 1 + half, running)
    for copy in copies:
        copy.wait()
    place_particles(tile_ins, rows, cols, pad_ref)
    done = 2 * half * inner

    ends = 2 * cols

    def outer_tiles(n, running):
        late = n // ends
        i = (1 - late) * (n // cols) * (rows - 1) + late * (1 + (n - ends) // 2)
        j = (1 - late) * (n % cols) + late * (n % 2) * (cols - 1)
        return tile(i, j, done + n, running)

    lax.fori_loop(0, ends + 2 * (rows - 2), outer_tiles, running, unroll=6)

    for i in range(rows):
        at = slice(i * cols, (i + 1) * cols)
        s0 = sums_ref[0, at, :]
        density = s0 / 128.0
        dens_ref[at, :] = density
        volume = mass_ref[i] / density
        vals_ref[0, at, :] = cell_ref[at, :].astype(F32)
        vals_ref[1, at, :] = volume
        vals_ref[2, at, :] = volume * (sums_ref[1, at, :] / s0)
        vals_ref[3, at, :] = volume * (sums_ref[2, at, :] / s0)
    pack(dest_ref, vals_ref, rank_ref, send_ref, pleft_ref, pslots_ref, pacc_ref)

    per_group = na // GROUPS

    def send_out(group):
        def start(along, across):
            to = (lax.rem(a + along, na), ahead[across])
            pltpu.make_async_remote_copy(
                src_ref=send_ref.at[block(to[0] * nc + to[1]), :],
                dst_ref=got_ref.at[block(along * nc + across), :],
                send_sem=out_sem,
                recv_sem=in_sem.at[group],
                device_id=to,
                device_id_type=MESH,
            ).start()

        each_other(group * per_group, (group + 1) * per_group, start)

    for group in range(GROUPS):
        send_out(group)
    pltpu.make_async_copy(send_ref.at[block(me), :], got_ref.at[0:8, :], in_sem.at[0]).start()

    first_outs = [q0, q1, q2, q3, q4, q5, q6, q7]
    first_ins = [g0, g1, g2, g3, g4, g5, g6, g7]
    for copy in fill:
        copy.wait()
    write_rims(first_outs, [0, 0, 0, 0, 0], [
        lambda r, c: even[0, r, c],
        lambda r, c: even[1, r, c],
        lambda r, c: even[2, r, c],
        lambda r, c: deep[0, r, c],
    ])
    copies = rim_copies(first_outs, first_ins, first_send, first_recv)
    for copy in copies:
        copy.start()
    acc_ref[...] = jnp.zeros_like(acc_ref)
    for copy in copies:
        copy.wait()
    for f in range(3):
        place_rims(even, f, f, first_ins, [0, 0, 0])
    place_rims(deep, 0, 3, first_ins, [0, 0, 0])
    for b in range(TALL // 8):
        at = slice(b * 8, b * 8 + 8)
        for f in range(3):
            even[f, at, :] = jnp.where(inside_grid(b), even[f, at, :], 0.0)

    water_step(even, odd, deep)
    def take_group(group, carry):
        span = PER_GROUP * 8
        landed = got_ref.at[pl.ds(pl.multiple_of(group * span, span), span), :]
        pltpu.make_async_copy(landed, landed, in_sem.at[group]).wait()
        unfold(got_ref, slots_ref, group)
        deposit_group(group, slots_ref, cells_ref, [left0, left1], [right0, right1], acc_ref)
        return carry

    lax.fori_loop(0, GROUPS, take_group, 0)
    for k in range(3):
        wide_source[k, 0:128, 0:512] = deposit_sum(acc_ref, k)

    outs = [o0, o1, o2, o3, o4, o5, o6, o7]
    ins = [i0, i1, i2, i3, i4, i5, i6, i7]
    write_rims(outs, [0, 0, 0, 0, 0], [
        lambda r, c: wide_source[0, r, c],
        lambda r, c: wide_source[1, r, c],
        lambda r, c: wide_source[2, r, c],
    ])
    copies = rim_copies(outs, ins, rim_send, rim_recv)
    for copy in copies:
        copy.start()
    for copy in copies:
        copy.wait()
    for f in range(3):
        place_rims(wide_source, f, f, ins, [0, 0, 0])

    for b in range(TALL // 8):
        at = slice(b * 8, b * 8 + 8)
        for f in range(3):
            odd[f, at, :] = jnp.where(inside_grid(b), odd[f, at, :] + wide_source[f, at, :], 0.0)
    water_step(odd, even, deep, wide_source)
    for _ in range(SUBSTEPS // 2 - 1):
        water_step(even, odd, deep, wide_source)
        water_step(odd, even, deep, wide_source)
    keep = pltpu.make_async_copy(even.at[:, 0:128, 0:512], state_ref, state_sem)
    keep.start()
    undo = [lookup_table(even[k, 0:128, 0:512], k, high_ref, low_ref) for k in range(3)]

    def send_back(along, across):
        pltpu.make_async_remote_copy(
            src_ref=back_ref.at[block(along * nc + across), :],
            dst_ref=back_got.at[block(me), :],
            send_sem=back_out_sem,
            recv_sem=back_in_sem,
            device_id=(lax.rem(a - along + na, na), behind[across]),
            device_id_type=MESH,
        ).start()

    for group in range(GROUPS):
        ready = (group - 1) * per_group
        if group == 1:
            each_other(0, 1, send_back)
            ready = 1

        def beside(step):
            for across in range(nc):
                send_back(ready + step, across)

        lookup_group(
            group, cells_ref, high_ref, low_ref, undo, found_ref, back_ref,
            beside, max(0, group * per_group - ready) if group else 0,
        )
    each_other((GROUPS - 1) * per_group, na, send_back)
    back_got[block(me), :] = back_ref[0:8, :]
    others = (count - 1) * 8
    for ref, sem in (
        (back_got, back_in_sem),
        (send_ref, out_sem),
        (back_ref, back_out_sem),
    ):
        pltpu.make_async_copy(ref.at[0:others, :], ref.at[0:others, :], sem).wait()
    keep.wait()


def main_call(offsets, velocity, mass, near, dest, cell, surface, depth):
    def buffers(heights):
        return [pltpu.VMEM((h, 128), F32) for h in heights + [8, 8, 8, 8]]

    rows, cols = mass.shape[0], mass.shape[1]
    dma = pltpu.SemaphoreType.DMA
    anywhere = pl.BlockSpec(memory_space=pl.ANY)
    return pl.pallas_call(
        main_kernel,
        out_shape=(
            jax.ShapeDtypeStruct((64, 128), F32),
            jax.ShapeDtypeStruct((64, 128), F32),
            jax.ShapeDtypeStruct((3, 128, 512), F32),
            jax.ShapeDtypeStruct((1024, 128), F32),
        ),
        in_specs=[vmem()] * 3
        + [pl.BlockSpec(memory_space=pltpu.SMEM)]
        + [vmem()] * 2
        + [anywhere] * 2,
        out_specs=(vmem(), vmem(), anywhere, vmem()),
        scratch_shapes=[
            pltpu.VMEM((5, rows + 2, cols + 2, 128), F32),
            pltpu.VMEM((3, 64, 128), F32),
            pltpu.VMEM((4, 64, 128), F32),
            pltpu.VMEM((1024, 1024), BF16),
            pltpu.VMEM((192, 1024), BF16),
            pltpu.VMEM((1024, 256), F32),
            pltpu.VMEM((1024, 128), F32),
            pltpu.VMEM((1024, 128), F32),
            pltpu.VMEM((4, 48, 128), F32),
            pltpu.VMEM((192, 128), F32),
            pltpu.VMEM((1152, STEP * 128), F8),
            pltpu.VMEM((1152, STEP * 128), F8),
            pltpu.VMEM((512, STEP * 128), F8),
            pltpu.VMEM((512, STEP * 128), F8),
            pltpu.VMEM((1152, 512), F32),
            pltpu.VMEM((3, TALL, BROAD), F32),
            pltpu.VMEM((3, TALL, BROAD), F32),
            pltpu.VMEM((1, TALL, BROAD), F32),
            pltpu.VMEM((3, TALL, BROAD), F32),
            pltpu.VMEM((384, 512), BF16),
            pltpu.VMEM((384, 512), F8),
            pltpu.VMEM((3, 48, 128), F32),
            pltpu.VMEM((1024, 128), F32),
            *buffers([96, 96, 128, 128]),
            *buffers([96, 96, 128, 128]),
            *buffers([128, 128, 128, 128]),
            *buffers([128, 128, 128, 128]),
            *buffers([5 * cols, 5 * cols, SIDE_PARTICLES, SIDE_PARTICLES]),
            *buffers([5 * cols, 5 * cols, SIDE_PARTICLES, SIDE_PARTICLES]),
            dma((8,)),
            dma((8,)),
            dma((8,)),
            dma((8,)),
            dma((8,)),
            dma((8,)),
            dma,
            dma((GROUPS,)),
            dma,
            dma,
            dma,
            dma((2,)),
        ],
        compiler_params=pltpu.CompilerParams(
            vmem_limit_bytes=VMEM_LIMIT, collective_id=1, has_side_effects=True
        ),
        name="main",
    )(offsets, velocity, mass, near, dest, cell, surface, depth)


def shards(
    offsets, velocity, particle_mass, neighbours, owner_device, target_cell, surface, water_depth
):
    dest = owner_device.reshape(64, 128)
    density, rank, water_state, back = main_call(
        offsets,
        velocity,
        particle_mass,
        jnp.transpose(neighbours, (2, 0, 1)),
        dest,
        target_cell.reshape(64, 128),
        surface,
        water_depth,
    )
    feedback, water_state, density = finish_call(back, dest, rank, water_state, density)
    return (
        water_state,
        density.reshape(particle_mass.shape),
        feedback.reshape((3,) + particle_mass.shape),
    )


def solution(mesh):
    in_specs = (
        P(None, "along", "cross", None),
        P(None, "along", "cross", None),
        P("along", "cross", None),
        P("along", "cross", None),
        P("along", "cross", None, None),
        P("along", "cross", None),
        P(None, "along", "cross"),
        P("along", "cross"),
    )
    out_specs = (
        P(None, "along", "cross"),
        P("along", "cross", None),
        P(None, "along", "cross", None),
    )
    return jax.shard_map(shards, mesh=mesh, in_specs=in_specs, out_specs=out_specs, check_vma=False)
```
